32 devices in a mesh: freq: 2 (over y), brick: 4 (over z), orb: 4 (over x, core).
Axes of the slice: x: 2, y: 2, z: 4, core: 2. Of those that a mesh axis runs over, the one named last changes fastest.
Arguments:
- orbitals: float32 [16, 24, 8192], P(None, 'brick'), may hold values from -6 to 6
- potential: float32 [24, 8192], P('brick'), may hold values from 0.5 to 2.5
- perturb: float32 [24, 8192], P('brick'), may hold values from 0.1 to 2
- energies: float32 [16], P('orb'), may hold values from -0.4 to 0
- omega: float32 [2], P('freq'), parts along dimension 0, may hold values from 0.05 to 1
Outputs:
- response: float32 [32, 24, 8192], P(('freq', 'orb'), 'brick'), parts along dimension 0
- induced: float32 [48, 8192], P(('freq', 'brick'), 'orb'), parts along dimension 0
The draws below stay inside these ranges and needn't reach their ends.
There are 2 independent parts, one for each index of `freq`. The reference program is written for one: setup_inputs(seed, part) draws one part's arguments, and reference() takes and returns one part's arrays. A program takes and returns all parts, laid end to end along the dimension named above; an argument that names none is the same for every part. Nothing has to cross between parts.
All inputs are finite; a program needn't handle non-finite values.
Results may differ from the reference program's by a relative error of at most 0.00011.
Values sent between devices are 32-bit elements; how exact they have to be, the bound alone decides.
No kernel may reach another device: no remote copies, remote signals or barrier semaphores. Data moves between devices by JAX's collectives and lax.ppermute only.
A program may use at most 128 MiB of HBM per device.

```python
import math
import jax
import jax.numpy as jnp
from jax import lax

NORB = 16
NY = 32
NX = 256
ITERS = 2
SWEEPS = 3
NZ = 24
COLS = 8192
NCELLS = 196608


def levels(own_key, shape, pieces, low, top_value):
    loudness, own = 1.0, jax.random.fold_in(own_key, 6)
    for position, parts in pieces:
        draws = jnp.exp(jax.random.uniform(jax.random.fold_in(own, position), (parts,), jnp.float32, low / len(pieces), top_value / len(pieces)))
        loudness = loudness * jnp.repeat(draws, shape[position] // parts).reshape([-1 if axis == position else 1 for axis in range(len(shape))])
    return loudness


def scatter_about(rng, extent, spread, bound, split=(), dtype=jnp.bfloat16):
    values = jax.random.normal(rng, extent, jnp.float32) * spread
    if len(split) > 0:
        values = levels(rng, extent, split, -0.22, 0.18) * values
    return jnp.clip(values, min=-bound, max=bound).astype(dtype)


def setup_inputs(seed: int = 0, part: int = 0) -> dict:
    streams_of = jax.random.split(jax.random.key(seed), 6)
    part_keys = jax.random.split(jax.random.fold_in(streams_of[5], part), 6)
    orbitals = scatter_about(streams_of[0], (NORB, NZ, COLS), 1.0, 6.0, ((1, 4),), jnp.float32)
    potential = jnp.clip(0.5 + 2.0 * jax.random.uniform(streams_of[1], (NZ, COLS), jnp.float32) ** levels(streams_of[1], (NZ, COLS), ((0, 4),), -0.2, 0.2), 0.5, 2.5)
    perturb = jnp.clip(jnp.exp(math.log(2.0) - 2.9957323 * jax.random.uniform(streams_of[2], (NZ, COLS), jnp.float32) ** levels(streams_of[2], (NZ, COLS), ((0, 4),), -0.2, 0.2)), 0.1, 2.0)
    energies = jnp.clip(-0.4 + 0.4 * jax.random.uniform(streams_of[3], (NORB,), jnp.float32) ** levels(streams_of[3], (NORB,), ((0, 4),), -0.2, 0.2), -0.4, 0.0)
    omega = jnp.clip(jnp.exp(jax.random.uniform(part_keys[4], (1,), jnp.float32, math.log(0.05), math.log(1.0))), 0.05, 1.0)
    return {"orbitals": orbitals, "potential": potential, "perturb": perturb, "energies": energies, "omega": omega}


COEFFS = (-5369.0 / 1800.0, 12.0 / 7.0, -15.0 / 56.0, 10.0 / 189.0, -1.0 / 112.0, 2.0 / 825.0, -1.0 / 5544.0)
SCREEN = 0.25
HIGHEST = lax.Precision.HIGHEST


def laplace(field):
    leading, layers, columns = field.shape
    cuboid = field.reshape(leading, layers, NY, columns // NY)
    total = 3.0 * COEFFS[0] * cuboid
    for offset in range(1, 7):
        for dimension in (1, 2, 3):
            total = total + COEFFS[offset] * (jnp.roll(cuboid, offset, dimension) + jnp.roll(cuboid, -offset, dimension))
    return total.reshape(leading, layers, columns)


def project(orbitals, field):
    coeffs = jnp.einsum('mzc,nzc->nm', orbitals, field, precision=HIGHEST)
    return field - jnp.einsum('nm,mzc->nzc', coeffs, orbitals, precision=HIGHEST) / NCELLS


def reference(orbitals, potential, perturb, energies, omega):
    shift = potential[None] + (omega[0] - energies)[:, None, None]
    source = -project(orbitals, perturb[None] * orbitals)
    solution = jnp.zeros_like(source)
    residual = source
    direction = source
    norm_now = jnp.sum(residual * residual, axis=(1, 2))
    for iteration in range(ITERS):
        inner = project(orbitals, direction)
        applied = -0.5 * laplace(inner) + shift * inner
        image = project(orbitals, applied)
        curvature = jnp.sum(direction * image, axis=(1, 2))
        alpha = norm_now / curvature
        solution = solution + alpha[:, None, None] * direction
        residual = residual - alpha[:, None, None] * image
        norm_next = jnp.sum(residual * residual, axis=(1, 2))
        direction = residual + (norm_next / norm_now)[:, None, None] * direction
        norm_now = norm_next
    density = 4.0 * jnp.sum(orbitals * solution, axis=0)
    dense_cube = density.reshape(NZ, NY, NX)
    field_cube = jnp.zeros((NZ, NY, NX), jnp.float32)
    for sweep in range(SWEEPS):
        beside = jnp.zeros((NZ, NY, NX), jnp.float32)
        for dimension in (0, 1, 2):
            beside = beside + jnp.roll(field_cube, 1, dimension) + jnp.roll(field_cube, -1, dimension)
        field_cube = (dense_cube + beside) / (6.0 + SCREEN)
    return solution, field_cube.reshape(NZ, NY * NX)
```

```python
import functools
import jax
import jax.numpy as jnp
from jax import lax
from jax.experimental import pallas as pl
from jax.experimental.pallas import tpu as pltpu
from jax.sharding import PartitionSpec as P

NY = 32
LANES = 128
SUB = 8

COEFFS = (
    -5369.0 / 1800.0,
    12.0 / 7.0,
    -15.0 / 56.0,
    10.0 / 189.0,
    -1.0 / 112.0,
    2.0 / 825.0,
    -1.0 / 5544.0,
)
SCREEN = 0.25
HIGHEST = lax.Precision.HIGHEST
VMEM_LIMIT = 48 * 1024 * 1024
SMEM = pl.BlockSpec(memory_space=pltpu.SMEM)
VMEM = pl.BlockSpec(memory_space=pltpu.VMEM)
f32 = jnp.float32


def call(kernel, outs, scratch, smem, *args):
    return pl.pallas_call(
        kernel,
        out_shape=[jax.ShapeDtypeStruct(s, f32) for s in outs],
        in_specs=[SMEM] * smem + [VMEM] * (len(args) - smem),
        out_specs=[VMEM] * len(outs),
        scratch_shapes=[pltpu.VMEM(s, f32) for s in scratch],
        compiler_params=pltpu.CompilerParams(vmem_limit_bytes=VMEM_LIMIT),
    )(*args)


def parts_of(array, axis):
    size = lax.axis_size(axis)
    if size > 4:
        return [lax.psum(array, axis)]
    rotated = [
        lax.ppermute(array, axis, [(i, (i + k) % size) for i in range(size)]) for k in range(1, size)
    ]
    return [array] + rotated


def shifted(array, axis, step):
    size = lax.axis_size(axis)
    return lax.ppermute(array, axis, [(i, (i + step) % size) for i in range(size)])


def add_all(refs):
    total = refs[0][...]
    for ref in refs[1:]:
        total = total + ref[...]
    return total


def column(matrix, index):
    lane = lax.broadcasted_iota(jnp.int32, matrix.shape, 1)
    picked = jnp.sum(jnp.where(lane == index, matrix, 0.0), axis=1, keepdims=True)
    return jnp.broadcast_to(picked, (matrix.shape[0], LANES))


def blocks(plane):
    return plane.reshape(-1, NY, LANES)


def gram_kernel(shape, rows_ref, perturb_ref, planes_ref, gram_ref):
    norb, layers, halves = shape
    groups = norb // SUB
    tiles = NY * halves
    step = 16

    def layer(z, total):
        for c0 in range(0, tiles, step):
            pieces = []
            for t in range(groups):
                base = ((z * groups + t) * tiles + c0) * SUB
                pieces.append(
                    jnp.concatenate(
                        [rows_ref[pl.ds(base + c * SUB, SUB), :] for c in range(step)], axis=1
                    )
                )
            field = jnp.concatenate(pieces, axis=0)
            weight = perturb_ref[pl.ds(z, 1), c0 * LANES : (c0 + step) * LANES]
            both = jnp.concatenate([field, field * weight], axis=0)
            high = both.astype(jnp.bfloat16)
            low = (both - high.astype(f32)).astype(jnp.bfloat16)
            left = jnp.concatenate([high, low], axis=0)
            right = jnp.concatenate([high[:norb], low[:norb]], axis=0)
            total = total + lax.dot_general(
                left, right, (((1,), (1,)), ((), ())), preferred_element_type=f32
            )
        for t in range(groups):
            base = (z * groups + t) * tiles * SUB
            for s in range(SUB):
                for h in range(halves):
                    for q in range(NY // SUB):
                        start = base + (q * SUB * halves + h) * SUB + s
                        planes_ref[t * SUB + s, z, h * (NY // SUB) + q] = rows_ref[
                            pl.ds(start, SUB, stride=SUB * halves), :
                        ]
        return total

    total = lax.fori_loop(0, layers, layer, jnp.zeros((4 * norb, 2 * norb), f32))
    total = total[: 2 * norb] + total[2 * norb :]
    gram_ref[...] = total[:, :norb] + total[:, norb:]


def small_matrices(norb, gram_refs, ncell):
    total = add_all(gram_refs)
    overlap, weighted = total[:norb], total[norb:]
    twice = jnp.dot(overlap, weighted, precision=HIGHEST, preferred_element_type=f32) * (1.0 / ncell)
    return overlap, weighted, twice


def combine(layers, group, norb, planes_ref, coef_ref, start, finish):
    def layer(z, carry):
        sums = [start(n, z) for n in range(group)]
        for m in range(norb):
            field = planes_ref[m, z]
            for n in range(group):
                sums[n] = sums[n] + field * coef_ref[pl.ds(n * norb + m, 1), :]
        for n in range(group):
            finish(n, z, sums[n])
        return carry

    lax.fori_loop(0, layers, layer, 0)


def inner_kernel(shape, ncell, planes_ref, perturb_ref, *refs):
    norb, layers, group, parts = shape
    gram_refs, inner_ref, coef_ref = refs[:parts], refs[parts], refs[parts + 1]
    first = lax.axis_index("orb") * group
    overlap, weighted, twice = small_matrices(norb, gram_refs, ncell)
    coefs = (2.0 * weighted - twice) * (1.0 / ncell)
    for n in range(group):
        coef_ref[n * norb : (n + 1) * norb, :] = column(coefs, first + n)

    def start(n, z):
        return -(perturb_ref[z] * planes_ref[first + n, z])

    def finish(n, z, value):
        inner_ref[n, z] = value

    combine(layers, group, norb, planes_ref, coef_ref, start, finish)


def roll_x(halves_list, amount):
    count = len(halves_list)
    lane = lax.broadcasted_iota(jnp.int32, halves_list[0].shape, 1)
    turned = [pltpu.roll(v, amount % LANES, 1) for v in halves_list]
    if amount > 0:
        return [jnp.where(lane >= amount, turned[h], turned[(h - 1) % count]) for h in range(count)]
    return [
        jnp.where(lane < LANES + amount, turned[h], turned[(h + 1) % count]) for h in range(count)
    ]


def roll_y(value, amount):
    return pltpu.roll(value, amount % NY, 0)


def local_kernel(shape, ncell, shift_ref, planes_ref, perturb_ref, potential_ref, inner_ref, *refs):
    norb, layers, group, parts, halves = shape
    gram_refs = refs[:parts]
    source_ref, partial_ref, overlap_ref, along_ref, square_ref, coef_ref = refs[parts:]
    first = lax.axis_index("orb") * group
    overlap, weighted, twice = small_matrices(norb, gram_refs, ncell)
    for m in range(norb):
        overlap_ref[m] = column(overlap, m)
    for n in range(group):
        rows = slice(n * norb, (n + 1) * norb)
        coef_ref[rows, :] = column(weighted * (1.0 / ncell), first + n)
        along_ref[rows, :] = column(twice - weighted, first + n)
    square_ref[...] = jnp.zeros_like(square_ref)

    def start(n, z):
        return -(perturb_ref[z] * planes_ref[first + n, z])

    def finish(n, z, value):
        source_ref[n, z] = value
        square_ref[n] += jnp.sum(value * value, axis=0)

    combine(layers, group, norb, planes_ref, coef_ref, start, finish)

    for n in range(group):
        def layer(z, carry):
            plane = blocks(inner_ref[n, z])
            sheets = [plane[h] for h in range(halves)]
            sums = [(3.0 * COEFFS[0]) * v for v in sheets]
            for k in range(1, 7):
                right, left = roll_x(sheets, k), roll_x(sheets, -k)
                for h in range(halves):
                    around = right[h] + left[h] + roll_y(sheets[h], k) + roll_y(sheets[h], -k)
                    sums[h] = sums[h] + COEFFS[k] * around
            total = jnp.stack(sums).reshape(inner_ref.shape[2:])
            shift = potential_ref[z] + shift_ref[n]
            partial_ref[n, z] = shift * inner_ref[n, z] - 0.5 * total
            return carry

        lax.fori_loop(0, layers, layer, 0)
        for z in range(layers):
            total = None
            for other in range(layers):
                k = abs(other - z)
                if k == 0 or k > 6:
                    continue
                term = (-0.5 * COEFFS[k]) * inner_ref[n, other]
                total = term if total is None else total + term
            if total is not None:
                partial_ref[n, z] += total


def image_kernel(shape, planes_ref, inner_ref, partial_ref, square_ref, before_ref, after_ref, applied_ref, sums_ref, acc_ref):
    norb, layers, group = shape
    acc_ref[...] = jnp.zeros_like(acc_ref)
    for n in range(group):
        for z in range(layers):
            total = partial_ref[n, z]
            for j in range(layers):
                k = z + layers - j
                if k <= 6:
                    total = total + (-0.5 * COEFFS[k]) * before_ref[n, j]
                k = j + layers - z
                if k <= 6:
                    total = total + (-0.5 * COEFFS[k]) * after_ref[n, j]
            applied_ref[n, z] = total

    def layer(z, carry):
        fields = [applied_ref[n, z] for n in range(group)]
        for n in range(group):
            acc_ref[group * norb + n] += jnp.sum(fields[n] * inner_ref[n, z], axis=0)
        for m in range(norb):
            orbital = planes_ref[m, z]
            for n in range(group):
                acc_ref[n * norb + m] += jnp.sum(orbital * fields[n], axis=0)
        return carry

    lax.fori_loop(0, layers, layer, 0)
    count = group * norb + group
    sums_ref[:count, :] = jnp.sum(acc_ref[:count], axis=1)
    sums_ref[count : count + group, :] = jnp.sum(square_ref[...], axis=1)
    if sums_ref.shape[0] > count + group:
        sums_ref[count + group :, :] = jnp.zeros((sums_ref.shape[0] - count - group, LANES), f32)


def spread(value):
    return jnp.broadcast_to(jnp.sum(value, axis=1, keepdims=True), value.shape)


def residual_kernel(shape, ncell, planes_ref, source_ref, applied_ref, overlap_ref, along_ref, *refs):
    norb, layers, group, parts = shape
    sums_refs = refs[:parts]
    ahead_ref, plain_ref, numbers_ref, coef_ref, step_ref = refs[parts:]
    total = spread(add_all(sums_refs))
    count = group * norb
    curve = total[count : count + group]
    norm = total[count + group : count + 2 * group]
    step = norm / curve
    numbers_ref[:group, :] = norm
    numbers_ref[group : 2 * group, :] = curve
    numbers_ref[2 * group : 3 * group, :] = step
    step_ref[...] = step
    for n in range(group):
        rows = slice(n * norb, (n + 1) * norb)
        product = total[rows]
        alpha = step[n : n + 1]
        again = jnp.zeros((norb, LANES), f32)
        for m in range(norb):
            again = again + overlap_ref[m] * product[m : m + 1]
        left = along_ref[rows, :] - alpha * (product - again * (1.0 / ncell))
        plain_ref[rows, :] = alpha * product * (1.0 / ncell)
        coef_ref[rows, :] = (alpha * product - left) * (1.0 / ncell)

    def start(n, z):
        return source_ref[n, z] - step_ref[n : n + 1, :] * applied_ref[n, z]

    def finish(n, z, value):
        ahead_ref[n, z] = value

    combine(layers, group, norb, planes_ref, coef_ref, start, finish)


def second_kernel(shape, shift_ref, planes_ref, potential_ref, source_ref, applied_ref, ahead_ref, plain_ref, numbers_ref, residual_ref, acc_ref):
    norb, layers, group, halves = shape
    acc_ref[...] = jnp.zeros_like(acc_ref)

    def start(n, z):
        alpha = numbers_ref[2 * group + n : 2 * group + n + 1, :]
        return source_ref[n, z] - alpha * applied_ref[n, z]

    def finish(n, z, value):
        residual_ref[n, z] = value
        acc_ref[2 * group + n] += jnp.sum(value * value, axis=0)

    combine(layers, group, norb, planes_ref, plain_ref, start, finish)

    for n in range(group):
        def layer(z, carry):
            whole = ahead_ref[n, z]
            plane = blocks(whole)
            sheets = [plane[h] for h in range(halves)]
            sums = [(-1.5 * COEFFS[0]) * v for v in sheets]
            for k in range(1, 7):
                right = roll_x(sheets, k)
                for h in range(halves):
                    sums[h] = sums[h] - COEFFS[k] * (right[h] + roll_y(sheets[h], k))
            total = jnp.stack(sums).reshape(whole.shape)
            total = total + (potential_ref[z] + shift_ref[n]) * whole
            acc_ref[n] += jnp.sum(whole * total, axis=0)
            acc_ref[group + n] += jnp.sum(whole * applied_ref[n, z], axis=0)
            return carry

        lax.fori_loop(0, layers, layer, 0)
        for z in range(layers - 1):
            total = None
            for other in range(z + 1, min(layers, z + 7)):
                term = -COEFFS[other - z] * ahead_ref[n, other]
                total = term if total is None else total + term
            acc_ref[n] += jnp.sum(ahead_ref[n, z] * total, axis=0)


def pairs_kernel(shape, ahead_ref, after_ref, acc_ref, sums_ref):
    layers, group = shape
    sums_ref[...] = jnp.sum(acc_ref[...], axis=1)
    for n in range(group):
        total = None
        for z in range(layers):
            line = None
            for j in range(layers):
                k = j + layers - z
                if k <= 6:
                    term = -COEFFS[k] * after_ref[n, j]
                    line = term if line is None else line + term
            if line is not None:
                line = line * ahead_ref[n, z]
                total = line if total is None else total + line
        sums_ref[n : n + 1, :] += jnp.sum(jnp.sum(total, axis=0), axis=0, keepdims=True)


def density_kernel(shape, planes_ref, source_ref, residual_ref, numbers_ref, *refs):
    layers, group, parts, halves, members, width, margin = shape
    sums_refs = refs[:parts]
    cuts_ref, scales_ref, ring_ref = refs[parts:]
    first = lax.axis_index("orb")
    total = spread(add_all(sums_refs))
    norm, curve, alpha = (numbers_ref[i * group : (i + 1) * group, :] for i in range(3))
    squares, cross, bend = total[2 * group : 3 * group], total[group : 2 * group], total[:group]
    beta = squares / norm
    bend = bend + 2.0 * beta * cross + beta * beta * curve
    second = squares / bend
    scales_ref[:group, :] = alpha + second * beta
    scales_ref[group : 2 * group, :] = second

    def layer(z, carry):
        total = jnp.zeros(planes_ref.shape[2:], f32)
        for n in range(group):
            field = scales_ref[n : n + 1, :] * source_ref[n, z]
            field = field + scales_ref[group + n : group + n + 1, :] * residual_ref[n, z]
            total = total + field * planes_ref[first * group + n, z]
        total = blocks(4.0 * total)
        for h in range(halves):
            ring_ref[z, h, SUB : SUB + NY, :] = total[h]
            ring_ref[z, h, :SUB, :] = total[h, NY - SUB :]
            ring_ref[z, h, SUB + NY :, :] = total[h, :SUB]
        return carry

    lax.fori_loop(0, layers, layer, 0)
    for k in range(members):
        owner = lax.rem(first + k, members)
        for z in range(layers):
            for h in range(halves):
                cuts_ref[k, z, h] = ring_ref[z, h, pl.ds(owner * width + SUB - margin, width + 2 * margin), :]


def response_kernel(shape, source_ref, residual_ref, scales_ref, response_ref):
    layers, group, halves = shape
    tiles = NY * halves

    def layer(z, carry):
        for n in range(group):
            field = scales_ref[n : n + 1, :] * source_ref[n, z]
            field = field + scales_ref[group + n : group + n + 1, :] * residual_ref[n, z]
            for h in range(halves):
                for q in range(NY // SUB):
                    start = (z * tiles + q * SUB * halves + h) * group + n
                    response_ref[pl.ds(start, SUB, stride=group * halves), :] = field[h * (NY // SUB) + q]
        return carry

    lax.fori_loop(0, layers, layer, 0)


def gather_kernel(cuts_ref, *refs):
    total = cuts_ref[0]
    for ref in refs[:-1]:
        total = total + ref[...]
    refs[-1][...] = total


def jacobi_kernel(shape, dense_ref, before_ref, after_ref, induced_ref):
    layers, halves, width, margin = shape
    scale = 1.0 / (6.0 + SCREEN)
    dense = [[before_ref[j, h] for h in range(halves)] for j in range(2)]
    dense = dense + [[dense_ref[z, h] for h in range(halves)] for z in range(layers)]
    dense = dense + [[after_ref[j, h] for h in range(halves)] for j in range(2)]
    field = [[scale * v for v in sheet] for sheet in dense]
    rows = width + 2 * margin

    def up(value):
        return pltpu.roll(value, 1, 0)

    def down(value):
        return pltpu.roll(value, rows - 1, 0)

    for sweep in range(2):
        fresh = []
        for z in range(1, len(field) - 1):
            right, left = roll_x(field[z], 1), roll_x(field[z], -1)
            sheet = []
            for h in range(halves):
                value = dense[z][h] + field[z - 1][h] + field[z + 1][h] + right[h] + left[h]
                value = value + up(field[z][h]) + down(field[z][h])
                sheet.append(scale * value)
            fresh.append(sheet)
        field, dense = fresh, dense[1:-1]
    for z in range(layers):
        for h in range(halves):
            for y in range(width):
                c = y * halves + h
                induced_ref[z : z + 1, c * LANES : (c + 1) * LANES] = field[z][h][margin + y : margin + y + 1]


def per_device(orbitals, potential, perturb, energies, omega):
    norb, layers, columns = orbitals.shape
    group = energies.shape[0]
    bricks, members = lax.axis_size("brick"), lax.axis_size("orb")
    ncell = layers * bricks * columns
    halves = columns // NY // LANES
    tiles = columns // LANES
    spots = tiles // SUB
    rows = orbitals.transpose(1, 0, 2).reshape(layers, norb // SUB, SUB, tiles, LANES)
    rows = rows.transpose(0, 1, 3, 2, 4).reshape(layers * norb * tiles, LANES)

    def as_planes(array):
        array = array.reshape(layers, NY, halves, LANES).transpose(0, 2, 1, 3)
        return array.reshape(layers, spots, SUB, LANES)

    shift = omega[0] - energies
    own = (group, layers, spots, SUB, LANES)
    flat = (group * norb, LANES)

    planes, gram = call(
        functools.partial(gram_kernel, (norb, layers, halves)),
        [(norb, layers, spots, SUB, LANES), (2 * norb, norb)],
        [],
        0,
        rows,
        perturb,
    )
    grams = parts_of(gram, "brick")
    perturb_planes, potential_planes = as_planes(perturb), as_planes(potential)
    (inner,) = call(
        functools.partial(inner_kernel, (norb, layers, group, len(grams)), ncell),
        [own],
        [flat],
        0,
        planes,
        perturb_planes,
        *grams,
    )
    before, after = shifted(inner, "brick", 1), shifted(inner, "brick", -1)
    source, partial, overlap, along, square = call(
        functools.partial(local_kernel, (norb, layers, group, len(grams), halves), ncell),
        [own, own, (norb, norb, LANES), flat, (group, SUB, LANES)],
        [flat],
        1,
        shift,
        planes,
        perturb_planes,
        potential_planes,
        inner,
        *grams,
    )
    height = -(-(group * norb + 2 * group) // SUB) * SUB
    applied, sums = call(
        functools.partial(image_kernel, (norb, layers, group)),
        [own, (height, LANES)],
        [(group * norb + group, SUB, LANES)],
        0,
        planes,
        inner,
        partial,
        square,
        before,
        after,
    )
    sums = parts_of(sums, "brick")
    ahead, plain, numbers = call(
        functools.partial(residual_kernel, (norb, layers, group, len(sums)), ncell),
        [own, flat, (3 * group, LANES)],
        [flat, (group, LANES)],
        0,
        planes,
        source,
        applied,
        overlap,
        along,
        *sums,
    )
    after = shifted(ahead, "brick", -1)
    residual, acc = call(
        functools.partial(second_kernel, (norb, layers, group, halves)),
        [own, (3 * group, SUB, LANES)],
        [],
        1,
        shift,
        planes,
        potential_planes,
        source,
        applied,
        ahead,
        plain,
        numbers,
    )
    (sums,) = call(
        functools.partial(pairs_kernel, (layers, group)),
        [(3 * group, LANES)],
        [],
        0,
        ahead,
        after,
        acc,
    )
    sums = parts_of(sums, "brick")
    width = NY // members
    margin = 4 if width % SUB == 0 else 2
    cut = (layers, halves, width + 2 * margin, LANES)
    cuts, scales = call(
        functools.partial(density_kernel, (layers, group, len(sums), halves, members, width, margin)),
        [(members,) + cut, (2 * group, LANES)],
        [(layers, halves, NY + 2 * SUB, LANES)],
        0,
        planes,
        source,
        residual,
        numbers,
        *sums,
    )
    others = [shifted(cuts[k], "orb", k) for k in range(1, members)]
    (response,) = call(
        functools.partial(response_kernel, (layers, group, halves)),
        [(layers * tiles * group, LANES)],
        [],
        0,
        source,
        residual,
        scales,
    )
    (dense,) = call(gather_kernel, [cut], [], 0, cuts, *others)
    before = shifted(dense[layers - 2 :], "brick", 1)
    after = shifted(dense[:2], "brick", -1)
    (induced,) = call(
        functools.partial(jacobi_kernel, (layers, halves, width, margin)),
        [(layers, width * halves * LANES)],
        [],
        0,
        dense,
        before,
        after,
    )
    response = response.reshape(layers, tiles, group, LANES).transpose(2, 0, 1, 3)
    return response.reshape(group, layers, columns), induced


def solution(mesh):
    placed = (P(None, "brick", None), P("brick", None), P("brick", None), P("orb"), P("freq"))
    return jax.shard_map(
        per_device,
        mesh=mesh,
        in_specs=placed,
        out_specs=(P(("freq", "orb"), "brick", None), P(("freq", "brick"), "orb")),
        check_vma=False,
    )
```

```python
import functools
import jax
import jax.numpy as jnp
from jax import lax
from jax.experimental import pallas as pl
from jax.experimental.pallas import tpu as pltpu
from jax.sharding import PartitionSpec as P

NY = 32
LANES = 128
SUB = 8

COEFFS = (
    -5369.0 / 1800.0,
    12.0 / 7.0,
    -15.0 / 56.0,
    10.0 / 189.0,
    -1.0 / 112.0,
    2.0 / 825.0,
    -1.0 / 5544.0,
)
SCREEN = 0.25
HIGHEST = lax.Precision.HIGHEST
VMEM_LIMIT = 16 * 1024 * 1024
SMEM = pl.BlockSpec(memory_space=pltpu.SMEM)
VMEM = pl.BlockSpec(memory_space=pltpu.VMEM)
HBM = pl.BlockSpec(memory_space=pltpu.HBM)
f32 = jnp.float32


def call(kernel, outs, scratch, smem, *args, far=0):
    return pl.pallas_call(
        kernel,
        out_shape=[jax.ShapeDtypeStruct(s, f32) for s in outs],
        in_specs=[SMEM] * smem + [HBM] * far + [VMEM] * (len(args) - smem - far),
        out_specs=[VMEM] * len(outs),
        scratch_shapes=[pltpu.VMEM(s, f32) if isinstance(s, tuple) else s for s in scratch],
        compiler_params=pltpu.CompilerParams(vmem_limit_bytes=VMEM_LIMIT),
    )(*args)


def parts_of(array, axis):
    size = lax.axis_size(axis)
    if size > 4 or size & (size - 1):
        return [lax.psum(array, axis)]
    others = [lax.ppermute(array, axis, [(i, i ^ k) for i in range(size)]) for k in range(1, size)]
    return [array] + others


def shifted(array, axis, step):
    size = lax.axis_size(axis)
    return lax.ppermute(array, axis, [(i, (i + step) % size) for i in range(size)])


def add_all(refs):
    total = refs[0][...]
    for ref in refs[1:]:
        total = total + ref[...]
    return total


def rows_to_lanes(matrix):
    count = matrix.shape[0]
    lane = lax.broadcasted_iota(jnp.int32, (count, LANES), 1)
    row = lax.broadcasted_iota(jnp.int32, (count, LANES), 0)
    value = jnp.broadcast_to(jnp.sum(matrix, axis=1, keepdims=True), (count, LANES))
    line = jnp.sum(jnp.where(lane == row, value, 0.0), axis=0, keepdims=True)
    return jnp.broadcast_to(line, (SUB, LANES))


def lanes_to_rows(line, count):
    wide = line.shape[1]
    lane = lax.broadcasted_iota(jnp.int32, (count, wide), 1)
    row = lax.broadcasted_iota(jnp.int32, (count, wide), 0)
    picked = jnp.where(lane == row, jnp.broadcast_to(line, (count, wide)), 0.0)
    return jnp.broadcast_to(jnp.sum(picked, axis=1, keepdims=True), (count, LANES))


def blocks(plane):
    return plane.reshape(-1, NY, LANES)


def gram_kernel(shape, far_rows_ref, far_perturb_ref, planes_ref, gram_ref, rows_ref, perturb_ref, row_sems, perturb_sem):
    norb, layers, halves, group = shape
    groups = norb // SUB
    tiles = NY * halves
    step = 16
    size = norb * tiles
    own = lax.axis_index("orb") * group // SUB

    def fetch(z):
        piece = pl.ds(z * size, size)
        return pltpu.make_async_copy(far_rows_ref.at[piece], rows_ref.at[piece], row_sems.at[z])

    weights = pltpu.make_async_copy(far_perturb_ref, perturb_ref, perturb_sem)
    fetch(0).start()
    weights.start()
    for z in range(1, layers):
        fetch(z).start()
    weights.wait()

    def tile_row(z, t, c0):
        base = ((z * groups + t) * tiles + c0) * SUB
        return jnp.concatenate([rows_ref[pl.ds(base + c * SUB, SUB), :] for c in range(step)], axis=1)

    def rounded(value):
        return value.astype(jnp.bfloat16).astype(f32)

    def layer(z, total):
        fetch(z).wait()
        for c0 in range(0, tiles, step):
            field = jnp.concatenate([tile_row(z, t, c0) for t in range(groups)], axis=0)
            weighted = perturb_ref[pl.ds(z, 1), c0 * LANES : (c0 + step) * LANES] * tile_row(z, own, c0)
            rest = (field - rounded(field)).astype(jnp.bfloat16)
            field = field.astype(jnp.bfloat16)
            pair = jnp.concatenate([weighted, weighted - rounded(weighted)], axis=0).astype(jnp.bfloat16)
            left = jnp.concatenate([field, rest, pair], axis=0)
            right = jnp.concatenate([field, rest], axis=0)
            total = total + lax.dot_general(
                left, right, (((1,), (1,)), ((), ())), preferred_element_type=f32
            )
        for t in range(groups):
            base = (z * groups + t) * tiles * SUB
            for s in range(SUB):
                for h in range(halves):
                    for q in range(NY // SUB):
                        start = base + (q * SUB * halves + h) * SUB + s
                        planes_ref[t * SUB + s, z, h * (NY // SUB) + q] = rows_ref[
                            pl.ds(start, SUB, stride=SUB * halves), :
                        ]
        return total

    total = lax.fori_loop(0, layers, layer, jnp.zeros((2 * norb + 2 * SUB, 2 * norb), f32))
    total = total[:, :norb] + total[:, norb:]
    gram_ref[:norb, :] = total[:norb] + total[norb : 2 * norb]
    gram_ref[norb:, :] = total[2 * norb : 2 * norb + SUB] + total[2 * norb + SUB :]


def small_matrices(shape, ncell, gram_refs, lines_ref):
    norb, group = shape
    total = add_all(gram_refs)
    overlap = total[:norb]
    lines_ref[...] = total[norb:]
    start = lax.rem(lax.axis_index("orb") * group, SUB)
    rows = []
    for n in range(group):
        line = lines_ref[pl.ds(start + n, 1), :]
        again = jnp.sum(lanes_to_rows(line, norb)[:, :norb] * overlap, axis=0, keepdims=True)
        rows.append((line, again * (1.0 / ncell)))
    return overlap, rows


def combine(layers, group, norb, planes_ref, coef_ref, start, finish):
    def layer(z, carry):
        sums = [start(n, z) for n in range(group)]
        for m in range(norb):
            field = planes_ref[m, z]
            for n in range(group):
                sums[n] = sums[n] + field * coef_ref[pl.ds(n * norb + m, 1), :]
        for n in range(group):
            finish(n, z, sums[n])
        return carry

    lax.fori_loop(0, layers, layer, 0)


def inner_kernel(shape, ncell, planes_ref, perturb_ref, *refs):
    norb, layers, group, parts, share = shape
    gram_refs = refs[:parts]
    inner_ref, rest_ref = refs[parts : parts + 2]
    coef_ref, lines_ref = refs[-2:]
    first = lax.axis_index("orb") * group
    overlap, rows = small_matrices((norb, group), ncell, gram_refs, lines_ref)
    for n, (line, again) in enumerate(rows):
        coefs = (2.0 * line - again) * (1.0 / ncell)
        coef_ref[n * norb : (n + 1) * norb, :] = lanes_to_rows(coefs, norb)
    place = lax.axis_index("freq") * share

    def start(n, z):
        return -(perturb_ref[z] * planes_ref[first + n, z])

    def finish(n, z, value):
        inner_ref[n, z] = value
        rest_ref[n, z] = value[2 * share :]
        if share:
            refs[parts + 2][n, z] = inner_ref[n, z, pl.ds(place, share)]

    combine(layers, group, norb, planes_ref, coef_ref, start, finish)


def roll_x(halves_list, amount):
    count = len(halves_list)
    lane = lax.broadcasted_iota(jnp.int32, halves_list[0].shape, 1)
    turned = [pltpu.roll(v, amount % LANES, 1) for v in halves_list]
    if amount > 0:
        return [jnp.where(lane >= amount, turned[h], turned[(h - 1) % count]) for h in range(count)]
    return [
        jnp.where(lane < LANES + amount, turned[h], turned[(h + 1) % count]) for h in range(count)
    ]


def roll_y(value, amount):
    return pltpu.roll(value, amount % NY, 0)


def local_kernel(shape, ncell, shift_ref, planes_ref, perturb_ref, potential_ref, inner_ref, *refs):
    norb, layers, group, parts, halves = shape
    gram_refs = refs[:parts]
    source_ref, partial_ref, overlap_ref, along_ref, square_ref, coef_ref, lines_ref = refs[parts:]
    first = lax.axis_index("orb") * group
    overlap, rows = small_matrices((norb, group), ncell, gram_refs, lines_ref)
    for m in range(norb):
        overlap_ref[m] = jnp.broadcast_to(overlap[:, m : m + 1], (norb, LANES))
    for n, (line, again) in enumerate(rows):
        place = slice(n * norb, (n + 1) * norb)
        coef_ref[place, :] = lanes_to_rows(line * (1.0 / ncell), norb)
        along_ref[place, :] = lanes_to_rows(again - line, norb)
    square_ref[...] = jnp.zeros_like(square_ref)

    def start(n, z):
        return -(perturb_ref[z] * planes_ref[first + n, z])

    def finish(n, z, value):
        source_ref[n, z] = value
        square_ref[n] += jnp.sum(value * value, axis=0)

    combine(layers, group, norb, planes_ref, coef_ref, start, finish)

    for n in range(group):
        def layer(z, carry):
            plane = blocks(inner_ref[n, z])
            sheets = [plane[h] for h in range(halves)]
            sums = [(3.0 * COEFFS[0]) * v for v in sheets]
            for k in range(1, 7):
                right, left = roll_x(sheets, k), roll_x(sheets, -k)
                for h in range(halves):
                    around = right[h] + left[h] + roll_y(sheets[h], k) + roll_y(sheets[h], -k)
                    sums[h] = sums[h] + COEFFS[k] * around
            total = jnp.stack(sums).reshape(inner_ref.shape[2:])
            shift = potential_ref[z] + shift_ref[n]
            partial_ref[n, z] = shift * inner_ref[n, z] - 0.5 * total
            return carry

        lax.fori_loop(0, layers, layer, 0)
        for z in range(layers):
            total = None
            for other in range(layers):
                k = abs(other - z)
                if k == 0 or k > 6:
                    continue
                term = (-0.5 * COEFFS[k]) * inner_ref[n, other]
                total = term if total is None else total + term
            if total is not None:
                partial_ref[n, z] += total


def halo_sum(layers, n, z, before_ref, after_ref):
    total = None
    for j in range(layers):
        for k, ref in ((z + layers - j, before_ref), (j + layers - z, after_ref)):
            if k <= 6:
                term = (-0.5 * COEFFS[k]) * ref[n, j]
                total = term if total is None else total + term
    return total


def halo_kernel(shape, before_ref, after_ref, halo_ref):
    layers, group = shape
    for n in range(group):
        for z in range(layers):
            halo_ref[n, z] = halo_sum(layers, n, z, before_ref, after_ref)


def image_kernel(shape, planes_ref, inner_ref, partial_ref, square_ref, before_ref, after_ref, *refs):
    norb, layers, group, share = shape
    applied_ref, sums_ref, acc_ref = refs[-3:]
    place = lax.axis_index("freq") * share
    acc_ref[...] = jnp.zeros_like(acc_ref)
    for n in range(group):
        for z in range(layers):
            applied_ref[n, z, 2 * share :] = partial_ref[n, z, 2 * share :] + halo_sum(
                layers, n, z, before_ref, after_ref
            )
            if share:
                mine, other = pl.ds(place, share), pl.ds(share - place, share)
                applied_ref[n, z, mine] = partial_ref[n, z, mine] + refs[0][n, z]
                applied_ref[n, z, other] = partial_ref[n, z, other] + refs[1][n, z]

    def layer(z, carry):
        fields = [applied_ref[n, z] for n in range(group)]
        for n in range(group):
            acc_ref[group * norb + n] += jnp.sum(fields[n] * inner_ref[n, z], axis=0)
        for m in range(norb):
            orbital = planes_ref[m, z]
            for n in range(group):
                acc_ref[n * norb + m] += jnp.sum(orbital * fields[n], axis=0)
        return carry

    lax.fori_loop(0, layers, layer, 0)
    totals = jnp.concatenate([jnp.sum(acc_ref[...], axis=1), jnp.sum(square_ref[...], axis=1)], axis=0)
    sums_ref[...] = rows_to_lanes(totals)


def residual_kernel(shape, ncell, planes_ref, source_ref, applied_ref, overlap_ref, along_ref, *refs):
    norb, layers, group, parts = shape
    sums_refs = refs[:parts]
    ahead_ref, plain_ref, numbers_ref, coef_ref, step_ref = refs[parts:]
    count = group * norb
    total = lanes_to_rows(add_all(sums_refs)[:1], count + 2 * group)
    curve = total[count : count + group]
    norm = total[count + group : count + 2 * group]
    step = norm / curve
    numbers_ref[:group, :] = norm
    numbers_ref[group : 2 * group, :] = curve
    numbers_ref[2 * group : 3 * group, :] = step
    step_ref[...] = step
    for n in range(group):
        rows = slice(n * norb, (n + 1) * norb)
        product = total[rows]
        alpha = step[n : n + 1]
        again = jnp.zeros((norb, LANES), f32)
        for m in range(norb):
            again = again + overlap_ref[m] * product[m : m + 1]
        left = along_ref[rows, :] - alpha * (product - again * (1.0 / ncell))
        plain_ref[rows, :] = alpha * product * (1.0 / ncell)
        coef_ref[rows, :] = (alpha * product - left) * (1.0 / ncell)

    def start(n, z):
        return source_ref[n, z] - step_ref[n : n + 1, :] * applied_ref[n, z]

    def finish(n, z, value):
        ahead_ref[n, z] = value

    combine(layers, group, norb, planes_ref, coef_ref, start, finish)


def second_kernel(shape, shift_ref, planes_ref, potential_ref, source_ref, applied_ref, ahead_ref, plain_ref, numbers_ref, residual_ref, acc_ref):
    norb, layers, group, halves = shape
    acc_ref[...] = jnp.zeros_like(acc_ref)

    def start(n, z):
        alpha = numbers_ref[2 * group + n : 2 * group + n + 1, :]
        return source_ref[n, z] - alpha * applied_ref[n, z]

    def finish(n, z, value):
        residual_ref[n, z] = value
        acc_ref[2 * group + n] += jnp.sum(value * value, axis=0)

    combine(layers, group, norb, planes_ref, plain_ref, start, finish)

    for n in range(group):
        def layer(z, carry):
            whole = ahead_ref[n, z]
            plane = blocks(whole)
            sheets = [plane[h] for h in range(halves)]
            sums = [(-1.5 * COEFFS[0]) * v for v in sheets]
            for k in range(1, 7):
                right = roll_x(sheets, k)
                for h in range(halves):
                    sums[h] = sums[h] - COEFFS[k] * (right[h] + roll_y(sheets[h], k))
            total = jnp.stack(sums).reshape(whole.shape)
            total = total + (potential_ref[z] + shift_ref[n]) * whole
            acc_ref[n] += jnp.sum(whole * total, axis=0)
            acc_ref[group + n] += jnp.sum(whole * applied_ref[n, z], axis=0)
            return carry

        lax.fori_loop(0, layers, layer, 0)
        for z in range(layers - 1):
            total = None
            for other in range(z + 1, min(layers, z + 7)):
                term = -COEFFS[other - z] * ahead_ref[n, other]
                total = term if total is None else total + term
            acc_ref[n] += jnp.sum(ahead_ref[n, z] * total, axis=0)


def pairs_kernel(shape, ahead_ref, after_ref, acc_ref, sums_ref):
    layers, group = shape
    sums = jnp.sum(acc_ref[...], axis=1)
    lines = []
    for n in range(group):
        total = None
        for z in range(layers):
            line = None
            for j in range(layers):
                k = j + layers - z
                if k <= 6:
                    term = -COEFFS[k] * after_ref[n, j]
                    line = term if line is None else line + term
            if line is not None:
                line = line * ahead_ref[n, z]
                total = line if total is None else total + line
        lines.append(jnp.sum(jnp.sum(total, axis=0), axis=0, keepdims=True))
    sums_ref[...] = rows_to_lanes(jnp.concatenate([sums[:group] + jnp.concatenate(lines, axis=0), sums[group:]], axis=0))


def density_kernel(shape, planes_ref, source_ref, residual_ref, numbers_ref, *refs):
    layers, group, parts, halves, members, width, margin = shape
    sums_refs = refs[:parts]
    cuts_ref, scales_ref, ring_ref = refs[parts:]
    first = lax.axis_index("orb")
    total = lanes_to_rows(add_all(sums_refs)[:1], 3 * group)
    norm, curve, alpha = (numbers_ref[i * group : (i + 1) * group, :] for i in range(3))
    squares, cross, bend = total[2 * group : 3 * group], total[group : 2 * group], total[:group]
    beta = squares / norm
    bend = bend + 2.0 * beta * cross + beta * beta * curve
    second = squares / bend
    scales_ref[:group, :] = alpha + second * beta
    scales_ref[group : 2 * group, :] = second

    def layer(z, carry):
        total = jnp.zeros(planes_ref.shape[2:], f32)
        for n in range(group):
            field = scales_ref[n : n + 1, :] * source_ref[n, z]
            field = field + scales_ref[group + n : group + n + 1, :] * residual_ref[n, z]
            total = total + field * planes_ref[first * group + n, z]
        total = blocks(4.0 * total)
        for h in range(halves):
            ring_ref[z, h, SUB : SUB + NY, :] = total[h]
            ring_ref[z, h, :SUB, :] = total[h, NY - SUB :]
            ring_ref[z, h, SUB + NY :, :] = total[h, :SUB]
        return carry

    lax.fori_loop(0, layers, layer, 0)
    for k in range(members):
        owner = lax.rem(first + k, members)
        for z in range(layers):
            for h in range(halves):
                rows = width + 2 * margin
                cuts_ref[k, pl.ds((z * halves + h) * rows, rows)] = ring_ref[
                    z, h, pl.ds(owner * width + SUB - margin, rows), :
                ]


def response_kernel(shape, source_ref, residual_ref, scales_ref, response_ref):
    layers, group, halves = shape
    tiles = NY * halves

    def layer(z, carry):
        for n in range(group):
            field = scales_ref[n : n + 1, :] * source_ref[n, z]
            field = field + scales_ref[group + n : group + n + 1, :] * residual_ref[n, z]
            for h in range(halves):
                for q in range(NY // SUB):
                    start = (z * tiles + q * SUB * halves + h) * group + n
                    response_ref[pl.ds(start, SUB, stride=group * halves), :] = field[h * (NY // SUB) + q]
        return carry

    lax.fori_loop(0, layers, layer, 0)


def gather_kernel(edge, cuts_ref, *refs):
    dense_ref, top_ref, bottom_ref = refs[-3:]
    total = cuts_ref[0]
    for ref in refs[:-3]:
        total = total + ref[...]
    dense_ref[...] = total
    top_ref[...] = total[-edge:]
    bottom_ref[...] = total[:edge]


def jacobi_kernel(shape, dense_ref, before_ref, after_ref, induced_ref):
    layers, halves, width, margin = shape
    rows = width + 2 * margin
    scale = 1.0 / (6.0 + SCREEN)

    def sheets(ref, count):
        return [[ref[pl.ds((z * halves + h) * rows, rows), :] for h in range(halves)] for z in range(count)]

    dense = sheets(before_ref, 2) + sheets(dense_ref, layers) + sheets(after_ref, 2)
    field = [[scale * v for v in sheet] for sheet in dense]

    def up(value):
        return pltpu.roll(value, 1, 0)

    def down(value):
        return pltpu.roll(value, rows - 1, 0)

    for sweep in range(2):
        fresh = []
        for z in range(1, len(field) - 1):
            right, left = roll_x(field[z], 1), roll_x(field[z], -1)
            sheet = []
            for h in range(halves):
                value = dense[z][h] + field[z - 1][h] + field[z + 1][h] + right[h] + left[h]
                value = value + up(field[z][h]) + down(field[z][h])
                sheet.append(scale * value)
            fresh.append(sheet)
        field, dense = fresh, dense[1:-1]
    for z in range(layers):
        for h in range(halves):
            for y in range(width):
                c = y * halves + h
                induced_ref[z : z + 1, c * LANES : (c + 1) * LANES] = field[z][h][margin + y : margin + y + 1]


def per_device(orbitals, potential, perturb, energies, omega):
    norb, layers, columns = orbitals.shape
    group = energies.shape[0]
    bricks, members = lax.axis_size("brick"), lax.axis_size("orb")
    ncell = layers * bricks * columns
    halves = columns // NY // LANES
    tiles = columns // LANES
    spots = tiles // SUB
    rows = orbitals.transpose(1, 0, 2).reshape(layers, norb // SUB, SUB, tiles, LANES)
    rows = rows.transpose(0, 1, 3, 2, 4).reshape(layers * norb * tiles, LANES)

    def as_planes(array):
        array = array.reshape(layers, NY, halves, LANES).transpose(0, 2, 1, 3)
        return array.reshape(layers, spots, SUB, LANES)

    shift = omega[0] - energies
    own = (group, layers, spots, SUB, LANES)
    flat = (group * norb, LANES)

    size = norb * tiles
    planes, gram = call(
        functools.partial(gram_kernel, (norb, layers, halves, group)),
        [(norb, layers, spots, SUB, LANES), (norb + SUB, norb)],
        [
            (layers * size, LANES),
            (layers, columns),
            pltpu.SemaphoreType.DMA((layers,)),
            pltpu.SemaphoreType.DMA,
        ],
        0,
        rows,
        perturb,
        far=2,
    )
    grams = parts_of(gram, "brick")
    perturb_planes, potential_planes = as_planes(perturb), as_planes(potential)
    share = 3 * spots // 8 if lax.axis_size("freq") == 2 else 0
    cells = (SUB, LANES)
    inner, rest, *shared = call(
        functools.partial(inner_kernel, (norb, layers, group, len(grams), share), ncell),
        [own, (group, layers, spots - 2 * share) + cells] + [(group, layers, share) + cells] * (share > 0),
        [flat, (SUB, norb)],
        0,
        planes,
        perturb_planes,
        *grams,
    )
    halos = []
    if share:
        before, after = shifted(shared[0], "brick", 1), shifted(shared[0], "brick", -1)
        halos = call(
            functools.partial(halo_kernel, (layers, group)), [shared[0].shape], [], 0, before, after
        )
        halos = [halos[0], lax.ppermute(halos[0], "freq", [(0, 1), (1, 0)])]
    before, after = shifted(rest, "brick", 1), shifted(rest, "brick", -1)
    source, partial, overlap, along, square = call(
        functools.partial(local_kernel, (norb, layers, group, len(grams), halves), ncell),
        [own, own, (norb, norb, LANES), flat, (group, SUB, LANES)],
        [flat, (SUB, norb)],
        1,
        shift,
        planes,
        perturb_planes,
        potential_planes,
        inner,
        *grams,
    )
    applied, sums = call(
        functools.partial(image_kernel, (norb, layers, group, share)),
        [own, cells],
        [(group * norb + group,) + cells],
        0,
        planes,
        inner,
        partial,
        square,
        before,
        after,
        *halos,
    )
    sums = parts_of(sums, "brick")
    ahead, plain, numbers = call(
        functools.partial(residual_kernel, (norb, layers, group, len(sums)), ncell),
        [own, flat, (3 * group, LANES)],
        [flat, (group, LANES)],
        0,
        planes,
        source,
        applied,
        overlap,
        along,
        *sums,
    )
    after = shifted(ahead, "brick", -1)
    residual, acc = call(
        functools.partial(second_kernel, (norb, layers, group, halves)),
        [own, (3 * group, SUB, LANES)],
        [],
        1,
        shift,
        planes,
        potential_planes,
        source,
        applied,
        ahead,
        plain,
        numbers,
    )
    (sums,) = call(
        functools.partial(pairs_kernel, (layers, group)),
        [cells],
        [],
        0,
        ahead,
        after,
        acc,
    )
    sums = parts_of(sums, "brick")
    width = NY // members
    margin = 2
    edge = 2 * halves * (width + 2 * margin)
    cut = (layers * halves * (width + 2 * margin), LANES)
    cuts, scales = call(
        functools.partial(density_kernel, (layers, group, len(sums), halves, members, width, margin)),
        [(members,) + cut, (2 * group, LANES)],
        [(layers, halves, NY + 2 * SUB, LANES)],
        0,
        planes,
        source,
        residual,
        numbers,
        *sums,
    )
    others = [shifted(cuts[k], "orb", k) for k in range(1, members)]
    (response,) = call(
        functools.partial(response_kernel, (layers, group, halves)),
        [(layers * tiles * group, LANES)],
        [],
        0,
        source,
        residual,
        scales,
    )
    dense, top, bottom = call(
        functools.partial(gather_kernel, edge), [cut, (edge, LANES), (edge, LANES)], [], 0, cuts, *others
    )
    before, after = shifted(top, "brick", 1), shifted(bottom, "brick", -1)
    (induced,) = call(
        functools.partial(jacobi_kernel, (layers, halves, width, margin)),
        [(layers, width * halves * LANES)],
        [],
        0,
        dense,
        before,
        after,
    )
    response = response.reshape(layers, tiles, group, LANES).transpose(2, 0, 1, 3)
    return response.reshape(group, layers, columns), induced


def solution(mesh):
    placed = (P(None, "brick", None), P("brick", None), P("brick", None), P("orb"), P("freq"))
    return jax.shard_map(
        per_device,
        mesh=mesh,
        in_specs=placed,
        out_specs=(P(("freq", "orb"), "brick", None), P(("freq", "brick"), "orb")),
        check_vma=False,
    )
```

```python
import functools
import jax
import jax.numpy as jnp
from jax import lax
from jax.experimental import pallas as pl
from jax.experimental.pallas import tpu as pltpu
from jax.sharding import PartitionSpec as P

NY = 32
LANES = 128
SUB = 8

COEFFS = (
    -5369.0 / 1800.0,
    12.0 / 7.0,
    -15.0 / 56.0,
    10.0 / 189.0,
    -1.0 / 112.0,
    2.0 / 825.0,
    -1.0 / 5544.0,
)
SCREEN = 0.25
HIGHEST = lax.Precision.HIGHEST
VMEM_LIMIT = 16 * 1024 * 1024
SMEM = pl.BlockSpec(memory_space=pltpu.SMEM)
VMEM = pl.BlockSpec(memory_space=pltpu.VMEM)
HBM = pl.BlockSpec(memory_space=pltpu.HBM)
f32 = jnp.float32


def call(kernel, outs, scratch, smem, *args, far=0, limit=VMEM_LIMIT):
    return pl.pallas_call(
        kernel,
        out_shape=[jax.ShapeDtypeStruct(s, f32) for s in outs],
        in_specs=[SMEM] * smem + [HBM] * far + [VMEM] * (len(args) - smem - far),
        out_specs=[VMEM] * len(outs),
        scratch_shapes=[pltpu.VMEM(s, f32) if isinstance(s, tuple) else s for s in scratch],
        compiler_params=pltpu.CompilerParams(vmem_limit_bytes=limit),
    )(*args)


def parts_of(array, axis):
    size = lax.axis_size(axis)
    if size > 4 or size & (size - 1):
        return [lax.psum(array, axis)]
    others = [lax.ppermute(array, axis, [(i, i ^ k) for i in range(size)]) for k in range(1, size)]
    return [array] + others


def shifted(array, axis, step):
    size = lax.axis_size(axis)
    return lax.ppermute(array, axis, [(i, (i + step) % size) for i in range(size)])


def add_all(refs):
    total = refs[0][...]
    for ref in refs[1:]:
        total = total + ref[...]
    return total


def rows_to_lanes(matrix):
    count = matrix.shape[0]
    lane = lax.broadcasted_iota(jnp.int32, (count, LANES), 1)
    row = lax.broadcasted_iota(jnp.int32, (count, LANES), 0)
    value = jnp.broadcast_to(jnp.sum(matrix, axis=1, keepdims=True), (count, LANES))
    line = jnp.sum(jnp.where(lane == row, value, 0.0), axis=0, keepdims=True)
    return jnp.broadcast_to(line, (SUB, LANES))


def lanes_to_rows(line, count):
    wide = line.shape[1]
    lane = lax.broadcasted_iota(jnp.int32, (count, wide), 1)
    row = lax.broadcasted_iota(jnp.int32, (count, wide), 0)
    picked = jnp.where(lane == row, jnp.broadcast_to(line, (count, wide)), 0.0)
    return jnp.broadcast_to(jnp.sum(picked, axis=1, keepdims=True), (count, LANES))


def blocks(plane):
    return plane.reshape(-1, NY, LANES)


def gram_kernel(shape, far_rows_ref, far_perturb_ref, planes_ref, gram_ref, rows_ref, perturb_ref, row_sems, perturb_sem):
    norb, layers, halves, group = shape
    groups = norb // SUB
    tiles = NY * halves
    step = 16
    size = norb * tiles
    own = lax.axis_index("orb") * group // SUB

    def fetch(z):
        piece = pl.ds(z * size, size)
        return pltpu.make_async_copy(far_rows_ref.at[piece], rows_ref.at[piece], row_sems.at[z])

    weights = pltpu.make_async_copy(far_perturb_ref, perturb_ref, perturb_sem)
    fetch(0).start()
    weights.start()
    for z in range(1, layers):
        fetch(z).start()
    weights.wait()

    def tile_row(z, t, c0):
        base = ((z * groups + t) * tiles + c0) * SUB
        return jnp.concatenate([rows_ref[pl.ds(base + c * SUB, SUB), :] for c in range(step)], axis=1)

    def rounded(value):
        return value.astype(jnp.bfloat16).astype(f32)

    def layer(z, total):
        fetch(z).wait()
        for c0 in range(0, tiles, step):
            field = jnp.concatenate([tile_row(z, t, c0) for t in range(groups)], axis=0)
            weighted = perturb_ref[pl.ds(z, 1), c0 * LANES : (c0 + step) * LANES] * tile_row(z, own, c0)
            rest = (field - rounded(field)).astype(jnp.bfloat16)
            field = field.astype(jnp.bfloat16)
            pair = jnp.concatenate([weighted, weighted - rounded(weighted)], axis=0).astype(jnp.bfloat16)
            left = jnp.concatenate([field, rest, pair], axis=0)
            right = jnp.concatenate([field, rest], axis=0)
            total = total + lax.dot_general(
                left, right, (((1,), (1,)), ((), ())), preferred_element_type=f32
            )
        for t in range(groups):
            base = (z * groups + t) * tiles * SUB
            for s in range(SUB):
                for h in range(halves):
                    for q in range(NY // SUB):
                        start = base + (q * SUB * halves + h) * SUB + s
                        planes_ref[t * SUB + s, z, h * (NY // SUB) + q] = rows_ref[
                            pl.ds(start, SUB, stride=SUB * halves), :
                        ]
        return total

    total = lax.fori_loop(0, layers, layer, jnp.zeros((2 * norb + 2 * SUB, 2 * norb), f32))
    total = total[:, :norb] + total[:, norb:]
    gram_ref[:norb, :] = total[:norb] + total[norb : 2 * norb]
    gram_ref[norb:, :] = total[2 * norb : 2 * norb + SUB] + total[2 * norb + SUB :]


def tile_kernel(shape, *refs):
    layers, halves = shape
    count = len(refs) // 2
    for array_ref, planes_ref in zip(refs[:count], refs[count:]):
        for z in range(layers):
            for y in range(NY):
                for h in range(halves):
                    c = y * halves + h
                    planes_ref[z, h * (NY // SUB) + y // SUB, y % SUB : y % SUB + 1, :] = array_ref[
                        z : z + 1, c * LANES : (c + 1) * LANES
                    ]


def small_matrices(shape, ncell, gram_refs, lines_ref):
    norb, group = shape
    total = add_all(gram_refs)
    overlap = total[:norb]
    lines_ref[...] = total[norb:]
    start = lax.rem(lax.axis_index("orb") * group, SUB)
    rows = []
    for n in range(group):
        line = lines_ref[pl.ds(start + n, 1), :]
        again = jnp.sum(lanes_to_rows(line, norb)[:, :norb] * overlap, axis=0, keepdims=True)
        rows.append((line, again * (1.0 / ncell)))
    return overlap, rows


def combine(layers, group, norb, planes_ref, coef_ref, start, finish):
    def layer(z, carry):
        sums = [start(n, z) for n in range(group)]
        for m in range(norb):
            field = planes_ref[m, z]
            for n in range(group):
                sums[n] = sums[n] + field * coef_ref[pl.ds(n * norb + m, 1), :]
        for n in range(group):
            finish(n, z, sums[n])
        return carry

    lax.fori_loop(0, layers, layer, 0)


def inner_kernel(shape, ncell, planes_ref, perturb_ref, *refs):
    norb, layers, group, parts, share = shape
    gram_refs = refs[:parts]
    inner_ref, rest_ref = refs[parts : parts + 2]
    coef_ref, lines_ref = refs[-2:]
    first = lax.axis_index("orb") * group
    overlap, rows = small_matrices((norb, group), ncell, gram_refs, lines_ref)
    for n, (line, again) in enumerate(rows):
        coefs = (2.0 * line - again) * (1.0 / ncell)
        coef_ref[n * norb : (n + 1) * norb, :] = lanes_to_rows(coefs, norb)
    place = lax.axis_index("freq") * share

    def start(n, z):
        return -(perturb_ref[z] * planes_ref[first + n, z])

    def finish(n, z, value):
        inner_ref[n, z] = value
        rest_ref[n, z] = value[2 * share :]
        if share:
            refs[parts + 2][n, z] = inner_ref[n, z, pl.ds(place, share)]

    combine(layers, group, norb, planes_ref, coef_ref, start, finish)


def roll_x(halves_list, amount):
    count = len(halves_list)
    lane = lax.broadcasted_iota(jnp.int32, halves_list[0].shape, 1)
    turned = [pltpu.roll(v, amount % LANES, 1) for v in halves_list]
    if amount > 0:
        return [jnp.where(lane >= amount, turned[h], turned[(h - 1) % count]) for h in range(count)]
    return [
        jnp.where(lane < LANES + amount, turned[h], turned[(h + 1) % count]) for h in range(count)
    ]


def roll_y(value, amount):
    return pltpu.roll(value, amount % NY, 0)


def local_kernel(shape, ncell, omega_ref, energies_ref, planes_ref, perturb_ref, potential_ref, inner_ref, *refs):
    norb, layers, group, parts, halves = shape
    gram_refs = refs[:parts]
    source_ref, partial_ref, overlap_ref, along_ref, square_ref, coef_ref, lines_ref = refs[parts:]
    first = lax.axis_index("orb") * group
    overlap, rows = small_matrices((norb, group), ncell, gram_refs, lines_ref)
    for m in range(norb):
        overlap_ref[m] = jnp.broadcast_to(overlap[:, m : m + 1], (norb, LANES))
    for n, (line, again) in enumerate(rows):
        place = slice(n * norb, (n + 1) * norb)
        coef_ref[place, :] = lanes_to_rows(line * (1.0 / ncell), norb)
        along_ref[place, :] = lanes_to_rows(again - line, norb)
    square_ref[...] = jnp.zeros_like(square_ref)

    def start(n, z):
        return -(perturb_ref[z] * planes_ref[first + n, z])

    def finish(n, z, value):
        source_ref[n, z] = value
        square_ref[n] += jnp.sum(value * value, axis=0)

    combine(layers, group, norb, planes_ref, coef_ref, start, finish)

    for n in range(group):
        def layer(z, carry):
            plane = blocks(inner_ref[n, z])
            sheets = [plane[h] for h in range(halves)]
            sums = [(3.0 * COEFFS[0]) * v for v in sheets]
            for k in range(1, 7):
                right, left = roll_x(sheets, k), roll_x(sheets, -k)
                for h in range(halves):
                    around = right[h] + left[h] + roll_y(sheets[h], k) + roll_y(sheets[h], -k)
                    sums[h] = sums[h] + COEFFS[k] * around
            total = jnp.stack(sums).reshape(inner_ref.shape[2:])
            shift = potential_ref[z] + (omega_ref[0] - energies_ref[n])
            partial_ref[n, z] = shift * inner_ref[n, z] - 0.5 * total
            return carry

        lax.fori_loop(0, layers, layer, 0)
        for z in range(layers):
            total = None
            for other in range(layers):
                k = abs(other - z)
                if k == 0 or k > 6:
                    continue
                term = (-0.5 * COEFFS[k]) * inner_ref[n, other]
                total = term if total is None else total + term
            if total is not None:
                partial_ref[n, z] += total


def halo_sum(layers, n, z, before_ref, after_ref):
    total = None
    for j in range(layers):
        for k, ref in ((z + layers - j, before_ref), (j + layers - z, after_ref)):
            if k <= 6:
                term = (-0.5 * COEFFS[k]) * ref[n, j]
                total = term if total is None else total + term
    return total


def halo_kernel(shape, before_ref, after_ref, square_ref, *halo_refs):
    layers, group = shape
    each = group // len(halo_refs)
    for n in range(group):
        for z in range(layers):
            halo_refs[n // each][n % each, z] = halo_sum(layers, n, z, before_ref, after_ref)


def image_kernel(shape, planes_ref, inner_ref, partial_ref, square_ref, before_ref, after_ref, *refs):
    norb, layers, group, share = shape
    applied_ref, sums_ref, acc_ref = refs[-3:]
    pieces = (len(refs) - 3) // 2
    place = lax.axis_index("freq") * share
    acc_ref[...] = jnp.zeros_like(acc_ref)
    for n in range(group):
        for z in range(layers):
            applied_ref[n, z, 2 * share :] = partial_ref[n, z, 2 * share :] + halo_sum(
                layers, n, z, before_ref, after_ref
            )
            if share:
                mine, other = pl.ds(place, share), pl.ds(share - place, share)
                piece, i = divmod(n, group // pieces)
                applied_ref[n, z, mine] = partial_ref[n, z, mine] + refs[piece][i, z]
                applied_ref[n, z, other] = partial_ref[n, z, other] + refs[pieces + piece][i, z]

    def layer(z, carry):
        fields = [applied_ref[n, z] for n in range(group)]
        for n in range(group):
            acc_ref[group * norb + n] += jnp.sum(fields[n] * inner_ref[n, z], axis=0)
        for m in range(norb):
            orbital = planes_ref[m, z]
            for n in range(group):
                acc_ref[n * norb + m] += jnp.sum(orbital * fields[n], axis=0)
        return carry

    lax.fori_loop(0, layers, layer, 0)
    totals = jnp.concatenate([jnp.sum(acc_ref[...], axis=1), jnp.sum(square_ref[...], axis=1)], axis=0)
    sums_ref[...] = rows_to_lanes(totals)


def residual_kernel(shape, ncell, planes_ref, source_ref, applied_ref, overlap_ref, along_ref, *refs):
    norb, layers, group, parts = shape
    sums_refs = refs[:parts]
    ahead_ref, plain_ref, numbers_ref, coef_ref, step_ref = refs[parts:]
    count = group * norb
    total = lanes_to_rows(add_all(sums_refs)[:1], count + 2 * group)
    curve = total[count : count + group]
    norm = total[count + group : count + 2 * group]
    step = norm / curve
    numbers_ref[:group, :] = norm
    numbers_ref[group : 2 * group, :] = curve
    numbers_ref[2 * group : 3 * group, :] = step
    step_ref[...] = step
    for n in range(group):
        rows = slice(n * norb, (n + 1) * norb)
        product = total[rows]
        alpha = step[n : n + 1]
        again = jnp.zeros((norb, LANES), f32)
        for m in range(norb):
            again = again + overlap_ref[m] * product[m : m + 1]
        left = along_ref[rows, :] - alpha * (product - again * (1.0 / ncell))
        plain_ref[rows, :] = alpha * product * (1.0 / ncell)
        coef_ref[rows, :] = (alpha * product - left) * (1.0 / ncell)

    def start(n, z):
        return source_ref[n, z] - step_ref[n : n + 1, :] * applied_ref[n, z]

    def finish(n, z, value):
        ahead_ref[n, z] = value

    combine(layers, group, norb, planes_ref, coef_ref, start, finish)


def second_kernel(shape, omega_ref, energies_ref, planes_ref, potential_ref, source_ref, applied_ref, ahead_ref, plain_ref, numbers_ref, residual_ref, acc_ref):
    norb, layers, group, halves = shape
    acc_ref[...] = jnp.zeros_like(acc_ref)

    def start(n, z):
        alpha = numbers_ref[2 * group + n : 2 * group + n + 1, :]
        return source_ref[n, z] - alpha * applied_ref[n, z]

    def finish(n, z, value):
        residual_ref[n, z] = value
        acc_ref[2 * group + n] += jnp.sum(value * value, axis=0)

    combine(layers, group, norb, planes_ref, plain_ref, start, finish)

    for n in range(group):
        def layer(z, carry):
            whole = ahead_ref[n, z]
            plane = blocks(whole)
            sheets = [plane[h] for h in range(halves)]
            sums = [(-1.5 * COEFFS[0]) * v for v in sheets]
            for k in range(1, 7):
                right = roll_x(sheets, k)
                for h in range(halves):
                    sums[h] = sums[h] - COEFFS[k] * (right[h] + roll_y(sheets[h], k))
            total = jnp.stack(sums).reshape(whole.shape)
            total = total + (potential_ref[z] + (omega_ref[0] - energies_ref[n])) * whole
            acc_ref[n] += jnp.sum(whole * total, axis=0)
            acc_ref[group + n] += jnp.sum(whole * applied_ref[n, z], axis=0)
            return carry

        lax.fori_loop(0, layers, layer, 0)
        for z in range(layers - 1):
            total = None
            for other in range(z + 1, min(layers, z + 7)):
                term = -COEFFS[other - z] * ahead_ref[n, other]
                total = term if total is None else total + term
            acc_ref[n] += jnp.sum(ahead_ref[n, z] * total, axis=0)


def pairs_kernel(shape, ahead_ref, after_ref, acc_ref, sums_ref):
    layers, group = shape
    sums = jnp.sum(acc_ref[...], axis=1)
    lines = []
    for n in range(group):
        total = None
        for z in range(layers):
            line = None
            for j in range(layers):
                k = j + layers - z
                if k <= 6:
                    term = -COEFFS[k] * after_ref[n, j]
                    line = term if line is None else line + term
            if line is not None:
                line = line * ahead_ref[n, z]
                total = line if total is None else total + line
        lines.append(jnp.sum(jnp.sum(total, axis=0), axis=0, keepdims=True))
    sums_ref[...] = rows_to_lanes(jnp.concatenate([sums[:group] + jnp.concatenate(lines, axis=0), sums[group:]], axis=0))


def density_kernel(shape, planes_ref, source_ref, residual_ref, numbers_ref, *refs):
    layers, group, parts, halves, members, width, margin = shape
    sums_refs = refs[:parts]
    cuts_ref, scales_ref, ring_ref = refs[parts:]
    first = lax.axis_index("orb")
    total = lanes_to_rows(add_all(sums_refs)[:1], 3 * group)
    norm, curve, alpha = (numbers_ref[i * group : (i + 1) * group, :] for i in range(3))
    squares, cross, bend = total[2 * group : 3 * group], total[group : 2 * group], total[:group]
    beta = squares / norm
    bend = bend + 2.0 * beta * cross + beta * beta * curve
    second = squares / bend
    scales_ref[:group, :] = alpha + second * beta
    scales_ref[group : 2 * group, :] = second

    def layer(z, carry):
        total = jnp.zeros(planes_ref.shape[2:], f32)
        for n in range(group):
            field = scales_ref[n : n + 1, :] * source_ref[n, z]
            field = field + scales_ref[group + n : group + n + 1, :] * residual_ref[n, z]
            total = total + field * planes_ref[first * group + n, z]
        total = blocks(4.0 * total)
        for h in range(halves):
            ring_ref[z, h, SUB : SUB + NY, :] = total[h]
            ring_ref[z, h, :SUB, :] = total[h, NY - SUB :]
            ring_ref[z, h, SUB + NY :, :] = total[h, :SUB]
        return carry

    lax.fori_loop(0, layers, layer, 0)
    for k in range(members):
        owner = lax.rem(first + k, members)
        for z in range(layers):
            for h in range(halves):
                rows = width + 2 * margin
                cuts_ref[k, pl.ds((z * halves + h) * rows, rows)] = ring_ref[
                    z, h, pl.ds(owner * width + SUB - margin, rows), :
                ]


def response_kernel(shape, source_ref, residual_ref, scales_ref, response_ref):
    layers, group, halves = shape
    tiles = NY * halves

    def layer(z, carry):
        for n in range(group):
            field = scales_ref[n : n + 1, :] * source_ref[n, z]
            field = field + scales_ref[group + n : group + n + 1, :] * residual_ref[n, z]
            for h in range(halves):
                for q in range(NY // SUB):
                    start = (z * tiles + q * SUB * halves + h) * group + n
                    response_ref[pl.ds(start, SUB, stride=group * halves), :] = field[h * (NY // SUB) + q]
        return carry

    lax.fori_loop(0, layers, layer, 0)


def gather_kernel(edge, cuts_ref, *refs):
    dense_ref, top_ref, bottom_ref = refs[-3:]
    total = cuts_ref[0]
    for ref in refs[:-3]:
        total = total + ref[...]
    dense_ref[...] = total
    top_ref[...] = total[-edge:]
    bottom_ref[...] = total[:edge]


def jacobi_kernel(shape, dense_ref, before_ref, after_ref, induced_ref):
    layers, halves, width, margin = shape
    rows = width + 2 * margin
    scale = 1.0 / (6.0 + SCREEN)

    def sheets(ref, count):
        return [[ref[pl.ds((z * halves + h) * rows, rows), :] for h in range(halves)] for z in range(count)]

    dense = sheets(before_ref, 2) + sheets(dense_ref, layers) + sheets(after_ref, 2)
    field = [[scale * v for v in sheet] for sheet in dense]

    def up(value):
        return pltpu.roll(value, 1, 0)

    def down(value):
        return pltpu.roll(value, rows - 1, 0)

    for sweep in range(2):
        fresh = []
        for z in range(1, len(field) - 1):
            right, left = roll_x(field[z], 1), roll_x(field[z], -1)
            sheet = []
            for h in range(halves):
                value = dense[z][h] + field[z - 1][h] + field[z + 1][h] + right[h] + left[h]
                value = value + up(field[z][h]) + down(field[z][h])
                sheet.append(scale * value)
            fresh.append(sheet)
        field, dense = fresh, dense[1:-1]
    for z in range(layers):
        for h in range(halves):
            for y in range(width):
                c = y * halves + h
                induced_ref[z : z + 1, c * LANES : (c + 1) * LANES] = field[z][h][margin + y : margin + y + 1]


def per_device(orbitals, potential, perturb, energies, omega):
    norb, layers, columns = orbitals.shape
    group = energies.shape[0]
    bricks, members = lax.axis_size("brick"), lax.axis_size("orb")
    ncell = layers * bricks * columns
    halves = columns // NY // LANES
    tiles = columns // LANES
    spots = tiles // SUB
    rows = orbitals.transpose(1, 0, 2).reshape(layers, norb // SUB, SUB, tiles, LANES)
    rows = rows.transpose(0, 1, 3, 2, 4).reshape(layers * norb * tiles, LANES)
    own = (group, layers, spots, SUB, LANES)
    flat = (group * norb, LANES)

    size = norb * tiles
    planes, gram = call(
        functools.partial(gram_kernel, (norb, layers, halves, group)),
        [(norb, layers, spots, SUB, LANES), (norb + SUB, norb)],
        [
            (layers * size, LANES),
            (layers, columns),
            pltpu.SemaphoreType.DMA((layers,)),
            pltpu.SemaphoreType.DMA,
        ],
        0,
        rows,
        perturb,
        far=2,
        limit=48 * 1024 * 1024,
    )
    grams = parts_of(gram, "brick")
    plane = (layers, spots, SUB, LANES)
    perturb_planes, potential_planes = call(
        functools.partial(tile_kernel, (layers, halves)), [plane, plane], [], 0, perturb, potential
    )
    share = 3 * spots // 8 if lax.axis_size("freq") == 2 else 0
    cells = (SUB, LANES)
    inner, rest, *shared = call(
        functools.partial(inner_kernel, (norb, layers, group, len(grams), share), ncell),
        [own, (group, layers, spots - 2 * share) + cells] + [(group, layers, share) + cells] * (share > 0),
        [flat, (SUB, norb)],
        0,
        planes,
        perturb_planes,
        *grams,
    )
    source, partial, overlap, along, square = call(
        functools.partial(local_kernel, (norb, layers, group, len(grams), halves), ncell),
        [own, own, (norb, norb, LANES), flat, (group, SUB, LANES)],
        [flat, (SUB, norb)],
        2,
        omega,
        energies,
        planes,
        perturb_planes,
        potential_planes,
        inner,
        *grams,
    )
    halos = []
    pieces = 1 if group % 2 else 2
    if share:
        before, after = shifted(shared[0], "brick", 1), shifted(shared[0], "brick", -1)
        halos = call(
            functools.partial(halo_kernel, (layers, group)),
            [(group // pieces, layers, share) + cells] * pieces,
            [],
            0,
            before,
            after,
            square,
        )
        halos = [*halos] + [lax.ppermute(halo, "freq", [(0, 1), (1, 0)]) for halo in halos]
    before, after = shifted(rest, "brick", 1), shifted(rest, "brick", -1)
    applied, sums = call(
        functools.partial(image_kernel, (norb, layers, group, share)),
        [own, cells],
        [(group * norb + group,) + cells],
        0,
        planes,
        inner,
        partial,
        square,
        before,
        after,
        *halos,
    )
    sums = parts_of(sums, "brick")
    ahead, plain, numbers = call(
        functools.partial(residual_kernel, (norb, layers, group, len(sums)), ncell),
        [own, flat, (3 * group, LANES)],
        [flat, (group, LANES)],
        0,
        planes,
        source,
        applied,
        overlap,
        along,
        *sums,
    )
    after = shifted(ahead, "brick", -1)
    residual, acc = call(
        functools.partial(second_kernel, (norb, layers, group, halves)),
        [own, (3 * group, SUB, LANES)],
        [],
        2,
        omega,
        energies,
        planes,
        potential_planes,
        source,
        applied,
        ahead,
        plain,
        numbers,
    )
    (sums,) = call(
        functools.partial(pairs_kernel, (layers, group)),
        [cells],
        [],
        0,
        ahead,
        after,
        acc,
    )
    sums = parts_of(sums, "brick")
    width = NY // members
    margin = 2
    edge = 2 * halves * (width + 2 * margin)
    cut = (layers * halves * (width + 2 * margin), LANES)
    cuts, scales = call(
        functools.partial(density_kernel, (layers, group, len(sums), halves, members, width, margin)),
        [(members,) + cut, (2 * group, LANES)],
        [(layers, halves, NY + 2 * SUB, LANES)],
        0,
        planes,
        source,
        residual,
        numbers,
        *sums,
    )
    others = [shifted(cuts[k], "orb", k) for k in range(1, members)]
    (response,) = call(
        functools.partial(response_kernel, (layers, group, halves)),
        [(layers * tiles * group, LANES)],
        [],
        0,
        source,
        residual,
        scales,
    )
    dense, top, bottom = call(
        functools.partial(gather_kernel, edge), [cut, (edge, LANES), (edge, LANES)], [], 0, cuts, *others
    )
    before, after = shifted(top, "brick", 1), shifted(bottom, "brick", -1)
    (induced,) = call(
        functools.partial(jacobi_kernel, (layers, halves, width, margin)),
        [(layers, width * halves * LANES)],
        [],
        0,
        dense,
        before,
        after,
    )
    response = response.reshape(layers, tiles, group, LANES).transpose(2, 0, 1, 3)
    return response.reshape(group, layers, columns), induced


def solution(mesh):
    placed = (P(None, "brick", None), P("brick", None), P("brick", None), P("orb"), P("freq"))
    return jax.shard_map(
        per_device,
        mesh=mesh,
        in_specs=placed,
        out_specs=(P(("freq", "orb"), "brick", None), P(("freq", "brick"), "orb")),
        check_vma=False,
    )
```

```python
import functools
import jax
import jax.numpy as jnp
from jax import lax
from jax.experimental import pallas as pl
from jax.experimental.pallas import tpu as pltpu
from jax.sharding import PartitionSpec as P

NY = 32
LANES = 128
SUB = 8

COEFFS = (
    -5369.0 / 1800.0,
    12.0 / 7.0,
    -15.0 / 56.0,
    10.0 / 189.0,
    -1.0 / 112.0,
    2.0 / 825.0,
    -1.0 / 5544.0,
)
SCREEN = 0.25
HIGHEST = lax.Precision.HIGHEST
VMEM_LIMIT = 16 * 1024 * 1024
SMEM = pl.BlockSpec(memory_space=pltpu.SMEM)
VMEM = pl.BlockSpec(memory_space=pltpu.VMEM)
HBM = pl.BlockSpec(memory_space=pltpu.HBM)
f32 = jnp.float32


def call(kernel, outs, scratch, smem, *args, far=0, limit=VMEM_LIMIT):
    return pl.pallas_call(
        kernel,
        out_shape=[jax.ShapeDtypeStruct(s, f32) for s in outs],
        in_specs=[SMEM] * smem + [HBM] * far + [VMEM] * (len(args) - smem - far),
        out_specs=[VMEM] * len(outs),
        scratch_shapes=[pltpu.VMEM(s, f32) if isinstance(s, tuple) else s for s in scratch],
        compiler_params=pltpu.CompilerParams(vmem_limit_bytes=limit),
    )(*args)


def copies(axis, rows, columns):
    size = lax.axis_size(axis)
    direct = size <= 4 and size & (size - 1) == 0
    return [(rows + SUB * k, columns) for k in range(size - 1 if direct else 1)]


def parts_of(arrays, axis):
    size = lax.axis_size(axis)
    if len(arrays) < size - 1:
        return [lax.psum(arrays[0], axis)]
    others = [
        lax.ppermute(array, axis, [(i, i ^ (k + 1)) for i in range(size)]) for k, array in enumerate(arrays)
    ]
    return [arrays[0]] + others


def put_copies(refs, value):
    rows = value.shape[0]
    for ref in refs:
        ref[:rows, :] = value
        if ref.shape[0] > rows:
            ref[rows:, :] = jnp.zeros((ref.shape[0] - rows, ref.shape[1]), f32)


def shifted(array, axis, step):
    size = lax.axis_size(axis)
    return lax.ppermute(array, axis, [(i, (i + step) % size) for i in range(size)])


def add_all(refs):
    total = refs[0][...]
    for ref in refs[1:]:
        total = total + ref[: total.shape[0], :]
    return total


def rows_to_lanes(matrix):
    count = matrix.shape[0]
    lane = lax.broadcasted_iota(jnp.int32, (count, LANES), 1)
    row = lax.broadcasted_iota(jnp.int32, (count, LANES), 0)
    value = jnp.broadcast_to(jnp.sum(matrix, axis=1, keepdims=True), (count, LANES))
    line = jnp.sum(jnp.where(lane == row, value, 0.0), axis=0, keepdims=True)
    return jnp.broadcast_to(line, (SUB, LANES))


def lanes_to_rows(line, count):
    wide = line.shape[1]
    lane = lax.broadcasted_iota(jnp.int32, (count, wide), 1)
    row = lax.broadcasted_iota(jnp.int32, (count, wide), 0)
    picked = jnp.where(lane == row, jnp.broadcast_to(line, (count, wide)), 0.0)
    return jnp.broadcast_to(jnp.sum(picked, axis=1, keepdims=True), (count, LANES))


def blocks(plane):
    return plane.reshape(-1, NY, LANES)


def gram_kernel(shape, far_rows_ref, far_perturb_ref, *refs):
    gram_refs, (rows_ref, perturb_ref, row_sems, perturb_sem) = refs[:-4], refs[-4:]
    norb, layers, halves, group = shape
    groups = norb // SUB
    tiles = NY * halves
    step = 16
    ahead = 3
    size = norb * tiles
    own = lax.axis_index("orb") * group // SUB

    def fetch(z):
        piece = pl.ds(z * size, size)
        return pltpu.make_async_copy(far_rows_ref.at[piece], rows_ref.at[piece], row_sems.at[z])

    weights = pltpu.make_async_copy(far_perturb_ref, perturb_ref, perturb_sem)
    fetch(0).start()
    weights.start()
    for z in range(1, min(ahead, layers)):
        fetch(z).start()
    weights.wait()

    def tile_row(z, t, c0):
        base = ((z * groups + t) * tiles + c0) * SUB
        return jnp.concatenate([rows_ref[pl.ds(base + c * SUB, SUB), :] for c in range(step)], axis=1)

    def rounded(value):
        return value.astype(jnp.bfloat16).astype(f32)

    def layer(z, total):
        fetch(z).wait()

        @pl.when(z + ahead < layers)
        def _():
            fetch(z + ahead).start()

        for c0 in range(0, tiles, step):
            field = jnp.concatenate([tile_row(z, t, c0) for t in range(groups)], axis=0)
            weighted = perturb_ref[pl.ds(z, 1), c0 * LANES : (c0 + step) * LANES] * tile_row(z, own, c0)
            rest = (field - rounded(field)).astype(jnp.bfloat16)
            field = field.astype(jnp.bfloat16)
            pair = jnp.concatenate([weighted, weighted - rounded(weighted)], axis=0).astype(jnp.bfloat16)
            left = jnp.concatenate([field, pair], axis=0)
            right = jnp.concatenate([field, rest], axis=0)
            total = total + lax.dot_general(
                left, right, (((1,), (1,)), ((), ())), preferred_element_type=f32
            )
        return total

    total = lax.fori_loop(0, layers, layer, jnp.zeros((norb + 2 * SUB, 2 * norb), f32))
    cross = total[:norb, norb:]
    overlap = total[:norb, :norb] + cross + cross.T
    total = total[norb:, :norb] + total[norb:, norb:]
    put_copies(gram_refs, jnp.concatenate([overlap, total[:SUB] + total[SUB:]], axis=0))


def tile_kernel(shape, rows_ref, perturb_ref, potential_ref, planes_ref, *refs):
    norb, layers, halves = shape
    tiles = NY * halves

    def layer(z, carry):
        for m in range(norb):
            base = (z * (norb // SUB) + m // SUB) * tiles * SUB + m % SUB
            for h in range(halves):
                for q in range(NY // SUB):
                    start = base + (q * SUB * halves + h) * SUB
                    planes_ref[m, z, h * (NY // SUB) + q] = rows_ref[pl.ds(start, SUB, stride=SUB * halves), :]
        return carry

    lax.fori_loop(0, layers, layer, 0)
    for array_ref, planes_ref in zip((perturb_ref, potential_ref), refs):
        for z in range(layers):
            for y in range(NY):
                for h in range(halves):
                    c = y * halves + h
                    planes_ref[z, h * (NY // SUB) + y // SUB, y % SUB : y % SUB + 1, :] = array_ref[
                        z : z + 1, c * LANES : (c + 1) * LANES
                    ]


def small_matrices(shape, ncell, gram_refs, lines_ref):
    norb, group = shape
    total = add_all(gram_refs)
    overlap = total[:norb]
    lines_ref[...] = total[norb:]
    start = lax.rem(lax.axis_index("orb") * group, SUB)
    rows = []
    for n in range(group):
        line = lines_ref[pl.ds(start + n, 1), :]
        again = jnp.sum(lanes_to_rows(line, norb)[:, :norb] * overlap, axis=0, keepdims=True)
        rows.append((line, again * (1.0 / ncell)))
    return overlap, rows


def whole(ref, n, z):
    return ref[n, z]


def combine(layers, group, norb, planes_ref, coef_ref, start, finish, pick=whole):
    def layer(z, carry):
        sums = [start(n, z) for n in range(group)]
        for m in range(norb):
            field = pick(planes_ref, m, z)
            for n in range(group):
                sums[n] = sums[n] + field * coef_ref[pl.ds(n * norb + m, 1), :]
        for n in range(group):
            finish(n, z, sums[n])
        return carry

    lax.fori_loop(0, layers, layer, 0)


def inner_kernel(shape, ncell, planes_ref, perturb_ref, *refs):
    norb, layers, group, parts, share = shape
    gram_refs = refs[:parts]
    shared_ref, rest_ref, coef_ref, lines_ref = refs[parts:]
    first = lax.axis_index("orb") * group
    overlap, rows = small_matrices((norb, group), ncell, gram_refs, lines_ref)
    for n, (line, again) in enumerate(rows):
        coefs = (2.0 * line - again) * (1.0 / ncell)
        coef_ref[n * norb : (n + 1) * norb, :] = lanes_to_rows(coefs, norb)
    mine = pl.ds(lax.axis_index("freq") * share, share)

    def pick(ref, n, z):
        return jnp.concatenate([ref[n, z, mine], ref[n, z, 2 * share :]], axis=0)

    def start(n, z):
        weight = jnp.concatenate([perturb_ref[z, mine], perturb_ref[z, 2 * share :]], axis=0)
        return -(weight * pick(planes_ref, first + n, z))

    def finish(n, z, value):
        shared_ref[n, z] = value[:share]
        rest_ref[n, z] = value[share:]

    combine(layers, group, norb, planes_ref, coef_ref, start, finish, pick)


def roll_x(halves_list, amount):
    count = len(halves_list)
    lane = lax.broadcasted_iota(jnp.int32, halves_list[0].shape, 1)
    turned = [pltpu.roll(v, amount % LANES, 1) for v in halves_list]
    if amount > 0:
        return [jnp.where(lane >= amount, turned[h], turned[(h - 1) % count]) for h in range(count)]
    return [
        jnp.where(lane < LANES + amount, turned[h], turned[(h + 1) % count]) for h in range(count)
    ]


def roll_y(value, amount):
    return pltpu.roll(value, amount % NY, 0)


def local_kernel(shape, ncell, omega_ref, energies_ref, planes_ref, perturb_ref, potential_ref, shared_ref, rest_ref, inner_coef_ref, *refs):
    norb, layers, group, parts, halves, share = shape
    gram_refs = refs[:parts]
    inner_ref, source_ref, partial_ref, overlap_ref, along_ref, square_ref, coef_ref, lines_ref = refs[parts:]
    first = lax.axis_index("orb") * group
    overlap, rows = small_matrices((norb, group), ncell, gram_refs, lines_ref)
    for m in range(norb):
        overlap_ref[m] = jnp.broadcast_to(overlap[:, m : m + 1], (norb, LANES))
    for n, (line, again) in enumerate(rows):
        place = slice(n * norb, (n + 1) * norb)
        coef_ref[place, :] = lanes_to_rows(line * (1.0 / ncell), norb)
        along_ref[place, :] = lanes_to_rows(again - line, norb)
    square_ref[...] = jnp.zeros_like(square_ref)

    def start(n, z):
        return -(perturb_ref[z] * planes_ref[first + n, z])

    def finish(n, z, value):
        source_ref[n, z] = value
        square_ref[n] += jnp.sum(value * value, axis=0)

    combine(layers, group, norb, planes_ref, coef_ref, start, finish)

    place = lax.axis_index("freq") * share
    mine, other = pl.ds(place, share), pl.ds(share - place, share)

    def start_other(n, z):
        return -(perturb_ref[z, other] * planes_ref[first + n, z, other])

    def finish_other(n, z, value):
        inner_ref[n, z, other] = value
        inner_ref[n, z, mine] = shared_ref[n, z]
        inner_ref[n, z, 2 * share :] = rest_ref[n, z]

    def pick_other(ref, n, z):
        return ref[n, z, other]

    combine(layers, group, norb, planes_ref, inner_coef_ref, start_other, finish_other, pick_other)

    for n in range(group):
        def layer(z, carry):
            plane = blocks(inner_ref[n, z])
            sheets = [plane[h] for h in range(halves)]
            sums = [(3.0 * COEFFS[0]) * v for v in sheets]
            for k in range(1, 7):
                right, left = roll_x(sheets, k), roll_x(sheets, -k)
                for h in range(halves):
                    around = right[h] + left[h] + roll_y(sheets[h], k) + roll_y(sheets[h], -k)
                    sums[h] = sums[h] + COEFFS[k] * around
            total = jnp.stack(sums).reshape(inner_ref.shape[2:])
            shift = potential_ref[z] + (omega_ref[0] - energies_ref[n])
            partial_ref[n, z] = shift * inner_ref[n, z] - 0.5 * total
            return carry

        lax.fori_loop(0, layers, layer, 0)
        for z in range(layers):
            total = None
            for other in range(layers):
                k = abs(other - z)
                if k == 0 or k > 6:
                    continue
                term = (-0.5 * COEFFS[k]) * inner_ref[n, other]
                total = term if total is None else total + term
            if total is not None:
                partial_ref[n, z] += total


def halo_sum(layers, n, z, before_ref, after_ref):
    total = None
    for j in range(layers):
        for k, ref in ((z + layers - j, before_ref), (j + layers - z, after_ref)):
            if k <= 6:
                term = (-0.5 * COEFFS[k]) * ref[n, j]
                total = term if total is None else total + term
    return total


def halo_kernel(shape, after_ref, before_ref, square_ref, *halo_refs):
    layers, group = shape
    each = group // len(halo_refs)
    for n in range(group):
        for z in range(layers):
            halo_refs[n // each][n % each, z] = halo_sum(layers, n, z, before_ref, after_ref)


def multiply(shape, spots, planes_ref, inner_ref, field_ref, acc_ref):
    norb, layers, group = shape
    acc_ref[...] = jnp.zeros_like(acc_ref)

    def layer(z, carry):
        fields = [field_ref[n, z] for n in range(group)]
        for n in range(group):
            acc_ref[group * norb + n] += jnp.sum(fields[n] * inner_ref[n, z, spots], axis=0)
        for m in range(norb):
            orbital = planes_ref[m, z, spots]
            for n in range(group):
                acc_ref[n * norb + m] += jnp.sum(orbital * fields[n], axis=0)
        return carry

    lax.fori_loop(0, layers, layer, 0)
    return jnp.sum(acc_ref[...], axis=1)


def mine_kernel(shape, share, planes_ref, inner_ref, partial_ref, *refs):
    norb, layers, group = shape
    field_ref, sums_ref, acc_ref = refs[-3:]
    each = group // (len(refs) - 3)
    spots = pl.ds(lax.axis_index("freq") * share, share)
    for n in range(group):
        for z in range(layers):
            field_ref[n, z] = partial_ref[n, z, spots] + refs[n // each][n % each, z]
    sums_ref[...] = multiply(shape, spots, planes_ref, inner_ref, field_ref, acc_ref)


def rest_kernel(shape, share, planes_ref, inner_ref, partial_ref, after_ref, before_ref, field_ref, sums_ref, acc_ref):
    norb, layers, group = shape
    spots = pl.ds(2 * share, field_ref.shape[2])
    for n in range(group):
        for z in range(layers):
            field_ref[n, z] = partial_ref[n, z, spots] + halo_sum(layers, n, z, before_ref, after_ref)
    sums_ref[...] = multiply(shape, spots, planes_ref, inner_ref, field_ref, acc_ref)


def other_kernel(shape, share, planes_ref, inner_ref, partial_ref, square_ref, mine_ref, mine_sums_ref, rest_ref, rest_sums_ref, *refs):
    norb, layers, group, pieces = shape
    halo_refs, applied_ref, sums_refs, (field_ref, acc_ref) = refs[:pieces], refs[pieces], refs[pieces + 1 : -2], refs[-2:]
    each = group // pieces
    place = lax.axis_index("freq") * share
    mine, spots = pl.ds(place, share), pl.ds(share - place, share)
    for n in range(group):
        for z in range(layers):
            field = partial_ref[n, z, spots] + halo_refs[n // each][n % each, z]
            field_ref[n, z] = field
            applied_ref[n, z, spots] = field
            applied_ref[n, z, mine] = mine_ref[n, z]
            applied_ref[n, z, 2 * share :] = rest_ref[n, z]
    sums = multiply(shape[:3], spots, planes_ref, inner_ref, field_ref, acc_ref)
    sums = sums + mine_sums_ref[...] + rest_sums_ref[...]
    sums = rows_to_lanes(jnp.concatenate([sums, jnp.sum(square_ref[...], axis=1)], axis=0))
    put_copies(sums_refs, sums)


def residual_kernel(shape, ncell, planes_ref, source_ref, applied_ref, overlap_ref, along_ref, *refs):
    norb, layers, group, parts, begin, count = shape
    sums_refs = refs[:parts]
    ahead_ref, plain_ref, numbers_ref, coef_ref = refs[parts:]
    size = group * norb
    total = lanes_to_rows(add_all(sums_refs)[:1], size + 2 * group)
    curve = total[size + begin : size + begin + count]
    norm = total[size + group + begin : size + group + begin + count]
    step = norm / curve
    numbers_ref[:count, :] = norm
    numbers_ref[count : 2 * count, :] = curve
    numbers_ref[2 * count : 3 * count, :] = step
    for i in range(count):
        n = begin + i
        rows = slice(i * norb, (i + 1) * norb)
        product = total[n * norb : (n + 1) * norb]
        alpha = step[i : i + 1]
        again = jnp.zeros((norb, LANES), f32)
        for m in range(norb):
            again = again + overlap_ref[m] * product[m : m + 1]
        left = along_ref[n * norb : (n + 1) * norb, :] - alpha * (product - again * (1.0 / ncell))
        plain_ref[rows, :] = alpha * product * (1.0 / ncell)
        coef_ref[rows, :] = (alpha * product - left) * (1.0 / ncell)

    def start(i, z):
        return source_ref[begin + i, z] - numbers_ref[2 * count + i : 2 * count + i + 1, :] * applied_ref[begin + i, z]

    def finish(i, z, value):
        ahead_ref[i, z] = value

    combine(layers, count, norb, planes_ref, coef_ref, start, finish)


def second_kernel(shape, omega_ref, energies_ref, planes_ref, potential_ref, source_ref, applied_ref, *refs):
    norb, layers, group, halves, parts = shape
    ahead_refs, plain_refs, numbers_refs = refs[:parts], refs[parts : 2 * parts], refs[2 * parts : 3 * parts]
    residual_ref, acc_ref = refs[3 * parts :]
    each = group // parts
    acc_ref[...] = jnp.zeros_like(acc_ref)

    for part in range(parts):
        first = part * each

        def start(i, z):
            alpha = numbers_refs[part][2 * each + i : 2 * each + i + 1, :]
            return source_ref[first + i, z] - alpha * applied_ref[first + i, z]

        def finish(i, z, value):
            residual_ref[first + i, z] = value
            acc_ref[2 * group + first + i] += jnp.sum(value * value, axis=0)

        combine(layers, each, norb, planes_ref, plain_refs[part], start, finish)

    for n in range(group):
        ahead_ref, i = ahead_refs[n // each], n % each

        def layer(z, carry):
            whole = ahead_ref[i, z]
            plane = blocks(whole)
            sheets = [plane[h] for h in range(halves)]
            sums = [(-1.5 * COEFFS[0]) * v for v in sheets]
            for k in range(1, 7):
                right = roll_x(sheets, k)
                for h in range(halves):
                    sums[h] = sums[h] - COEFFS[k] * (right[h] + roll_y(sheets[h], k))
            total = jnp.stack(sums).reshape(whole.shape)
            total = total + (potential_ref[z] + (omega_ref[0] - energies_ref[n])) * whole
            acc_ref[n] += jnp.sum(whole * total, axis=0)
            acc_ref[group + n] += jnp.sum(whole * applied_ref[n, z], axis=0)
            return carry

        lax.fori_loop(0, layers, layer, 0)
        for z in range(layers - 1):
            total = None
            for other in range(z + 1, min(layers, z + 7)):
                term = -COEFFS[other - z] * ahead_ref[i, other]
                total = term if total is None else total + term
            acc_ref[n] += jnp.sum(ahead_ref[i, z] * total, axis=0)


def pairs_kernel(shape, acc_ref, *refs):
    layers, group, parts = shape
    ahead_refs, after_refs, sums_refs = refs[:parts], refs[parts : 2 * parts], refs[2 * parts :]
    each = group // parts
    sums = jnp.sum(acc_ref[...], axis=1)
    lines = []
    for n in range(group):
        ahead_ref, after_ref, i = ahead_refs[n // each], after_refs[n // each], n % each
        total = None
        for z in range(layers):
            line = None
            for j in range(layers):
                k = j + layers - z
                if k <= 6:
                    term = -COEFFS[k] * after_ref[i, j]
                    line = term if line is None else line + term
            if line is not None:
                line = line * ahead_ref[i, z]
                total = line if total is None else total + line
        lines.append(jnp.sum(jnp.sum(total, axis=0), axis=0, keepdims=True))
    sums = jnp.concatenate([sums[:group] + jnp.concatenate(lines, axis=0), sums[group:]], axis=0)
    put_copies(sums_refs, rows_to_lanes(sums))


def density_kernel(shape, planes_ref, source_ref, residual_ref, *refs):
    layers, group, parts, halves, members, width, margin, cut = shape
    sums_refs, numbers_refs, refs = refs[:parts], refs[parts : parts + cut], refs[parts + cut :]
    cuts_ref, scales_ref, ring_ref = refs
    each = group // cut
    first = lax.axis_index("orb")
    total = lanes_to_rows(add_all(sums_refs)[:1], 3 * group)
    norm, curve, alpha = (
        jnp.concatenate([ref[i * each : (i + 1) * each, :] for ref in numbers_refs], axis=0) for i in range(3)
    )
    squares, cross, bend = total[2 * group : 3 * group], total[group : 2 * group], total[:group]
    beta = squares / norm
    bend = bend + 2.0 * beta * cross + beta * beta * curve
    second = squares / bend
    scales_ref[:group, :] = alpha + second * beta
    scales_ref[group : 2 * group, :] = second

    def layer(z, carry):
        total = jnp.zeros(planes_ref.shape[2:], f32)
        for n in range(group):
            field = scales_ref[n : n + 1, :] * source_ref[n, z]
            field = field + scales_ref[group + n : group + n + 1, :] * residual_ref[n, z]
            total = total + field * planes_ref[first * group + n, z]
        total = blocks(4.0 * total)
        for h in range(halves):
            ring_ref[z, h, SUB : SUB + NY, :] = total[h]
            ring_ref[z, h, :SUB, :] = total[h, NY - SUB :]
            ring_ref[z, h, SUB + NY :, :] = total[h, :SUB]
        return carry

    lax.fori_loop(0, layers, layer, 0)
    for k in range(members):
        owner = lax.rem(first + k, members)
        for z in range(layers):
            for h in range(halves):
                rows = width + 2 * margin
                cuts_ref[k, pl.ds((z * halves + h) * rows, rows)] = ring_ref[
                    z, h, pl.ds(owner * width + SUB - margin, rows), :
                ]


def response_kernel(shape, source_ref, residual_ref, scales_ref, response_ref):
    layers, group, halves = shape
    tiles = NY * halves

    def layer(z, carry):
        for n in range(group):
            field = scales_ref[n : n + 1, :] * source_ref[n, z]
            field = field + scales_ref[group + n : group + n + 1, :] * residual_ref[n, z]
            for h in range(halves):
                for q in range(NY // SUB):
                    start = (z * tiles + q * SUB * halves + h) * group + n
                    response_ref[pl.ds(start, SUB, stride=group * halves), :] = field[h * (NY // SUB) + q]
        return carry

    lax.fori_loop(0, layers, layer, 0)


def gather_kernel(edge, cuts_ref, *refs):
    dense_ref, top_ref, bottom_ref = refs[-3:]
    total = cuts_ref[0]
    for ref in refs[:-3]:
        total = total + ref[...]
    dense_ref[...] = total
    top_ref[...] = total[-edge:]
    bottom_ref[...] = total[:edge]


def jacobi_kernel(shape, dense_ref, before_ref, after_ref, induced_ref, slab_ref, out_ref):
    layers, halves, width, margin = shape
    rows = width + 2 * margin
    full = -(-rows // SUB) * SUB
    scale = 1.0 / (6.0 + SCREEN)
    edge = 2 * halves * rows
    middle = layers * halves * rows
    slab_ref[:edge, :] = before_ref[...]
    slab_ref[edge : edge + middle, :] = dense_ref[...]
    slab_ref[edge + middle : 2 * edge + middle, :] = after_ref[...]
    slab_ref[2 * edge + middle :, :] = jnp.zeros((slab_ref.shape[0] - 2 * edge - middle, LANES), f32)
    dense = [
        [slab_ref[(z * halves + h) * rows : (z * halves + h) * rows + full, :] for h in range(halves)]
        for z in range(layers + 4)
    ]
    field = [[scale * v for v in sheet] for sheet in dense]

    def up(value):
        return pltpu.roll(value, 1, 0)

    def down(value):
        return pltpu.roll(value, full - 1, 0)

    for sweep in range(2):
        fresh = []
        for z in range(1, len(field) - 1):
            right, left = roll_x(field[z], 1), roll_x(field[z], -1)
            sheet = []
            for h in range(halves):
                value = dense[z][h] + field[z - 1][h] + field[z + 1][h] + right[h] + left[h]
                value = value + up(field[z][h]) + down(field[z][h])
                sheet.append(scale * value)
            fresh.append(sheet)
        field, dense = fresh, dense[1:-1]
    for z in range(layers):
        for h in range(halves):
            out_ref[pl.ds((z * halves + h) * full, full), :] = field[z][h]
    for h in range(halves):
        for y in range(width):
            c = y * halves + h
            induced_ref[:, c * LANES : (c + 1) * LANES] = out_ref[
                pl.ds(h * full + margin + y, layers, stride=halves * full), :
            ]


def per_device(orbitals, potential, perturb, energies, omega):
    norb, layers, columns = orbitals.shape
    group = energies.shape[0]
    bricks, members = lax.axis_size("brick"), lax.axis_size("orb")
    ncell = layers * bricks * columns
    halves = columns // NY // LANES
    tiles = columns // LANES
    spots = tiles // SUB
    rows = orbitals.transpose(1, 0, 2).reshape(layers, norb // SUB, SUB, tiles, LANES)
    rows = rows.transpose(0, 1, 3, 2, 4).reshape(layers * norb * tiles, LANES)
    own = (group, layers, spots, SUB, LANES)
    flat = (group * norb, LANES)

    size = norb * tiles
    gram = call(
        functools.partial(gram_kernel, (norb, layers, halves, group)),
        copies("brick", norb + SUB, norb),
        [
            (layers * size, LANES),
            (layers, columns),
            pltpu.SemaphoreType.DMA((layers,)),
            pltpu.SemaphoreType.DMA,
        ],
        0,
        rows,
        perturb,
        far=2,
        limit=60 * 1024 * 1024,
    )
    grams = parts_of(gram, "brick")
    plane = (layers, spots, SUB, LANES)
    planes, perturb_planes, potential_planes = call(
        functools.partial(tile_kernel, (norb, layers, halves)),
        [(norb,) + plane, plane, plane],
        [],
        0,
        rows,
        perturb,
        potential,
    )
    share = 3 * spots // 8
    cells = (SUB, LANES)
    shared, rest, coefs = call(
        functools.partial(inner_kernel, (norb, layers, group, len(grams), share), ncell),
        [(group, layers, share) + cells, (group, layers, spots - 2 * share) + cells, flat],
        [(SUB, norb)],
        0,
        planes,
        perturb_planes,
        *grams,
    )
    inner, source, partial, overlap, along, square = call(
        functools.partial(local_kernel, (norb, layers, group, len(grams), halves, share), ncell),
        [own, own, own, (norb, norb, LANES), flat, (group,) + cells],
        [flat, (SUB, norb)],
        2,
        omega,
        energies,
        planes,
        perturb_planes,
        potential_planes,
        shared,
        rest,
        coefs,
        *grams,
    )
    before, after = shifted(shared, "brick", 1), shifted(shared, "brick", -1)
    pieces = 1 if group % 2 else 2
    each = group // pieces
    halos = call(
        functools.partial(halo_kernel, (layers, group)),
        [(each, layers, share) + cells] * pieces,
        [],
        0,
        after,
        before,
        square,
    )
    partner = [lax.ppermute(halo, "freq", [(0, 1), (1, 0)]) for halo in halos]
    count = group * norb + group
    before_rest, after_rest = shifted(rest, "brick", 1), shifted(rest, "brick", -1)
    mine, mine_sums = call(
        functools.partial(mine_kernel, (norb, layers, group), share),
        [shared.shape, (count, LANES)],
        [(count,) + cells],
        0,
        planes,
        inner,
        partial,
        *halos,
    )
    rest, rest_sums = call(
        functools.partial(rest_kernel, (norb, layers, group), share),
        [rest.shape, (count, LANES)],
        [(count,) + cells],
        0,
        planes,
        inner,
        partial,
        after_rest,
        before_rest,
    )
    applied, *sums = call(
        functools.partial(other_kernel, (norb, layers, group, pieces), share),
        [own] + copies("brick", SUB, LANES),
        [shared.shape, (count,) + cells],
        0,
        planes,
        inner,
        partial,
        square,
        mine,
        mine_sums,
        rest,
        rest_sums,
        *partner,
    )
    sums = parts_of(sums, "brick")
    runs = 1
    part = group // runs
    steps = [
        call(
            functools.partial(residual_kernel, (norb, layers, group, len(sums), i * part, part), ncell),
            [(part,) + own[1:], (part * norb, LANES), (3 * part, LANES)],
            [(part * norb, LANES)],
            0,
            planes,
            source,
            applied,
            overlap,
            along,
            *sums,
        )
        for i in range(runs)
    ]
    aheads, plains, numbers = zip(*steps)
    afters = [shifted(ahead, "brick", -1) for ahead in aheads]
    residual, acc = call(
        functools.partial(second_kernel, (norb, layers, group, halves, runs)),
        [own, (3 * group,) + cells],
        [],
        2,
        omega,
        energies,
        planes,
        potential_planes,
        source,
        applied,
        *aheads,
        *plains,
        *numbers,
    )
    sums = call(
        functools.partial(pairs_kernel, (layers, group, runs)),
        copies("brick", SUB, LANES),
        [],
        0,
        acc,
        *aheads,
        *afters,
    )
    sums = parts_of(sums, "brick")
    width = NY // members
    margin = 2
    span = width + 2 * margin
    edge = 2 * halves * span
    cut = (layers * halves * span, LANES)
    cuts, scales = call(
        functools.partial(density_kernel, (layers, group, len(sums), halves, members, width, margin, runs)),
        [(members,) + cut, (2 * group, LANES)],
        [(layers, halves, NY + 2 * SUB, LANES)],
        0,
        planes,
        source,
        residual,
        *sums,
        *numbers,
    )
    others = [shifted(cuts[k], "orb", k) for k in range(1, members)]
    (response,) = call(
        functools.partial(response_kernel, (layers, group, halves)),
        [(layers * tiles * group, LANES)],
        [],
        0,
        source,
        residual,
        scales,
    )
    dense, top, bottom = call(
        functools.partial(gather_kernel, edge), [cut, (edge, LANES), (edge, LANES)], [], 0, cuts, *others
    )
    before, after = shifted(top, "brick", 1), shifted(bottom, "brick", -1)
    (induced,) = call(
        functools.partial(jacobi_kernel, (layers, halves, width, margin)),
        [(layers, width * halves * LANES)],
        [((layers + 4) * halves * span + SUB, LANES), (layers * halves * (-(-span // SUB) * SUB), LANES)],
        0,
        dense,
        before,
        after,
    )
    response = response.reshape(layers, tiles, group, LANES).transpose(2, 0, 1, 3)
    return response.reshape(group, layers, columns), induced


def solution(mesh):
    placed = (P(None, "brick", None), P("brick", None), P("brick", None), P("orb"), P("freq"))
    return jax.shard_map(
        per_device,
        mesh=mesh,
        in_specs=placed,
        out_specs=(P(("freq", "orb"), "brick", None), P(("freq", "brick"), "orb")),
        check_vma=False,
    )
```

```python
import functools
import jax
import jax.numpy as jnp
from jax import lax
from jax.experimental import pallas as pl
from jax.experimental.pallas import tpu as pltpu
from jax.sharding import PartitionSpec as P

NY = 32
LANES = 128
SUB = 8

COEFFS = (
    -5369.0 / 1800.0,
    12.0 / 7.0,
    -15.0 / 56.0,
    10.0 / 189.0,
    -1.0 / 112.0,
    2.0 / 825.0,
    -1.0 / 5544.0,
)
SCREEN = 0.25
HIGHEST = lax.Precision.HIGHEST
VMEM_LIMIT = 16 * 1024 * 1024
SMEM = pl.BlockSpec(memory_space=pltpu.SMEM)
VMEM = pl.BlockSpec(memory_space=pltpu.VMEM)
HBM = pl.BlockSpec(memory_space=pltpu.HBM)
f32 = jnp.float32


def call(kernel, outs, scratch, smem, *args, far=0, limit=VMEM_LIMIT):
    return pl.pallas_call(
        kernel,
        out_shape=[jax.ShapeDtypeStruct(s, f32) for s in outs],
        in_specs=[SMEM] * smem + [HBM] * far + [VMEM] * (len(args) - smem - far),
        out_specs=[VMEM] * len(outs),
        scratch_shapes=[pltpu.VMEM(s, f32) if isinstance(s, tuple) else s for s in scratch],
        compiler_params=pltpu.CompilerParams(vmem_limit_bytes=limit),
    )(*args)


def copies(axis, rows, columns):
    size = lax.axis_size(axis)
    direct = size <= 4 and size & (size - 1) == 0
    return [(rows, columns) for k in range(size - 1 if direct else 1)]


def parts_of(arrays, axis):
    size = lax.axis_size(axis)
    if len(arrays) < size - 1:
        return [lax.psum(arrays[0], axis)]
    others = [
        lax.ppermute(array, axis, [(i, i ^ (k + 1)) for i in range(size)]) for k, array in enumerate(arrays)
    ]
    return [arrays[0]] + others


def put_copies(refs, value):
    rows = value.shape[0]
    for ref in refs:
        ref[:rows, :] = value
        if ref.shape[0] > rows:
            ref[rows:, :] = jnp.zeros((ref.shape[0] - rows, ref.shape[1]), f32)


def shifted(array, axis, step):
    size = lax.axis_size(axis)
    return lax.ppermute(array, axis, [(i, (i + step) % size) for i in range(size)])


def add_all(refs):
    total = refs[0][...]
    for ref in refs[1:]:
        total = total + ref[: total.shape[0], :]
    return total


def rows_to_lanes(matrix):
    count = matrix.shape[0]
    lane = lax.broadcasted_iota(jnp.int32, (count, LANES), 1)
    row = lax.broadcasted_iota(jnp.int32, (count, LANES), 0)
    value = jnp.broadcast_to(jnp.sum(matrix, axis=1, keepdims=True), (count, LANES))
    line = jnp.sum(jnp.where(lane == row, value, 0.0), axis=0, keepdims=True)
    return jnp.broadcast_to(line, (SUB, LANES))


def lanes_to_rows(line, count):
    wide = line.shape[1]
    lane = lax.broadcasted_iota(jnp.int32, (count, wide), 1)
    row = lax.broadcasted_iota(jnp.int32, (count, wide), 0)
    picked = jnp.where(lane == row, jnp.broadcast_to(line, (count, wide)), 0.0)
    return jnp.broadcast_to(jnp.sum(picked, axis=1, keepdims=True), (count, LANES))


def blocks(plane):
    return plane.reshape(-1, NY, LANES)


def gram_kernel(shape, far_rows_ref, far_perturb_ref, *refs):
    gram_refs, (rows_ref, perturb_ref, row_sems, perturb_sem) = refs[:-4], refs[-4:]
    norb, layers, halves, group = shape
    groups = norb // SUB
    tiles = NY * halves
    step = 16
    ahead = 3
    size = norb * tiles
    own = lax.axis_index("orb") * group // SUB

    def fetch(z):
        piece = pl.ds(z * size, size)
        return pltpu.make_async_copy(far_rows_ref.at[piece], rows_ref.at[piece], row_sems.at[z])

    weights = pltpu.make_async_copy(far_perturb_ref, perturb_ref, perturb_sem)
    fetch(0).start()
    weights.start()
    for z in range(1, min(ahead, layers)):
        fetch(z).start()
    weights.wait()

    def tile_row(z, t, c0):
        base = ((z * groups + t) * tiles + c0) * SUB
        return jnp.concatenate([rows_ref[pl.ds(base + c * SUB, SUB), :] for c in range(step)], axis=1)

    def rounded(value):
        return value.astype(jnp.bfloat16).astype(f32)

    def layer(z, total):
        fetch(z).wait()

        @pl.when(z + ahead < layers)
        def _():
            fetch(z + ahead).start()

        for c0 in range(0, tiles, step):
            field = jnp.concatenate([tile_row(z, t, c0) for t in range(groups)], axis=0)
            weighted = perturb_ref[pl.ds(z, 1), c0 * LANES : (c0 + step) * LANES] * tile_row(z, own, c0)
            rest = (field - rounded(field)).astype(jnp.bfloat16)
            field = field.astype(jnp.bfloat16)
            pair = jnp.concatenate([weighted, weighted - rounded(weighted)], axis=0).astype(jnp.bfloat16)
            left = jnp.concatenate([field, pair], axis=0)
            right = jnp.concatenate([field, rest], axis=0)
            total = total + lax.dot_general(
                left, right, (((1,), (1,)), ((), ())), preferred_element_type=f32
            )
        return total

    total = lax.fori_loop(0, layers, layer, jnp.zeros((norb + 2 * SUB, 2 * norb), f32))
    cross = total[:norb, norb:]
    overlap = total[:norb, :norb] + cross + cross.T
    total = total[norb:, :norb] + total[norb:, norb:]
    put_copies(gram_refs, jnp.concatenate([overlap, total[:SUB] + total[SUB:]], axis=0))


def tile_kernel(shape, rows_ref, perturb_ref, potential_ref, planes_ref, *refs):
    norb, layers, halves = shape
    tiles = NY * halves

    def layer(z, carry):
        for m in range(norb):
            base = (z * (norb // SUB) + m // SUB) * tiles * SUB + m % SUB
            for h in range(halves):
                for q in range(NY // SUB):
                    start = base + (q * SUB * halves + h) * SUB
                    planes_ref[m, z, h * (NY // SUB) + q] = rows_ref[pl.ds(start, SUB, stride=SUB * halves), :]
        return carry

    lax.fori_loop(0, layers, layer, 0)
    for array_ref, planes_ref in zip((perturb_ref, potential_ref), refs):
        for z in range(layers):
            for y in range(NY):
                for h in range(halves):
                    c = y * halves + h
                    planes_ref[z, h * (NY // SUB) + y // SUB, y % SUB : y % SUB + 1, :] = array_ref[
                        z : z + 1, c * LANES : (c + 1) * LANES
                    ]


def small_matrices(shape, ncell, gram_refs, lines_ref):
    norb, group = shape
    total = add_all(gram_refs)
    overlap = total[:norb]
    lines_ref[...] = total[norb:]
    start = lax.rem(lax.axis_index("orb") * group, SUB)
    rows = []
    for n in range(group):
        line = lines_ref[pl.ds(start + n, 1), :]
        again = jnp.sum(lanes_to_rows(line, norb)[:, :norb] * overlap, axis=0, keepdims=True)
        rows.append((line, again * (1.0 / ncell)))
    return overlap, rows


def whole(ref, n, z):
    return ref[n, z]


def combine(layers, group, norb, planes_ref, coef_ref, start, finish, pick=whole):
    def layer(z, carry):
        sums = [start(n, z) for n in range(group)]
        for m in range(norb):
            field = pick(planes_ref, m, z)
            for n in range(group):
                sums[n] = sums[n] + field * coef_ref[pl.ds(n * norb + m, 1), :]
        for n in range(group):
            finish(n, z, sums[n])
        return carry

    lax.fori_loop(0, layers, layer, 0)


def inner_kernel(shape, ncell, planes_ref, perturb_ref, *refs):
    norb, layers, group, parts, share = shape
    gram_refs = refs[:parts]
    shared_ref, rest_ref, coef_ref, lines_ref = refs[parts:]
    first = lax.axis_index("orb") * group
    overlap, rows = small_matrices((norb, group), ncell, gram_refs, lines_ref)
    for n, (line, again) in enumerate(rows):
        coefs = (2.0 * line - again) * (1.0 / ncell)
        coef_ref[n * norb : (n + 1) * norb, :] = lanes_to_rows(coefs, norb)
    mine = pl.ds(lax.axis_index("freq") * share, share)

    def pick(ref, n, z):
        return jnp.concatenate([ref[n, z, mine], ref[n, z, 2 * share :]], axis=0)

    def start(n, z):
        weight = jnp.concatenate([perturb_ref[z, mine], perturb_ref[z, 2 * share :]], axis=0)
        return -(weight * pick(planes_ref, first + n, z))

    def finish(n, z, value):
        shared_ref[n, z] = value[:share]
        rest_ref[n, z] = value[share:]

    combine(layers, group, norb, planes_ref, coef_ref, start, finish, pick)


def roll_x(halves_list, amount):
    count = len(halves_list)
    lane = lax.broadcasted_iota(jnp.int32, halves_list[0].shape, 1)
    turned = [pltpu.roll(v, amount % LANES, 1) for v in halves_list]
    if amount > 0:
        return [jnp.where(lane >= amount, turned[h], turned[(h - 1) % count]) for h in range(count)]
    return [
        jnp.where(lane < LANES + amount, turned[h], turned[(h + 1) % count]) for h in range(count)
    ]


def roll_y(value, amount):
    return pltpu.roll(value, amount % NY, 0)


def local_kernel(shape, ncell, omega_ref, energies_ref, planes_ref, perturb_ref, potential_ref, shared_ref, rest_ref, inner_coef_ref, *refs):
    norb, layers, group, parts, halves, share = shape
    gram_refs = refs[:parts]
    inner_ref, source_ref, partial_ref, overlap_ref, along_ref, square_ref, coef_ref, lines_ref = refs[parts:]
    first = lax.axis_index("orb") * group
    overlap, rows = small_matrices((norb, group), ncell, gram_refs, lines_ref)
    for m in range(norb):
        overlap_ref[m] = jnp.broadcast_to(overlap[:, m : m + 1], (norb, LANES))
    for n, (line, again) in enumerate(rows):
        place = slice(n * norb, (n + 1) * norb)
        coef_ref[place, :] = lanes_to_rows(line * (1.0 / ncell), norb)
        along_ref[place, :] = lanes_to_rows(again - line, norb)
    square_ref[...] = jnp.zeros_like(square_ref)

    def start(n, z):
        return -(perturb_ref[z] * planes_ref[first + n, z])

    def finish(n, z, value):
        source_ref[n, z] = value
        square_ref[n] += jnp.sum(value * value, axis=0)

    combine(layers, group, norb, planes_ref, coef_ref, start, finish)

    place = lax.axis_index("freq") * share
    mine, other = pl.ds(place, share), pl.ds(share - place, share)

    def start_other(n, z):
        return -(perturb_ref[z, other] * planes_ref[first + n, z, other])

    def finish_other(n, z, value):
        inner_ref[n, z, other] = value
        inner_ref[n, z, mine] = shared_ref[n, z]
        inner_ref[n, z, 2 * share :] = rest_ref[n, z]

    def pick_other(ref, n, z):
        return ref[n, z, other]

    combine(layers, group, norb, planes_ref, inner_coef_ref, start_other, finish_other, pick_other)

    for n in range(group):
        def layer(z, carry):
            plane = blocks(inner_ref[n, z])
            sheets = [plane[h] for h in range(halves)]
            sums = [(3.0 * COEFFS[0]) * v for v in sheets]
            for k in range(1, 7):
                right, left = roll_x(sheets, k), roll_x(sheets, -k)
                for h in range(halves):
                    around = right[h] + left[h] + roll_y(sheets[h], k) + roll_y(sheets[h], -k)
                    sums[h] = sums[h] + COEFFS[k] * around
            total = jnp.stack(sums).reshape(inner_ref.shape[2:])
            shift = potential_ref[z] + (omega_ref[0] - energies_ref[n])
            partial_ref[n, z] = shift * inner_ref[n, z] - 0.5 * total
            return carry

        lax.fori_loop(0, layers, layer, 0)
        for z in range(layers):
            total = None
            for other in range(layers):
                k = abs(other - z)
                if k == 0 or k > 6:
                    continue
                term = (-0.5 * COEFFS[k]) * inner_ref[n, other]
                total = term if total is None else total + term
            if total is not None:
                partial_ref[n, z] += total


def halo_sum(layers, n, z, before_ref, after_ref):
    total = None
    for j in range(layers):
        for k, ref in ((z + layers - j, before_ref), (j + layers - z, after_ref)):
            if k <= 6:
                term = (-0.5 * COEFFS[k]) * ref[n, j]
                total = term if total is None else total + term
    return total


def halo_kernel(shape, before_ref, after_ref, square_ref, *halo_refs):
    layers, group = shape
    each = group // len(halo_refs)
    for n in range(group):
        for z in range(layers):
            halo_refs[n // each][n % each, z] = halo_sum(layers, n, z, before_ref, after_ref)


def multiply(shape, spots, planes_ref, inner_ref, field_ref, acc_ref):
    norb, layers, group = shape
    acc_ref[...] = jnp.zeros_like(acc_ref)

    def layer(z, carry):
        fields = [field_ref[n, z] for n in range(group)]
        for n in range(group):
            acc_ref[group * norb + n] += jnp.sum(fields[n] * inner_ref[n, z, spots], axis=0)
        for m in range(norb):
            orbital = planes_ref[m, z, spots]
            for n in range(group):
                acc_ref[n * norb + m] += jnp.sum(orbital * fields[n], axis=0)
        return carry

    lax.fori_loop(0, layers, layer, 0)
    return jnp.sum(acc_ref[...], axis=1)


def mine_kernel(shape, share, planes_ref, inner_ref, partial_ref, *refs):
    norb, layers, group = shape
    field_ref, sums_ref, acc_ref = refs[-3:]
    each = group // (len(refs) - 3)
    spots = pl.ds(lax.axis_index("freq") * share, share)
    for n in range(group):
        for z in range(layers):
            field_ref[n, z] = partial_ref[n, z, spots] + refs[n // each][n % each, z]
    sums_ref[...] = multiply(shape, spots, planes_ref, inner_ref, field_ref, acc_ref)


def other_kernel(shape, share, planes_ref, inner_ref, partial_ref, earlier_ref, *refs):
    norb, layers, group = shape
    field_ref, sums_ref, acc_ref = refs[-3:]
    each = group // (len(refs) - 3)
    spots = pl.ds(share - lax.axis_index("freq") * share, share)
    for n in range(group):
        for z in range(layers):
            field_ref[n, z] = partial_ref[n, z, spots] + refs[n // each][n % each, z]
    sums = multiply(shape, spots, planes_ref, inner_ref, field_ref, acc_ref)
    sums_ref[...] = sums + earlier_ref[...]


def rest_kernel(shape, share, planes_ref, inner_ref, partial_ref, square_ref, mine_ref, other_ref, earlier_ref, after_ref, before_ref, *refs):
    norb, layers, group = shape
    applied_ref, sums_refs, (field_ref, acc_ref) = refs[0], refs[1:-2], refs[-2:]
    place = lax.axis_index("freq") * share
    mine, other = pl.ds(place, share), pl.ds(share - place, share)
    spots = pl.ds(2 * share, field_ref.shape[2])
    for n in range(group):
        for z in range(layers):
            field = partial_ref[n, z, spots] + halo_sum(layers, n, z, before_ref, after_ref)
            field_ref[n, z] = field
            applied_ref[n, z, 2 * share :] = field
            applied_ref[n, z, mine] = mine_ref[n, z]
            applied_ref[n, z, other] = other_ref[n, z]
    sums = multiply(shape, spots, planes_ref, inner_ref, field_ref, acc_ref) + earlier_ref[...]
    sums = rows_to_lanes(jnp.concatenate([sums, jnp.sum(square_ref[...], axis=1)], axis=0))
    put_copies(sums_refs, sums)


def residual_kernel(shape, ncell, planes_ref, source_ref, applied_ref, overlap_ref, along_ref, *refs):
    norb, layers, group, parts, begin, count = shape
    sums_refs = refs[:parts]
    ahead_ref, plain_ref, numbers_ref, coef_ref = refs[parts:]
    size = group * norb
    total = lanes_to_rows(add_all(sums_refs)[:1], size + 2 * group)
    curve = total[size + begin : size + begin + count]
    norm = total[size + group + begin : size + group + begin + count]
    step = norm / curve
    numbers_ref[:count, :] = norm
    numbers_ref[count : 2 * count, :] = curve
    numbers_ref[2 * count : 3 * count, :] = step
    for i in range(count):
        n = begin + i
        rows = slice(i * norb, (i + 1) * norb)
        product = total[n * norb : (n + 1) * norb]
        alpha = step[i : i + 1]
        again = jnp.zeros((norb, LANES), f32)
        for m in range(norb):
            again = again + overlap_ref[m] * product[m : m + 1]
        left = along_ref[n * norb : (n + 1) * norb, :] - alpha * (product - again * (1.0 / ncell))
        plain_ref[rows, :] = alpha * product * (1.0 / ncell)
        coef_ref[rows, :] = (alpha * product - left) * (1.0 / ncell)

    def start(i, z):
        return source_ref[begin + i, z] - numbers_ref[2 * count + i : 2 * count + i + 1, :] * applied_ref[begin + i, z]

    def finish(i, z, value):
        ahead_ref[i, z] = value

    combine(layers, count, norb, planes_ref, coef_ref, start, finish)


def second_kernel(shape, omega_ref, energies_ref, planes_ref, potential_ref, source_ref, applied_ref, *refs):
    norb, layers, group, halves, parts = shape
    ahead_refs, plain_refs, numbers_refs = refs[:parts], refs[parts : 2 * parts], refs[2 * parts : 3 * parts]
    residual_ref, acc_ref = refs[3 * parts :]
    each = group // parts
    acc_ref[...] = jnp.zeros_like(acc_ref)

    for part in range(parts):
        first = part * each

        def start(i, z):
            alpha = numbers_refs[part][2 * each + i : 2 * each + i + 1, :]
            return source_ref[first + i, z] - alpha * applied_ref[first + i, z]

        def finish(i, z, value):
            residual_ref[first + i, z] = value
            acc_ref[2 * group + first + i] += jnp.sum(value * value, axis=0)

        combine(layers, each, norb, planes_ref, plain_refs[part], start, finish)

    for n in range(group):
        ahead_ref, i = ahead_refs[n // each], n % each

        def layer(z, carry):
            whole = ahead_ref[i, z]
            plane = blocks(whole)
            sheets = [plane[h] for h in range(halves)]
            sums = [(-1.5 * COEFFS[0]) * v for v in sheets]
            for k in range(1, 7):
                right = roll_x(sheets, k)
                for h in range(halves):
                    sums[h] = sums[h] - COEFFS[k] * (right[h] + roll_y(sheets[h], k))
            total = jnp.stack(sums).reshape(whole.shape)
            total = total + (potential_ref[z] + (omega_ref[0] - energies_ref[n])) * whole
            acc_ref[n] += jnp.sum(whole * total, axis=0)
            acc_ref[group + n] += jnp.sum(whole * applied_ref[n, z], axis=0)
            return carry

        lax.fori_loop(0, layers, layer, 0)
        for z in range(layers - 1):
            total = None
            for other in range(z + 1, min(layers, z + 7)):
                term = -COEFFS[other - z] * ahead_ref[i, other]
                total = term if total is None else total + term
            acc_ref[n] += jnp.sum(ahead_ref[i, z] * total, axis=0)


def pairs_kernel(shape, acc_ref, *refs):
    layers, group, parts = shape
    ahead_refs, after_refs, sums_refs = refs[:parts], refs[parts : 2 * parts], refs[2 * parts :]
    each = group // parts
    sums = jnp.sum(acc_ref[...], axis=1)
    lines = []
    for n in range(group):
        ahead_ref, after_ref, i = ahead_refs[n // each], after_refs[n // each], n % each
        total = None
        for z in range(layers):
            line = None
            for j in range(layers):
                k = j + layers - z
                if k <= 6:
                    term = -COEFFS[k] * after_ref[i, j]
                    line = term if line is None else line + term
            if line is not None:
                line = line * ahead_ref[i, z]
                total = line if total is None else total + line
        lines.append(jnp.sum(jnp.sum(total, axis=0), axis=0, keepdims=True))
    sums = jnp.concatenate([sums[:group] + jnp.concatenate(lines, axis=0), sums[group:]], axis=0)
    put_copies(sums_refs, rows_to_lanes(sums))


def density_kernel(shape, planes_ref, source_ref, residual_ref, *refs):
    layers, group, parts, halves, members, width, margin, cut = shape
    sums_refs, numbers_refs, refs = refs[:parts], refs[parts : parts + cut], refs[parts + cut :]
    cuts_ref, scales_ref, ring_ref = refs
    each = group // cut
    first = lax.axis_index("orb")
    total = lanes_to_rows(add_all(sums_refs)[:1], 3 * group)
    norm, curve, alpha = (
        jnp.concatenate([ref[i * each : (i + 1) * each, :] for ref in numbers_refs], axis=0) for i in range(3)
    )
    squares, cross, bend = total[2 * group : 3 * group], total[group : 2 * group], total[:group]
    beta = squares / norm
    bend = bend + 2.0 * beta * cross + beta * beta * curve
    second = squares / bend
    scales_ref[:group, :] = alpha + second * beta
    scales_ref[group : 2 * group, :] = second

    def layer(z, carry):
        total = jnp.zeros(planes_ref.shape[2:], f32)
        for n in range(group):
            field = scales_ref[n : n + 1, :] * source_ref[n, z]
            field = field + scales_ref[group + n : group + n + 1, :] * residual_ref[n, z]
            total = total + field * planes_ref[first * group + n, z]
        total = blocks(4.0 * total)
        for h in range(halves):
            ring_ref[z, h, SUB : SUB + NY, :] = total[h]
            ring_ref[z, h, :SUB, :] = total[h, NY - SUB :]
            ring_ref[z, h, SUB + NY :, :] = total[h, :SUB]
        return carry

    lax.fori_loop(0, layers, layer, 0)
    for k in range(members):
        owner = lax.rem(first + k, members)
        for z in range(layers):
            for h in range(halves):
                rows = width + 2 * margin
                cuts_ref[k, pl.ds((z * halves + h) * rows, rows)] = ring_ref[
                    z, h, pl.ds(owner * width + SUB - margin, rows), :
                ]


def response_kernel(shape, source_ref, residual_ref, scales_ref, response_ref):
    layers, group, halves = shape
    tiles = NY * halves

    def layer(z, carry):
        for n in range(group):
            field = scales_ref[n : n + 1, :] * source_ref[n, z]
            field = field + scales_ref[group + n : group + n + 1, :] * residual_ref[n, z]
            for h in range(halves):
                for q in range(NY // SUB):
                    start = (z * tiles + q * SUB * halves + h) * group + n
                    response_ref[pl.ds(start, SUB, stride=group * halves), :] = field[h * (NY // SUB) + q]
        return carry

    lax.fori_loop(0, layers, layer, 0)


def gather_kernel(edge, cuts_ref, *refs):
    dense_ref, top_ref, bottom_ref = refs[-3:]
    total = cuts_ref[0]
    for ref in refs[:-3]:
        total = total + ref[...]
    dense_ref[...] = total
    top_ref[...] = total[-edge:]
    bottom_ref[...] = total[:edge]


def jacobi_kernel(shape, dense_ref, before_ref, after_ref, induced_ref, slab_ref, out_ref):
    layers, halves, width, margin = shape
    rows = width + 2 * margin
    full = -(-rows // SUB) * SUB
    scale = 1.0 / (6.0 + SCREEN)
    edge = 2 * halves * rows
    middle = layers * halves * rows
    slab_ref[:edge, :] = before_ref[...]
    slab_ref[edge : edge + middle, :] = dense_ref[...]
    slab_ref[edge + middle : 2 * edge + middle, :] = after_ref[...]
    slab_ref[2 * edge + middle :, :] = jnp.zeros((slab_ref.shape[0] - 2 * edge - middle, LANES), f32)
    dense = [
        [slab_ref[(z * halves + h) * rows : (z * halves + h) * rows + full, :] for h in range(halves)]
        for z in range(layers + 4)
    ]
    field = [[scale * v for v in sheet] for sheet in dense]

    def up(value):
        return pltpu.roll(value, 1, 0)

    def down(value):
        return pltpu.roll(value, full - 1, 0)

    for sweep in range(2):
        fresh = []
        for z in range(1, len(field) - 1):
            right, left = roll_x(field[z], 1), roll_x(field[z], -1)
            sheet = []
            for h in range(halves):
                value = dense[z][h] + field[z - 1][h] + field[z + 1][h] + right[h] + left[h]
                value = value + up(field[z][h]) + down(field[z][h])
                sheet.append(scale * value)
            fresh.append(sheet)
        field, dense = fresh, dense[1:-1]
    for z in range(layers):
        for h in range(halves):
            out_ref[pl.ds((z * halves + h) * full, full), :] = field[z][h]
    for h in range(halves):
        for y in range(width):
            c = y * halves + h
            induced_ref[:, c * LANES : (c + 1) * LANES] = out_ref[
                pl.ds(h * full + margin + y, layers, stride=halves * full), :
            ]


def per_device(orbitals, potential, perturb, energies, omega):
    norb, layers, columns = orbitals.shape
    group = energies.shape[0]
    bricks, members = lax.axis_size("brick"), lax.axis_size("orb")
    ncell = layers * bricks * columns
    halves = columns // NY // LANES
    tiles = columns // LANES
    spots = tiles // SUB
    rows = orbitals.transpose(1, 0, 2).reshape(layers, norb // SUB, SUB, tiles, LANES)
    rows = rows.transpose(0, 1, 3, 2, 4).reshape(layers * norb * tiles, LANES)
    own = (group, layers, spots, SUB, LANES)
    flat = (group * norb, LANES)

    size = norb * tiles
    gram = call(
        functools.partial(gram_kernel, (norb, layers, halves, group)),
        copies("brick", norb + SUB, norb),
        [
            (layers * size, LANES),
            (layers, columns),
            pltpu.SemaphoreType.DMA((layers,)),
            pltpu.SemaphoreType.DMA,
        ],
        0,
        rows,
        perturb,
        far=2,
        limit=60 * 1024 * 1024,
    )
    grams = parts_of(gram, "brick")
    plane = (layers, spots, SUB, LANES)
    planes, perturb_planes, potential_planes = call(
        functools.partial(tile_kernel, (norb, layers, halves)),
        [(norb,) + plane, plane, plane],
        [],
        0,
        rows,
        perturb,
        potential,
    )
    share = 3 * spots // 8
    cells = (SUB, LANES)
    shared, rest, coefs = call(
        functools.partial(inner_kernel, (norb, layers, group, len(grams), share), ncell),
        [(group, layers, share) + cells, (group, layers, spots - 2 * share) + cells, flat],
        [(SUB, norb)],
        0,
        planes,
        perturb_planes,
        *grams,
    )
    inner, source, partial, overlap, along, square = call(
        functools.partial(local_kernel, (norb, layers, group, len(grams), halves, share), ncell),
        [own, own, own, (norb, norb, LANES), flat, (group,) + cells],
        [flat, (SUB, norb)],
        2,
        omega,
        energies,
        planes,
        perturb_planes,
        potential_planes,
        shared,
        rest,
        coefs,
        *grams,
    )
    before, after = shifted(shared, "brick", 1), shifted(shared, "brick", -1)
    pieces = 1 if group % 2 else 2
    each = group // pieces
    halos = call(
        functools.partial(halo_kernel, (layers, group)),
        [(each, layers, share) + cells] * pieces,
        [],
        0,
        before,
        after,
        square,
    )
    partner = [lax.ppermute(halo, "freq", [(0, 1), (1, 0)]) for halo in halos]
    count = group * norb + group
    before_rest, after_rest = shifted(rest, "brick", 1), shifted(rest, "brick", -1)
    mine, earlier = call(
        functools.partial(mine_kernel, (norb, layers, group), share),
        [shared.shape, (count, LANES)],
        [(count,) + cells],
        0,
        planes,
        inner,
        partial,
        *halos,
    )
    other, earlier = call(
        functools.partial(other_kernel, (norb, layers, group), share),
        [shared.shape, (count, LANES)],
        [(count,) + cells],
        0,
        planes,
        inner,
        partial,
        earlier,
        *partner,
    )
    applied, *sums = call(
        functools.partial(rest_kernel, (norb, layers, group), share),
        [own] + copies("brick", SUB, LANES),
        [rest.shape, (count,) + cells],
        0,
        planes,
        inner,
        partial,
        square,
        mine,
        other,
        earlier,
        after_rest,
        before_rest,
    )
    sums = parts_of(sums, "brick")
    runs = 1
    part = group // runs
    steps = [
        call(
            functools.partial(residual_kernel, (norb, layers, group, len(sums), i * part, part), ncell),
            [(part,) + own[1:], (part * norb, LANES), (3 * part, LANES)],
            [(part * norb, LANES)],
            0,
            planes,
            source,
            applied,
            overlap,
            along,
            *sums,
        )
        for i in range(runs)
    ]
    aheads, plains, numbers = zip(*steps)
    afters = [shifted(ahead, "brick", -1) for ahead in aheads]
    residual, acc = call(
        functools.partial(second_kernel, (norb, layers, group, halves, runs)),
        [own, (3 * group,) + cells],
        [],
        2,
        omega,
        energies,
        planes,
        potential_planes,
        source,
        applied,
        *aheads,
        *plains,
        *numbers,
    )
    sums = call(
        functools.partial(pairs_kernel, (layers, group, runs)),
        copies("brick", SUB, LANES),
        [],
        0,
        acc,
        *aheads,
        *afters,
    )
    sums = parts_of(sums, "brick")
    width = NY // members
    margin = 2
    span = width + 2 * margin
    edge = 2 * halves * span
    cut = (layers * halves * span, LANES)
    cuts, scales = call(
        functools.partial(density_kernel, (layers, group, len(sums), halves, members, width, margin, runs)),
        [(members,) + cut, (2 * group, LANES)],
        [(layers, halves, NY + 2 * SUB, LANES)],
        0,
        planes,
        source,
        residual,
        *sums,
        *numbers,
    )
    others = [shifted(cuts[k], "orb", k) for k in range(1, members)]
    (response,) = call(
        functools.partial(response_kernel, (layers, group, halves)),
        [(layers * tiles * group, LANES)],
        [],
        0,
        source,
        residual,
        scales,
    )
    dense, top, bottom = call(
        functools.partial(gather_kernel, edge), [cut, (edge, LANES), (edge, LANES)], [], 0, cuts, *others
    )
    before, after = shifted(top, "brick", 1), shifted(bottom, "brick", -1)
    (induced,) = call(
        functools.partial(jacobi_kernel, (layers, halves, width, margin)),
        [(layers, width * halves * LANES)],
        [((layers + 4) * halves * span + SUB, LANES), (layers * halves * (-(-span // SUB) * SUB), LANES)],
        0,
        dense,
        before,
        after,
    )
    response = response.reshape(layers, tiles, group, LANES).transpose(2, 0, 1, 3)
    return response.reshape(group, layers, columns), induced


def solution(mesh):
    placed = (P(None, "brick", None), P("brick", None), P("brick", None), P("orb"), P("freq"))
    return jax.shard_map(
        per_device,
        mesh=mesh,
        in_specs=placed,
        out_specs=(P(("freq", "orb"), "brick", None), P(("freq", "brick"), "orb")),
        check_vma=False,
    )
```

```python
import functools
import jax
import jax.numpy as jnp
from jax import lax
from jax.experimental import pallas as pl
from jax.experimental.pallas import tpu as pltpu
from jax.sharding import PartitionSpec as P

NY = 32
LANES = 128
SUB = 8

COEFFS = (
    -5369.0 / 1800.0,
    12.0 / 7.0,
    -15.0 / 56.0,
    10.0 / 189.0,
    -1.0 / 112.0,
    2.0 / 825.0,
    -1.0 / 5544.0,
)
SCREEN = 0.25
HIGHEST = lax.Precision.HIGHEST
VMEM_LIMIT = 16 * 1024 * 1024
SMEM = pl.BlockSpec(memory_space=pltpu.SMEM)
VMEM = pl.BlockSpec(memory_space=pltpu.VMEM)
HBM = pl.BlockSpec(memory_space=pltpu.HBM)
f32 = jnp.float32


def call(kernel, outs, scratch, smem, *args, far=0, limit=VMEM_LIMIT):
    return pl.pallas_call(
        kernel,
        out_shape=[jax.ShapeDtypeStruct(s, f32) for s in outs],
        in_specs=[SMEM] * smem + [HBM] * far + [VMEM] * (len(args) - smem - far),
        out_specs=[VMEM] * len(outs),
        scratch_shapes=[pltpu.VMEM(s, f32) if isinstance(s, tuple) else s for s in scratch],
        compiler_params=pltpu.CompilerParams(vmem_limit_bytes=limit),
    )(*args)


def copies(axis, rows, columns):
    size = lax.axis_size(axis)
    direct = size <= 4 and size & (size - 1) == 0
    return [(rows, columns) for k in range(size - 1 if direct else 1)]


def parts_of(arrays, axis):
    size = lax.axis_size(axis)
    if len(arrays) < size - 1:
        return [lax.psum(arrays[0], axis)]
    others = [
        lax.ppermute(array, axis, [(i, i ^ (k + 1)) for i in range(size)]) for k, array in enumerate(arrays)
    ]
    return [arrays[0]] + others


def put_copies(refs, value):
    rows = value.shape[0]
    for ref in refs:
        ref[:rows, :] = value
        if ref.shape[0] > rows:
            ref[rows:, :] = jnp.zeros((ref.shape[0] - rows, ref.shape[1]), f32)


def shifted(array, axis, step):
    size = lax.axis_size(axis)
    return lax.ppermute(array, axis, [(i, (i + step) % size) for i in range(size)])


def add_all(refs):
    total = refs[0][...]
    for ref in refs[1:]:
        total = total + ref[: total.shape[0], :]
    return total


def rows_to_lanes(matrix):
    count = matrix.shape[0]
    lane = lax.broadcasted_iota(jnp.int32, (count, LANES), 1)
    row = lax.broadcasted_iota(jnp.int32, (count, LANES), 0)
    value = jnp.broadcast_to(jnp.sum(matrix, axis=1, keepdims=True), (count, LANES))
    line = jnp.sum(jnp.where(lane == row, value, 0.0), axis=0, keepdims=True)
    return jnp.broadcast_to(line, (SUB, LANES))


def lanes_to_rows(line, count):
    wide = line.shape[1]
    lane = lax.broadcasted_iota(jnp.int32, (count, wide), 1)
    row = lax.broadcasted_iota(jnp.int32, (count, wide), 0)
    picked = jnp.where(lane == row, jnp.broadcast_to(line, (count, wide)), 0.0)
    return jnp.broadcast_to(jnp.sum(picked, axis=1, keepdims=True), (count, LANES))


def blocks(plane):
    return plane.reshape(-1, NY, LANES)


def gram_kernel(shape, far_rows_ref, far_perturb_ref, *refs):
    gram_refs, (rows_ref, perturb_ref, row_sems, perturb_sem) = refs[:-4], refs[-4:]
    norb, layers, halves, group = shape
    groups = norb // SUB
    tiles = NY * halves
    step = 16
    ahead = 3
    size = norb * tiles
    own = lax.axis_index("orb") * group // SUB

    def fetch(z):
        piece = pl.ds(z * size, size)
        return pltpu.make_async_copy(far_rows_ref.at[piece], rows_ref.at[piece], row_sems.at[z])

    weights = pltpu.make_async_copy(far_perturb_ref, perturb_ref, perturb_sem)
    fetch(0).start()
    weights.start()
    for z in range(1, min(ahead, layers)):
        fetch(z).start()
    weights.wait()

    def tile_row(z, t, c0):
        base = ((z * groups + t) * tiles + c0) * SUB
        return jnp.concatenate([rows_ref[pl.ds(base + c * SUB, SUB), :] for c in range(step)], axis=1)

    def rounded(value):
        return value.astype(jnp.bfloat16).astype(f32)

    def layer(z, total):
        fetch(z).wait()

        @pl.when(z + ahead < layers)
        def _():
            fetch(z + ahead).start()

        for c0 in range(0, tiles, step):
            field = jnp.concatenate([tile_row(z, t, c0) for t in range(groups)], axis=0)
            weighted = perturb_ref[pl.ds(z, 1), c0 * LANES : (c0 + step) * LANES] * tile_row(z, own, c0)
            rest = (field - rounded(field)).astype(jnp.bfloat16)
            field = field.astype(jnp.bfloat16)
            pair = jnp.concatenate([weighted, weighted - rounded(weighted)], axis=0).astype(jnp.bfloat16)
            left = jnp.concatenate([field, pair], axis=0)
            right = jnp.concatenate([field, rest], axis=0)
            total = total + lax.dot_general(
                left, right, (((1,), (1,)), ((), ())), preferred_element_type=f32
            )
        return total

    total = lax.fori_loop(0, layers, layer, jnp.zeros((norb + 2 * SUB, 2 * norb), f32))
    cross = total[:norb, norb:]
    overlap = total[:norb, :norb] + cross + cross.T
    total = total[norb:, :norb] + total[norb:, norb:]
    put_copies(gram_refs, jnp.concatenate([overlap, total[:SUB] + total[SUB:]], axis=0))


def tile_kernel(shape, rows_ref, perturb_ref, potential_ref, planes_ref, *refs):
    norb, layers, halves = shape
    tiles = NY * halves

    def layer(z, carry):
        for m in range(norb):
            base = (z * (norb // SUB) + m // SUB) * tiles * SUB + m % SUB
            for h in range(halves):
                for q in range(NY // SUB):
                    start = base + (q * SUB * halves + h) * SUB
                    planes_ref[m, z, h * (NY // SUB) + q] = rows_ref[pl.ds(start, SUB, stride=SUB * halves), :]
        return carry

    lax.fori_loop(0, layers, layer, 0)
    for array_ref, planes_ref in zip((perturb_ref, potential_ref), refs):
        for z in range(layers):
            for y in range(NY):
                for h in range(halves):
                    c = y * halves + h
                    planes_ref[z, h * (NY // SUB) + y // SUB, y % SUB : y % SUB + 1, :] = array_ref[
                        z : z + 1, c * LANES : (c + 1) * LANES
                    ]


def small_matrices(shape, ncell, gram_refs, lines_ref):
    norb, group = shape
    total = add_all(gram_refs)
    overlap = total[:norb]
    lines_ref[...] = total[norb:]
    start = lax.rem(lax.axis_index("orb") * group, SUB)
    rows = []
    for n in range(group):
        line = lines_ref[pl.ds(start + n, 1), :]
        again = jnp.sum(lanes_to_rows(line, norb)[:, :norb] * overlap, axis=0, keepdims=True)
        rows.append((line, again * (1.0 / ncell)))
    return overlap, rows


def whole(ref, n, z):
    return ref[n, z]


def combine(layers, group, norb, planes_ref, coef_ref, start, finish, pick=whole):
    def layer(z, carry):
        sums = [start(n, z) for n in range(group)]
        for m in range(norb):
            field = pick(planes_ref, m, z)
            for n in range(group):
                sums[n] = sums[n] + field * coef_ref[pl.ds(n * norb + m, 1), :]
        for n in range(group):
            finish(n, z, sums[n])
        return carry

    lax.fori_loop(0, layers, layer, 0)


def inner_kernel(shape, ncell, planes_ref, perturb_ref, *refs):
    norb, layers, group, parts, share = shape
    gram_refs = refs[:parts]
    shared_ref, rest_ref, coef_ref, lines_ref = refs[parts:]
    first = lax.axis_index("orb") * group
    overlap, rows = small_matrices((norb, group), ncell, gram_refs, lines_ref)
    for n, (line, again) in enumerate(rows):
        coefs = (2.0 * line - again) * (1.0 / ncell)
        coef_ref[n * norb : (n + 1) * norb, :] = lanes_to_rows(coefs, norb)
    mine = pl.ds(lax.axis_index("freq") * share, share)

    def pick(ref, n, z):
        return jnp.concatenate([ref[n, z, mine], ref[n, z, 2 * share :]], axis=0)

    def start(n, z):
        weight = jnp.concatenate([perturb_ref[z, mine], perturb_ref[z, 2 * share :]], axis=0)
        return -(weight * pick(planes_ref, first + n, z))

    def finish(n, z, value):
        shared_ref[n, z] = value[:share]
        rest_ref[n, z] = value[share:]

    combine(layers, group, norb, planes_ref, coef_ref, start, finish, pick)


def roll_x(halves_list, amount):
    count = len(halves_list)
    lane = lax.broadcasted_iota(jnp.int32, halves_list[0].shape, 1)
    turned = [pltpu.roll(v, amount % LANES, 1) for v in halves_list]
    if amount > 0:
        return [jnp.where(lane >= amount, turned[h], turned[(h - 1) % count]) for h in range(count)]
    return [
        jnp.where(lane < LANES + amount, turned[h], turned[(h + 1) % count]) for h in range(count)
    ]


def roll_y(value, amount):
    return pltpu.roll(value, amount % NY, 0)


def local_kernel(shape, ncell, omega_ref, energies_ref, planes_ref, perturb_ref, potential_ref, shared_ref, rest_ref, inner_coef_ref, *refs):
    norb, layers, group, parts, halves, share = shape
    gram_refs = refs[:parts]
    inner_ref, source_ref, partial_ref, overlap_ref, along_ref, square_ref, coef_ref, lines_ref = refs[parts:]
    first = lax.axis_index("orb") * group
    overlap, rows = small_matrices((norb, group), ncell, gram_refs, lines_ref)
    for m in range(norb):
        overlap_ref[m] = jnp.broadcast_to(overlap[:, m : m + 1], (norb, LANES))
    for n, (line, again) in enumerate(rows):
        place = slice(n * norb, (n + 1) * norb)
        coef_ref[place, :] = lanes_to_rows(line * (1.0 / ncell), norb)
        along_ref[place, :] = lanes_to_rows(again - line, norb)
    square_ref[...] = jnp.zeros_like(square_ref)

    def start(n, z):
        return -(perturb_ref[z] * planes_ref[first + n, z])

    def finish(n, z, value):
        source_ref[n, z] = value
        square_ref[n] += jnp.sum(value * value, axis=0)

    combine(layers, group, norb, planes_ref, coef_ref, start, finish)

    place = lax.axis_index("freq") * share
    mine, other = pl.ds(place, share), pl.ds(share - place, share)

    def start_other(n, z):
        return -(perturb_ref[z, other] * planes_ref[first + n, z, other])

    def finish_other(n, z, value):
        inner_ref[n, z, other] = value
        inner_ref[n, z, mine] = shared_ref[n, z]
        inner_ref[n, z, 2 * share :] = rest_ref[n, z]

    def pick_other(ref, n, z):
        return ref[n, z, other]

    combine(layers, group, norb, planes_ref, inner_coef_ref, start_other, finish_other, pick_other)

    for n in range(group):
        def layer(z, carry):
            plane = blocks(inner_ref[n, z])
            sheets = [plane[h] for h in range(halves)]
            sums = [(3.0 * COEFFS[0]) * v for v in sheets]
            for k in range(1, 7):
                right, left = roll_x(sheets, k), roll_x(sheets, -k)
                for h in range(halves):
                    around = right[h] + left[h] + roll_y(sheets[h], k) + roll_y(sheets[h], -k)
                    sums[h] = sums[h] + COEFFS[k] * around
            total = jnp.stack(sums).reshape(inner_ref.shape[2:])
            shift = potential_ref[z] + (omega_ref[0] - energies_ref[n])
            partial_ref[n, z] = shift * inner_ref[n, z] - 0.5 * total
            return carry

        lax.fori_loop(0, layers, layer, 0)
        for z in range(layers):
            total = None
            for other in range(layers):
                k = abs(other - z)
                if k == 0 or k > 6:
                    continue
                term = (-0.5 * COEFFS[k]) * inner_ref[n, other]
                total = term if total is None else total + term
            if total is not None:
                partial_ref[n, z] += total


def halo_sum(layers, n, z, before_ref, after_ref):
    total = None
    for j in range(layers):
        for k, ref in ((z + layers - j, before_ref), (j + layers - z, after_ref)):
            if k <= 6:
                term = (-0.5 * COEFFS[k]) * ref[n, j]
                total = term if total is None else total + term
    return total


def halo_kernel(shape, before_ref, after_ref, square_ref, *halo_refs):
    layers, group = shape
    each = group // len(halo_refs)
    for n in range(group):
        for z in range(layers):
            halo_refs[n // each][n % each, z] = halo_sum(layers, n, z, before_ref, after_ref)


def multiply(shape, spots, planes_ref, inner_ref, field_ref, acc_ref):
    norb, layers, group = shape
    acc_ref[...] = jnp.zeros_like(acc_ref)

    def layer(z, carry):
        fields = [field_ref[n, z] for n in range(group)]
        for n in range(group):
            acc_ref[group * norb + n] += jnp.sum(fields[n] * inner_ref[n, z, spots], axis=0)
        for m in range(norb):
            orbital = planes_ref[m, z, spots]
            for n in range(group):
                acc_ref[n * norb + m] += jnp.sum(orbital * fields[n], axis=0)
        return carry

    lax.fori_loop(0, layers, layer, 0)
    return jnp.sum(acc_ref[...], axis=1)


def mine_kernel(shape, share, planes_ref, inner_ref, partial_ref, *refs):
    norb, layers, group = shape
    field_ref, sums_ref, acc_ref = refs[-3:]
    each = group // (len(refs) - 3)
    spots = pl.ds(lax.axis_index("freq") * share, share)
    for n in range(group):
        for z in range(layers):
            field_ref[n, z] = partial_ref[n, z, spots] + refs[n // each][n % each, z]
    sums_ref[...] = multiply(shape, spots, planes_ref, inner_ref, field_ref, acc_ref)


def other_kernel(shape, share, planes_ref, inner_ref, partial_ref, earlier_ref, *refs):
    norb, layers, group = shape
    field_ref, sums_ref, acc_ref = refs[-3:]
    each = group // (len(refs) - 3)
    spots = pl.ds(share - lax.axis_index("freq") * share, share)
    for n in range(group):
        for z in range(layers):
            field_ref[n, z] = partial_ref[n, z, spots] + refs[n // each][n % each, z]
    sums = multiply(shape, spots, planes_ref, inner_ref, field_ref, acc_ref)
    sums_ref[...] = sums + earlier_ref[...]


def rest_kernel(shape, share, planes_ref, inner_ref, partial_ref, square_ref, mine_ref, other_ref, earlier_ref, after_ref, before_ref, *refs):
    norb, layers, group = shape
    applied_ref, sums_refs, (field_ref, acc_ref) = refs[0], refs[1:-2], refs[-2:]
    place = lax.axis_index("freq") * share
    mine, other = pl.ds(place, share), pl.ds(share - place, share)
    spots = pl.ds(2 * share, field_ref.shape[2])
    for n in range(group):
        for z in range(layers):
            field = partial_ref[n, z, spots] + halo_sum(layers, n, z, before_ref, after_ref)
            field_ref[n, z] = field
            applied_ref[n, z, 2 * share :] = field
            applied_ref[n, z, mine] = mine_ref[n, z]
            applied_ref[n, z, other] = other_ref[n, z]
    sums = multiply(shape, spots, planes_ref, inner_ref, field_ref, acc_ref) + earlier_ref[...]
    sums = rows_to_lanes(jnp.concatenate([sums, jnp.sum(square_ref[...], axis=1)], axis=0))
    put_copies(sums_refs, sums)


def residual_kernel(shape, ncell, planes_ref, source_ref, applied_ref, overlap_ref, along_ref, *refs):
    norb, layers, group, parts, begin, count = shape
    sums_refs = refs[:parts]
    ahead_ref, plain_ref, numbers_ref, coef_ref = refs[parts:]
    size = group * norb
    total = lanes_to_rows(add_all(sums_refs)[:1], size + 2 * group)
    curve = total[size + begin : size + begin + count]
    norm = total[size + group + begin : size + group + begin + count]
    step = norm / curve
    numbers_ref[:count, :] = norm
    numbers_ref[count : 2 * count, :] = curve
    numbers_ref[2 * count : 3 * count, :] = step
    for i in range(count):
        n = begin + i
        rows = slice(i * norb, (i + 1) * norb)
        product = total[n * norb : (n + 1) * norb]
        alpha = step[i : i + 1]
        again = jnp.zeros((norb, LANES), f32)
        for m in range(norb):
            again = again + overlap_ref[m] * product[m : m + 1]
        left = along_ref[n * norb : (n + 1) * norb, :] - alpha * (product - again * (1.0 / ncell))
        plain_ref[rows, :] = alpha * product * (1.0 / ncell)
        coef_ref[rows, :] = (alpha * product - left) * (1.0 / ncell)

    def start(i, z):
        return source_ref[begin + i, z] - numbers_ref[2 * count + i : 2 * count + i + 1, :] * applied_ref[begin + i, z]

    def finish(i, z, value):
        ahead_ref[i, z] = value

    combine(layers, count, norb, planes_ref, coef_ref, start, finish)


def second_kernel(shape, omega_ref, energies_ref, planes_ref, potential_ref, source_ref, applied_ref, *refs):
    norb, layers, group, halves, parts = shape
    ahead_refs, plain_refs, numbers_refs = refs[:parts], refs[parts : 2 * parts], refs[2 * parts : 3 * parts]
    residual_ref, acc_ref = refs[3 * parts :]
    each = group // parts
    acc_ref[...] = jnp.zeros_like(acc_ref)

    for part in range(parts):
        first = part * each

        def start(i, z):
            alpha = numbers_refs[part][2 * each + i : 2 * each + i + 1, :]
            return source_ref[first + i, z] - alpha * applied_ref[first + i, z]

        def finish(i, z, value):
            residual_ref[first + i, z] = value
            acc_ref[2 * group + first + i] += jnp.sum(value * value, axis=0)

        combine(layers, each, norb, planes_ref, plain_refs[part], start, finish)

    for n in range(group):
        ahead_ref, i = ahead_refs[n // each], n % each

        def layer(z, carry):
            whole = ahead_ref[i, z]
            plane = blocks(whole)
            sheets = [plane[h] for h in range(halves)]
            sums = [(-1.5 * COEFFS[0]) * v for v in sheets]
            for k in range(1, 7):
                right = roll_x(sheets, k)
                for h in range(halves):
                    sums[h] = sums[h] - COEFFS[k] * (right[h] + roll_y(sheets[h], k))
            total = jnp.stack(sums).reshape(whole.shape)
            total = total + (potential_ref[z] + (omega_ref[0] - energies_ref[n])) * whole
            acc_ref[n] += jnp.sum(whole * total, axis=0)
            acc_ref[group + n] += jnp.sum(whole * applied_ref[n, z], axis=0)
            return carry

        lax.fori_loop(0, layers, layer, 0)
        for z in range(layers - 1):
            total = None
            for other in range(z + 1, min(layers, z + 7)):
                term = -COEFFS[other - z] * ahead_ref[i, other]
                total = term if total is None else total + term
            acc_ref[n] += jnp.sum(ahead_ref[i, z] * total, axis=0)


def pairs_kernel(shape, acc_ref, *refs):
    layers, group, parts = shape
    ahead_refs, after_refs, sums_refs = refs[:parts], refs[parts : 2 * parts], refs[2 * parts :]
    each = group // parts
    sums = jnp.sum(acc_ref[...], axis=1)
    lines = []
    for n in range(group):
        ahead_ref, after_ref, i = ahead_refs[n // each], after_refs[n // each], n % each
        total = None
        for z in range(layers):
            line = None
            for j in range(layers):
                k = j + layers - z
                if k <= 6:
                    term = -COEFFS[k] * after_ref[i, j]
                    line = term if line is None else line + term
            if line is not None:
                line = line * ahead_ref[i, z]
                total = line if total is None else total + line
        lines.append(jnp.sum(jnp.sum(total, axis=0), axis=0, keepdims=True))
    sums = jnp.concatenate([sums[:group] + jnp.concatenate(lines, axis=0), sums[group:]], axis=0)
    put_copies(sums_refs, rows_to_lanes(sums))


def density_kernel(shape, planes_ref, source_ref, residual_ref, *refs):
    layers, group, parts, halves, members, width, margin, cut = shape
    sums_refs, numbers_refs, refs = refs[:parts], refs[parts : parts + cut], refs[parts + cut :]
    cuts_ref, scales_ref, ring_ref = refs
    each = group // cut
    first = lax.axis_index("orb")
    total = lanes_to_rows(add_all(sums_refs)[:1], 3 * group)
    norm, curve, alpha = (
        jnp.concatenate([ref[i * each : (i + 1) * each, :] for ref in numbers_refs], axis=0) for i in range(3)
    )
    squares, cross, bend = total[2 * group : 3 * group], total[group : 2 * group], total[:group]
    beta = squares / norm
    bend = bend + 2.0 * beta * cross + beta * beta * curve
    second = squares / bend
    scales_ref[:group, :] = alpha + second * beta
    scales_ref[group : 2 * group, :] = second

    def layer(z, carry):
        total = jnp.zeros(planes_ref.shape[2:], f32)
        for n in range(group):
            field = scales_ref[n : n + 1, :] * source_ref[n, z]
            field = field + scales_ref[group + n : group + n + 1, :] * residual_ref[n, z]
            total = total + field * planes_ref[first * group + n, z]
        total = blocks(4.0 * total)
        for h in range(halves):
            ring_ref[z, h, SUB : SUB + NY, :] = total[h]
            ring_ref[z, h, :SUB, :] = total[h, NY - SUB :]
            ring_ref[z, h, SUB + NY :, :] = total[h, :SUB]
        return carry

    lax.fori_loop(0, layers, layer, 0)
    for k in range(members):
        owner = lax.rem(first + k, members)
        for z in range(layers):
            for h in range(halves):
                rows = width + 2 * margin
                cuts_ref[k, pl.ds((z * halves + h) * rows, rows)] = ring_ref[
                    z, h, pl.ds(owner * width + SUB - margin, rows), :
                ]


def response_kernel(shape, source_ref, residual_ref, scales_ref, response_ref):
    layers, group, halves = shape
    tiles = NY * halves

    def layer(z, carry):
        for n in range(group):
            field = scales_ref[n : n + 1, :] * source_ref[n, z]
            field = field + scales_ref[group + n : group + n + 1, :] * residual_ref[n, z]
            for h in range(halves):
                for q in range(NY // SUB):
                    start = (z * tiles + q * SUB * halves + h) * group + n
                    response_ref[pl.ds(start, SUB, stride=group * halves), :] = field[h * (NY // SUB) + q]
        return carry

    lax.fori_loop(0, layers, layer, 0)


def gather_kernel(edge, cuts_ref, *refs):
    dense_ref, top_ref, bottom_ref = refs[-3:]
    total = cuts_ref[0]
    for ref in refs[:-3]:
        total = total + ref[...]
    dense_ref[...] = total
    top_ref[...] = total[-edge:]
    bottom_ref[...] = total[:edge]


def jacobi_kernel(shape, dense_ref, before_ref, after_ref, induced_ref, slab_ref, out_ref):
    layers, halves, width, margin = shape
    rows = width + 2 * margin
    full = -(-rows // SUB) * SUB
    scale = 1.0 / (6.0 + SCREEN)
    edge = 2 * halves * rows
    middle = layers * halves * rows
    slab_ref[:edge, :] = before_ref[...]
    slab_ref[edge : edge + middle, :] = dense_ref[...]
    slab_ref[edge + middle : 2 * edge + middle, :] = after_ref[...]
    slab_ref[2 * edge + middle :, :] = jnp.zeros((slab_ref.shape[0] - 2 * edge - middle, LANES), f32)
    dense = [
        [slab_ref[(z * halves + h) * rows : (z * halves + h) * rows + full, :] for h in range(halves)]
        for z in range(layers + 4)
    ]
    field = [[scale * v for v in sheet] for sheet in dense]

    def up(value):
        return pltpu.roll(value, 1, 0)

    def down(value):
        return pltpu.roll(value, full - 1, 0)

    for sweep in range(2):
        fresh = []
        for z in range(1, len(field) - 1):
            right, left = roll_x(field[z], 1), roll_x(field[z], -1)
            sheet = []
            for h in range(halves):
                value = dense[z][h] + field[z - 1][h] + field[z + 1][h] + right[h] + left[h]
                value = value + up(field[z][h]) + down(field[z][h])
                sheet.append(scale * value)
            fresh.append(sheet)
        field, dense = fresh, dense[1:-1]
    for z in range(layers):
        for h in range(halves):
            out_ref[pl.ds((z * halves + h) * full, full), :] = field[z][h]
    for h in range(halves):
        for y in range(width):
            c = y * halves + h
            induced_ref[:, c * LANES : (c + 1) * LANES] = out_ref[
                pl.ds(h * full + margin + y, layers, stride=halves * full), :
            ]


def per_device(orbitals, potential, perturb, energies, omega):
    norb, layers, columns = orbitals.shape
    group = energies.shape[0]
    bricks, members = lax.axis_size("brick"), lax.axis_size("orb")
    ncell = layers * bricks * columns
    halves = columns // NY // LANES
    tiles = columns // LANES
    spots = tiles // SUB
    rows = orbitals.transpose(1, 0, 2).reshape(layers, norb // SUB, SUB, tiles, LANES)
    rows = rows.transpose(0, 1, 3, 2, 4).reshape(layers * norb * tiles, LANES)
    own = (group, layers, spots, SUB, LANES)
    flat = (group * norb, LANES)

    size = norb * tiles
    gram = call(
        functools.partial(gram_kernel, (norb, layers, halves, group)),
        copies("brick", norb + SUB, norb),
        [
            (layers * size, LANES),
            (layers, columns),
            pltpu.SemaphoreType.DMA((layers,)),
            pltpu.SemaphoreType.DMA,
        ],
        0,
        rows,
        perturb,
        far=2,
        limit=60 * 1024 * 1024,
    )
    grams = parts_of(gram, "brick")
    plane = (layers, spots, SUB, LANES)
    planes, perturb_planes, potential_planes = call(
        functools.partial(tile_kernel, (norb, layers, halves)),
        [(norb,) + plane, plane, plane],
        [],
        0,
        rows,
        perturb,
        potential,
    )
    share = 3 * spots // 8
    cells = (SUB, LANES)
    shared, rest, coefs = call(
        functools.partial(inner_kernel, (norb, layers, group, len(grams), share), ncell),
        [(group, layers, share) + cells, (group, layers, spots - 2 * share) + cells, flat],
        [(SUB, norb)],
        0,
        planes,
        perturb_planes,
        *grams,
    )
    inner, source, partial, overlap, along, square = call(
        functools.partial(local_kernel, (norb, layers, group, len(grams), halves, share), ncell),
        [own, own, own, (norb, norb, LANES), flat, (group,) + cells],
        [flat, (SUB, norb)],
        2,
        omega,
        energies,
        planes,
        perturb_planes,
        potential_planes,
        shared,
        rest,
        coefs,
        *grams,
    )
    before, after = shifted(shared, "brick", 1), shifted(shared, "brick", -1)
    pieces = 1 if group % 2 else 2
    each = group // pieces
    halos = call(
        functools.partial(halo_kernel, (layers, group)),
        [(each, layers, share) + cells] * pieces,
        [],
        0,
        before,
        after,
        square,
    )
    partner = [lax.ppermute(halo, "freq", [(0, 1), (1, 0)]) for halo in halos]
    count = group * norb + group
    before_rest, after_rest = shifted(rest, "brick", 1), shifted(rest, "brick", -1)
    mine, earlier = call(
        functools.partial(mine_kernel, (norb, layers, group), share),
        [shared.shape, (count, LANES)],
        [(count,) + cells],
        0,
        planes,
        inner,
        partial,
        *halos,
    )
    other, earlier = call(
        functools.partial(other_kernel, (norb, layers, group), share),
        [shared.shape, (count, LANES)],
        [(count,) + cells],
        0,
        planes,
        inner,
        partial,
        earlier,
        *partner,
    )
    applied, *sums = call(
        functools.partial(rest_kernel, (norb, layers, group), share),
        [own] + copies("brick", SUB, LANES),
        [rest.shape, (count,) + cells],
        0,
        planes,
        inner,
        partial,
        square,
        mine,
        other,
        earlier,
        after_rest,
        before_rest,
    )
    sums = parts_of(sums, "brick")
    runs = 1 if group % 2 else 2
    part = group // runs
    steps = [
        call(
            functools.partial(residual_kernel, (norb, layers, group, len(sums), i * part, part), ncell),
            [(part,) + own[1:], (part * norb, LANES), (3 * part, LANES)],
            [(part * norb, LANES)],
            0,
            planes,
            source,
            applied,
            overlap,
            along,
            *sums,
        )
        for i in range(runs)
    ]
    aheads, plains, numbers = zip(*steps)
    afters = [shifted(ahead, "brick", -1) for ahead in aheads]
    residual, acc = call(
        functools.partial(second_kernel, (norb, layers, group, halves, runs)),
        [own, (3 * group,) + cells],
        [],
        2,
        omega,
        energies,
        planes,
        potential_planes,
        source,
        applied,
        *aheads,
        *plains,
        *numbers,
    )
    sums = call(
        functools.partial(pairs_kernel, (layers, group, runs)),
        copies("brick", SUB, LANES),
        [],
        0,
        acc,
        *aheads,
        *afters,
    )
    sums = parts_of(sums, "brick")
    width = NY // members
    margin = 2
    span = width + 2 * margin
    edge = 2 * halves * span
    cut = (layers * halves * span, LANES)
    cuts, scales = call(
        functools.partial(density_kernel, (layers, group, len(sums), halves, members, width, margin, runs)),
        [(members,) + cut, (2 * group, LANES)],
        [(layers, halves, NY + 2 * SUB, LANES)],
        0,
        planes,
        source,
        residual,
        *sums,
        *numbers,
    )
    others = [shifted(cuts[k], "orb", k) for k in range(1, members)]
    (response,) = call(
        functools.partial(response_kernel, (layers, group, halves)),
        [(layers * tiles * group, LANES)],
        [],
        0,
        source,
        residual,
        scales,
    )
    dense, top, bottom = call(
        functools.partial(gather_kernel, edge), [cut, (edge, LANES), (edge, LANES)], [], 0, cuts, *others[::-1]
    )
    before, after = shifted(top, "brick", 1), shifted(bottom, "brick", -1)
    (induced,) = call(
        functools.partial(jacobi_kernel, (layers, halves, width, margin)),
        [(layers, width * halves * LANES)],
        [((layers + 4) * halves * span + SUB, LANES), (layers * halves * (-(-span // SUB) * SUB), LANES)],
        0,
        dense,
        before,
        after,
    )
    response = response.reshape(layers, tiles, group, LANES).transpose(2, 0, 1, 3)
    return response.reshape(group, layers, columns), induced


def solution(mesh):
    placed = (P(None, "brick", None), P("brick", None), P("brick", None), P("orb"), P("freq"))
    return jax.shard_map(
        per_device,
        mesh=mesh,
        in_specs=placed,
        out_specs=(P(("freq", "orb"), "brick", None), P(("freq", "brick"), "orb")),
        check_vma=False,
    )
```

```python
import functools
import jax
import jax.numpy as jnp
from jax import lax
from jax.experimental import pallas as pl
from jax.experimental.pallas import tpu as pltpu
from jax.sharding import PartitionSpec as P

NY = 32
LANES = 128
SUB = 8

COEFFS = (
    -5369.0 / 1800.0,
    12.0 / 7.0,
    -15.0 / 56.0,
    10.0 / 189.0,
    -1.0 / 112.0,
    2.0 / 825.0,
    -1.0 / 5544.0,
)
SCREEN = 0.25
HIGHEST = lax.Precision.HIGHEST
VMEM_LIMIT = 16 * 1024 * 1024
SMEM = pl.BlockSpec(memory_space=pltpu.SMEM)
VMEM = pl.BlockSpec(memory_space=pltpu.VMEM)
HBM = pl.BlockSpec(memory_space=pltpu.HBM)
f32 = jnp.float32


def call(kernel, outs, scratch, smem, *args, far=0, limit=VMEM_LIMIT):
    return pl.pallas_call(
        kernel,
        out_shape=[jax.ShapeDtypeStruct(s, f32) for s in outs],
        in_specs=[SMEM] * smem + [HBM] * far + [VMEM] * (len(args) - smem - far),
        out_specs=[VMEM] * len(outs),
        scratch_shapes=[pltpu.VMEM(s, f32) if isinstance(s, tuple) else s for s in scratch],
        compiler_params=pltpu.CompilerParams(vmem_limit_bytes=limit),
    )(*args)


def copies(axis, rows, columns):
    size = lax.axis_size(axis)
    direct = size <= 4 and size & (size - 1) == 0
    return [(rows, columns) for k in range(size - 1 if direct else 1)]


def parts_of(arrays, axis):
    size = lax.axis_size(axis)
    if len(arrays) < size - 1:
        return [lax.psum(arrays[0], axis)]
    others = [
        lax.ppermute(array, axis, [(i, i ^ (k + 1)) for i in range(size)]) for k, array in enumerate(arrays)
    ]
    return [arrays[0]] + others


def put_copies(refs, value):
    rows = value.shape[0]
    for ref in refs:
        ref[:rows, :] = value
        if ref.shape[0] > rows:
            ref[rows:, :] = jnp.zeros((ref.shape[0] - rows, ref.shape[1]), f32)


def shifted(array, axis, step):
    size = lax.axis_size(axis)
    return lax.ppermute(array, axis, [(i, (i + step) % size) for i in range(size)])


def add_all(refs):
    total = refs[0][...]
    for ref in refs[1:]:
        total = total + ref[: total.shape[0], :]
    return total


def rows_to_lanes(matrix):
    count = matrix.shape[0]
    lane = lax.broadcasted_iota(jnp.int32, (count, LANES), 1)
    row = lax.broadcasted_iota(jnp.int32, (count, LANES), 0)
    value = jnp.broadcast_to(jnp.sum(matrix, axis=1, keepdims=True), (count, LANES))
    line = jnp.sum(jnp.where(lane == row, value, 0.0), axis=0, keepdims=True)
    return jnp.broadcast_to(line, (SUB, LANES))


def lanes_to_rows(line, count):
    wide = line.shape[1]
    lane = lax.broadcasted_iota(jnp.int32, (count, wide), 1)
    row = lax.broadcasted_iota(jnp.int32, (count, wide), 0)
    picked = jnp.where(lane == row, jnp.broadcast_to(line, (count, wide)), 0.0)
    return jnp.broadcast_to(jnp.sum(picked, axis=1, keepdims=True), (count, LANES))


def blocks(plane):
    return plane.reshape(-1, NY, LANES)


def gram_kernel(shape, far_rows_ref, far_perturb_ref, *refs):
    gram_refs, (rows_ref, perturb_ref, row_sems, perturb_sem) = refs[:-4], refs[-4:]
    norb, layers, halves, group = shape
    groups = norb // SUB
    tiles = NY * halves
    step = 16
    ahead = 3
    size = norb * tiles
    own = lax.axis_index("orb") * group // SUB

    def fetch(z):
        piece = pl.ds(z * size, size)
        return pltpu.make_async_copy(far_rows_ref.at[piece], rows_ref.at[piece], row_sems.at[z])

    weights = pltpu.make_async_copy(far_perturb_ref, perturb_ref, perturb_sem)
    fetch(0).start()
    weights.start()
    for z in range(1, min(ahead, layers)):
        fetch(z).start()
    weights.wait()

    def tile_row(z, t, c0):
        base = ((z * groups + t) * tiles + c0) * SUB
        return jnp.concatenate([rows_ref[pl.ds(base + c * SUB, SUB), :] for c in range(step)], axis=1)

    def rounded(value):
        return value.astype(jnp.bfloat16).astype(f32)

    def layer(z, total):
        fetch(z).wait()

        @pl.when(z + ahead < layers)
        def _():
            fetch(z + ahead).start()

        for c0 in range(0, tiles, step):
            field = jnp.concatenate([tile_row(z, t, c0) for t in range(groups)], axis=0)
            weighted = perturb_ref[pl.ds(z, 1), c0 * LANES : (c0 + step) * LANES] * tile_row(z, own, c0)
            rest = (field - rounded(field)).astype(jnp.bfloat16)
            field = field.astype(jnp.bfloat16)
            pair = jnp.concatenate([weighted, weighted - rounded(weighted)], axis=0).astype(jnp.bfloat16)
            left = jnp.concatenate([field, pair], axis=0)
            right = jnp.concatenate([field, rest], axis=0)
            total = total + lax.dot_general(
                left, right, (((1,), (1,)), ((), ())), preferred_element_type=f32
            )
        return total

    total = lax.fori_loop(0, layers, layer, jnp.zeros((norb + 2 * SUB, 2 * norb), f32))
    cross = total[:norb, norb:]
    overlap = total[:norb, :norb] + cross + cross.T
    total = total[norb:, :norb] + total[norb:, norb:]
    put_copies(gram_refs, jnp.concatenate([overlap, total[:SUB] + total[SUB:]], axis=0))


def tile_kernel(shape, rows_ref, perturb_ref, potential_ref, planes_ref, *refs):
    norb, layers, halves = shape
    tiles = NY * halves

    def layer(z, carry):
        for m in range(norb):
            base = (z * (norb // SUB) + m // SUB) * tiles * SUB + m % SUB
            for h in range(halves):
                for q in range(NY // SUB):
                    start = base + (q * SUB * halves + h) * SUB
                    planes_ref[m, z, h * (NY // SUB) + q] = rows_ref[pl.ds(start, SUB, stride=SUB * halves), :]
        return carry

    lax.fori_loop(0, layers, layer, 0)
    for array_ref, planes_ref in zip((perturb_ref, potential_ref), refs):
        for z in range(layers):
            for y in range(NY):
                for h in range(halves):
                    c = y * halves + h
                    planes_ref[z, h * (NY // SUB) + y // SUB, y % SUB : y % SUB + 1, :] = array_ref[
                        z : z + 1, c * LANES : (c + 1) * LANES
                    ]


def small_matrices(shape, ncell, gram_refs, lines_ref):
    norb, group = shape
    total = add_all(gram_refs)
    overlap = total[:norb]
    lines_ref[...] = total[norb:]
    start = lax.rem(lax.axis_index("orb") * group, SUB)
    rows = []
    for n in range(group):
        line = lines_ref[pl.ds(start + n, 1), :]
        again = jnp.sum(lanes_to_rows(line, norb)[:, :norb] * overlap, axis=0, keepdims=True)
        rows.append((line, again * (1.0 / ncell)))
    return overlap, rows


def whole(ref, n, z):
    return ref[n, z]


def combine(layers, group, norb, planes_ref, coef_ref, start, finish, pick=whole):
    def layer(z, carry):
        sums = [start(n, z) for n in range(group)]
        for m in range(norb):
            field = pick(planes_ref, m, z)
            for n in range(group):
                sums[n] = sums[n] + field * coef_ref[pl.ds(n * norb + m, 1), :]
        for n in range(group):
            finish(n, z, sums[n])
        return carry

    lax.fori_loop(0, layers, layer, 0)


def inner_kernel(shape, ncell, planes_ref, perturb_ref, *refs):
    norb, layers, group, parts, share = shape
    gram_refs = refs[:parts]
    shared_ref, coef_ref, lines_ref = refs[parts:]
    first = lax.axis_index("orb") * group
    overlap, rows = small_matrices((norb, group), ncell, gram_refs, lines_ref)
    for n, (line, again) in enumerate(rows):
        coefs = (2.0 * line - again) * (1.0 / ncell)
        coef_ref[n * norb : (n + 1) * norb, :] = lanes_to_rows(coefs, norb)
    mine = pl.ds(lax.axis_index("freq") * share, share)

    def pick(ref, n, z):
        return ref[n, z, mine]

    def start(n, z):
        return -(perturb_ref[z, mine] * pick(planes_ref, first + n, z))

    def finish(n, z, value):
        shared_ref[n, z] = value

    combine(layers, group, norb, planes_ref, coef_ref, start, finish, pick)


def alone_kernel(shape, planes_ref, perturb_ref, coef_ref, rest_ref):
    norb, layers, group, share = shape
    first = lax.axis_index("orb") * group

    def pick(ref, n, z):
        return ref[n, z, 2 * share :]

    def start(n, z):
        return -(perturb_ref[z, 2 * share :] * pick(planes_ref, first + n, z))

    def finish(n, z, value):
        rest_ref[n, z] = value

    combine(layers, group, norb, planes_ref, coef_ref, start, finish, pick)


def roll_x(halves_list, amount):
    count = len(halves_list)
    lane = lax.broadcasted_iota(jnp.int32, halves_list[0].shape, 1)
    turned = [pltpu.roll(v, amount % LANES, 1) for v in halves_list]
    if amount > 0:
        return [jnp.where(lane >= amount, turned[h], turned[(h - 1) % count]) for h in range(count)]
    return [
        jnp.where(lane < LANES + amount, turned[h], turned[(h + 1) % count]) for h in range(count)
    ]


def roll_y(value, amount):
    return pltpu.roll(value, amount % NY, 0)


def local_kernel(shape, ncell, omega_ref, energies_ref, planes_ref, perturb_ref, potential_ref, shared_ref, rest_ref, inner_coef_ref, *refs):
    norb, layers, group, parts, halves, share = shape
    gram_refs = refs[:parts]
    inner_ref, source_ref, partial_ref, overlap_ref, along_ref, square_ref, coef_ref, lines_ref = refs[parts:]
    first = lax.axis_index("orb") * group
    overlap, rows = small_matrices((norb, group), ncell, gram_refs, lines_ref)
    for m in range(norb):
        overlap_ref[m] = jnp.broadcast_to(overlap[:, m : m + 1], (norb, LANES))
    for n, (line, again) in enumerate(rows):
        place = slice(n * norb, (n + 1) * norb)
        coef_ref[place, :] = lanes_to_rows(line * (1.0 / ncell), norb)
        along_ref[place, :] = lanes_to_rows(again - line, norb)
    square_ref[...] = jnp.zeros_like(square_ref)

    def start(n, z):
        return -(perturb_ref[z] * planes_ref[first + n, z])

    def finish(n, z, value):
        source_ref[n, z] = value
        square_ref[n] += jnp.sum(value * value, axis=0)

    combine(layers, group, norb, planes_ref, coef_ref, start, finish)

    place = lax.axis_index("freq") * share
    mine, other = pl.ds(place, share), pl.ds(share - place, share)

    def start_other(n, z):
        return -(perturb_ref[z, other] * planes_ref[first + n, z, other])

    def finish_other(n, z, value):
        inner_ref[n, z, other] = value
        inner_ref[n, z, mine] = shared_ref[n, z]
        inner_ref[n, z, 2 * share :] = rest_ref[n, z]

    def pick_other(ref, n, z):
        return ref[n, z, other]

    combine(layers, group, norb, planes_ref, inner_coef_ref, start_other, finish_other, pick_other)

    for n in range(group):
        def layer(z, carry):
            plane = blocks(inner_ref[n, z])
            sheets = [plane[h] for h in range(halves)]
            sums = [(3.0 * COEFFS[0]) * v for v in sheets]
            for k in range(1, 7):
                right, left = roll_x(sheets, k), roll_x(sheets, -k)
                for h in range(halves):
                    around = right[h] + left[h] + roll_y(sheets[h], k) + roll_y(sheets[h], -k)
                    sums[h] = sums[h] + COEFFS[k] * around
            total = jnp.stack(sums).reshape(inner_ref.shape[2:])
            shift = potential_ref[z] + (omega_ref[0] - energies_ref[n])
            partial_ref[n, z] = shift * inner_ref[n, z] - 0.5 * total
            return carry

        lax.fori_loop(0, layers, layer, 0)
        for z in range(layers):
            total = None
            for other in range(layers):
                k = abs(other - z)
                if k == 0 or k > 6:
                    continue
                term = (-0.5 * COEFFS[k]) * inner_ref[n, other]
                total = term if total is None else total + term
            if total is not None:
                partial_ref[n, z] += total


def halo_sum(layers, n, z, before_ref, after_ref):
    total = None
    for j in range(layers):
        for k, ref in ((z + layers - j, before_ref), (j + layers - z, after_ref)):
            if k <= 6:
                term = (-0.5 * COEFFS[k]) * ref[n, j]
                total = term if total is None else total + term
    return total


def halo_kernel(shape, before_ref, after_ref, square_ref, *halo_refs):
    layers, group = shape
    each = group // len(halo_refs)
    for n in range(group):
        for z in range(layers):
            halo_refs[n // each][n % each, z] = halo_sum(layers, n, z, before_ref, after_ref)


def multiply(shape, spots, planes_ref, inner_ref, field_ref, acc_ref):
    norb, layers, group = shape
    acc_ref[...] = jnp.zeros_like(acc_ref)

    def layer(z, carry):
        fields = [field_ref[n, z] for n in range(group)]
        for n in range(group):
            acc_ref[group * norb + n] += jnp.sum(fields[n] * inner_ref[n, z, spots], axis=0)
        for m in range(norb):
            orbital = planes_ref[m, z, spots]
            for n in range(group):
                acc_ref[n * norb + m] += jnp.sum(orbital * fields[n], axis=0)
        return carry

    lax.fori_loop(0, layers, layer, 0)
    return jnp.sum(acc_ref[...], axis=1)


def mine_kernel(shape, share, planes_ref, inner_ref, partial_ref, *refs):
    norb, layers, group = shape
    field_ref, sums_ref, acc_ref = refs[-3:]
    each = group // (len(refs) - 3)
    spots = pl.ds(lax.axis_index("freq") * share, share)
    for n in range(group):
        for z in range(layers):
            field_ref[n, z] = partial_ref[n, z, spots] + refs[n // each][n % each, z]
    sums_ref[...] = multiply(shape, spots, planes_ref, inner_ref, field_ref, acc_ref)


def other_kernel(shape, share, planes_ref, inner_ref, partial_ref, earlier_ref, *refs):
    norb, layers, group = shape
    refs = refs[:-3][::-1] + refs[-3:]
    field_ref, sums_ref, acc_ref = refs[-3:]
    each = group // (len(refs) - 3)
    spots = pl.ds(share - lax.axis_index("freq") * share, share)
    for n in range(group):
        for z in range(layers):
            field_ref[n, z] = partial_ref[n, z, spots] + refs[n // each][n % each, z]
    sums = multiply(shape, spots, planes_ref, inner_ref, field_ref, acc_ref)
    sums_ref[...] = sums + earlier_ref[...]


def rest_kernel(shape, share, planes_ref, inner_ref, partial_ref, square_ref, mine_ref, other_ref, earlier_ref, after_ref, before_ref, *refs):
    norb, layers, group = shape
    applied_ref, sums_refs, (field_ref, acc_ref) = refs[0], refs[1:-2], refs[-2:]
    place = lax.axis_index("freq") * share
    mine, other = pl.ds(place, share), pl.ds(share - place, share)
    spots = pl.ds(2 * share, field_ref.shape[2])
    for n in range(group):
        for z in range(layers):
            field = partial_ref[n, z, spots] + halo_sum(layers, n, z, before_ref, after_ref)
            field_ref[n, z] = field
            applied_ref[n, z, 2 * share :] = field
            applied_ref[n, z, mine] = mine_ref[n, z]
            applied_ref[n, z, other] = other_ref[n, z]
    sums = multiply(shape, spots, planes_ref, inner_ref, field_ref, acc_ref) + earlier_ref[...]
    sums = rows_to_lanes(jnp.concatenate([sums, jnp.sum(square_ref[...], axis=1)], axis=0))
    put_copies(sums_refs, sums)


def residual_kernel(shape, ncell, planes_ref, source_ref, applied_ref, overlap_ref, along_ref, *refs):
    norb, layers, group, parts, begin, count = shape
    sums_refs = refs[:parts]
    ahead_ref, plain_ref, numbers_ref, coef_ref = refs[parts:]
    size = group * norb
    total = lanes_to_rows(add_all(sums_refs)[:1], size + 2 * group)
    curve = total[size + begin : size + begin + count]
    norm = total[size + group + begin : size + group + begin + count]
    step = norm / curve
    numbers_ref[:count, :] = norm
    numbers_ref[count : 2 * count, :] = curve
    numbers_ref[2 * count : 3 * count, :] = step
    for i in range(count):
        n = begin + i
        rows = slice(i * norb, (i + 1) * norb)
        product = total[n * norb : (n + 1) * norb]
        alpha = step[i : i + 1]
        again = jnp.zeros((norb, LANES), f32)
        for m in range(norb):
            again = again + overlap_ref[m] * product[m : m + 1]
        left = along_ref[n * norb : (n + 1) * norb, :] - alpha * (product - again * (1.0 / ncell))
        plain_ref[rows, :] = alpha * product * (1.0 / ncell)
        coef_ref[rows, :] = (alpha * product - left) * (1.0 / ncell)

    def start(i, z):
        return source_ref[begin + i, z] - numbers_ref[2 * count + i : 2 * count + i + 1, :] * applied_ref[begin + i, z]

    def finish(i, z, value):
        ahead_ref[i, z] = value

    combine(layers, count, norb, planes_ref, coef_ref, start, finish)


def second_kernel(shape, omega_ref, energies_ref, planes_ref, potential_ref, source_ref, applied_ref, *refs):
    norb, layers, group, halves, parts = shape
    ahead_refs, plain_refs, numbers_refs = refs[:parts], refs[parts : 2 * parts], refs[2 * parts : 3 * parts]
    residual_ref, acc_ref = refs[3 * parts :]
    each = group // parts
    acc_ref[...] = jnp.zeros_like(acc_ref)

    for part in range(parts):
        first = part * each

        def start(i, z):
            alpha = numbers_refs[part][2 * each + i : 2 * each + i + 1, :]
            return source_ref[first + i, z] - alpha * applied_ref[first + i, z]

        def finish(i, z, value):
            residual_ref[first + i, z] = value
            acc_ref[2 * group + first + i] += jnp.sum(value * value, axis=0)

        combine(layers, each, norb, planes_ref, plain_refs[part], start, finish)

    for n in range(group):
        ahead_ref, i = ahead_refs[n // each], n % each

        def layer(z, carry):
            whole = ahead_ref[i, z]
            plane = blocks(whole)
            sheets = [plane[h] for h in range(halves)]
            sums = [(-1.5 * COEFFS[0]) * v for v in sheets]
            for k in range(1, 7):
                right = roll_x(sheets, k)
                for h in range(halves):
                    sums[h] = sums[h] - COEFFS[k] * (right[h] + roll_y(sheets[h], k))
            total = jnp.stack(sums).reshape(whole.shape)
            total = total + (potential_ref[z] + (omega_ref[0] - energies_ref[n])) * whole
            acc_ref[n] += jnp.sum(whole * total, axis=0)
            acc_ref[group + n] += jnp.sum(whole * applied_ref[n, z], axis=0)
            return carry

        lax.fori_loop(0, layers, layer, 0)
        for z in range(layers - 1):
            total = None
            for other in range(z + 1, min(layers, z + 7)):
                term = -COEFFS[other - z] * ahead_ref[i, other]
                total = term if total is None else total + term
            acc_ref[n] += jnp.sum(ahead_ref[i, z] * total, axis=0)


def pairs_kernel(shape, acc_ref, *refs):
    layers, group, parts = shape
    ahead_refs, after_refs, sums_refs = refs[:parts], refs[parts : 2 * parts], refs[2 * parts :]
    each = group // parts
    sums = jnp.sum(acc_ref[...], axis=1)
    lines = []
    for n in range(group):
        ahead_ref, after_ref, i = ahead_refs[n // each], after_refs[n // each], n % each
        total = None
        for z in range(layers):
            line = None
            for j in range(layers):
                k = j + layers - z
                if k <= 6:
                    term = -COEFFS[k] * after_ref[i, j]
                    line = term if line is None else line + term
            if line is not None:
                line = line * ahead_ref[i, z]
                total = line if total is None else total + line
        lines.append(jnp.sum(jnp.sum(total, axis=0), axis=0, keepdims=True))
    sums = jnp.concatenate([sums[:group] + jnp.concatenate(lines, axis=0), sums[group:]], axis=0)
    put_copies(sums_refs, rows_to_lanes(sums))


def density_kernel(shape, planes_ref, source_ref, residual_ref, *refs):
    layers, group, parts, halves, members, width, margin, cut = shape
    sums_refs, numbers_refs, refs = refs[:parts], refs[parts : parts + cut], refs[parts + cut :]
    cuts_ref, scales_ref, ring_ref = refs
    each = group // cut
    first = lax.axis_index("orb")
    total = lanes_to_rows(add_all(sums_refs)[:1], 3 * group)
    norm, curve, alpha = (
        jnp.concatenate([ref[i * each : (i + 1) * each, :] for ref in numbers_refs], axis=0) for i in range(3)
    )
    squares, cross, bend = total[2 * group : 3 * group], total[group : 2 * group], total[:group]
    beta = squares / norm
    bend = bend + 2.0 * beta * cross + beta * beta * curve
    second = squares / bend
    scales_ref[:group, :] = alpha + second * beta
    scales_ref[group : 2 * group, :] = second

    def layer(z, carry):
        total = jnp.zeros(planes_ref.shape[2:], f32)
        for n in range(group):
            field = scales_ref[n : n + 1, :] * source_ref[n, z]
            field = field + scales_ref[group + n : group + n + 1, :] * residual_ref[n, z]
            total = total + field * planes_ref[first * group + n, z]
        total = blocks(4.0 * total)
        for h in range(halves):
            ring_ref[z, h, SUB : SUB + NY, :] = total[h]
            ring_ref[z, h, :SUB, :] = total[h, NY - SUB :]
            ring_ref[z, h, SUB + NY :, :] = total[h, :SUB]
        return carry

    lax.fori_loop(0, layers, layer, 0)
    for k in range(members):
        owner = lax.rem(first + k, members)
        for z in range(layers):
            for h in range(halves):
                rows = width + 2 * margin
                cuts_ref[k, pl.ds((z * halves + h) * rows, rows)] = ring_ref[
                    z, h, pl.ds(owner * width + SUB - margin, rows), :
                ]


def response_kernel(shape, source_ref, residual_ref, scales_ref, response_ref):
    layers, group, halves = shape
    tiles = NY * halves

    def layer(z, carry):
        for n in range(group):
            field = scales_ref[n : n + 1, :] * source_ref[n, z]
            field = field + scales_ref[group + n : group + n + 1, :] * residual_ref[n, z]
            for h in range(halves):
                for q in range(NY // SUB):
                    start = (z * tiles + q * SUB * halves + h) * group + n
                    response_ref[pl.ds(start, SUB, stride=group * halves), :] = field[h * (NY // SUB) + q]
        return carry

    lax.fori_loop(0, layers, layer, 0)


def gather_kernel(edge, cuts_ref, *refs):
    dense_ref, top_ref, bottom_ref = refs[-3:]
    total = cuts_ref[0]
    for ref in refs[:-3]:
        total = total + ref[...]
    dense_ref[...] = total
    top_ref[...] = total[-edge:]
    bottom_ref[...] = total[:edge]


def jacobi_kernel(shape, dense_ref, before_ref, after_ref, induced_ref, slab_ref, out_ref):
    layers, halves, width, margin = shape
    rows = width + 2 * margin
    full = -(-rows // SUB) * SUB
    scale = 1.0 / (6.0 + SCREEN)
    edge = 2 * halves * rows
    middle = layers * halves * rows
    slab_ref[:edge, :] = before_ref[...]
    slab_ref[edge : edge + middle, :] = dense_ref[...]
    slab_ref[edge + middle : 2 * edge + middle, :] = after_ref[...]
    slab_ref[2 * edge + middle :, :] = jnp.zeros((slab_ref.shape[0] - 2 * edge - middle, LANES), f32)
    dense = [
        [slab_ref[(z * halves + h) * rows : (z * halves + h) * rows + full, :] for h in range(halves)]
        for z in range(layers + 4)
    ]
    field = [[scale * v for v in sheet] for sheet in dense]

    def up(value):
        return pltpu.roll(value, 1, 0)

    def down(value):
        return pltpu.roll(value, full - 1, 0)

    for sweep in range(2):
        fresh = []
        for z in range(1, len(field) - 1):
            right, left = roll_x(field[z], 1), roll_x(field[z], -1)
            sheet = []
            for h in range(halves):
                value = dense[z][h] + field[z - 1][h] + field[z + 1][h] + right[h] + left[h]
                value = value + up(field[z][h]) + down(field[z][h])
                sheet.append(scale * value)
            fresh.append(sheet)
        field, dense = fresh, dense[1:-1]
    for z in range(layers):
        for h in range(halves):
            out_ref[pl.ds((z * halves + h) * full, full), :] = field[z][h]
    for h in range(halves):
        for y in range(width):
            c = y * halves + h
            induced_ref[:, c * LANES : (c + 1) * LANES] = out_ref[
                pl.ds(h * full + margin + y, layers, stride=halves * full), :
            ]


def per_device(orbitals, potential, perturb, energies, omega):
    norb, layers, columns = orbitals.shape
    group = energies.shape[0]
    bricks, members = lax.axis_size("brick"), lax.axis_size("orb")
    ncell = layers * bricks * columns
    halves = columns // NY // LANES
    tiles = columns // LANES
    spots = tiles // SUB
    rows = orbitals.transpose(1, 0, 2).reshape(layers, norb // SUB, SUB, tiles, LANES)
    rows = rows.transpose(0, 1, 3, 2, 4).reshape(layers * norb * tiles, LANES)
    own = (group, layers, spots, SUB, LANES)
    flat = (group * norb, LANES)

    size = norb * tiles
    gram = call(
        functools.partial(gram_kernel, (norb, layers, halves, group)),
        copies("brick", norb + SUB, norb),
        [
            (layers * size, LANES),
            (layers, columns),
            pltpu.SemaphoreType.DMA((layers,)),
            pltpu.SemaphoreType.DMA,
        ],
        0,
        rows,
        perturb,
        far=2,
        limit=60 * 1024 * 1024,
    )
    grams = parts_of(gram, "brick")
    plane = (layers, spots, SUB, LANES)
    planes, perturb_planes, potential_planes = call(
        functools.partial(tile_kernel, (norb, layers, halves)),
        [(norb,) + plane, plane, plane],
        [],
        0,
        rows,
        perturb,
        potential,
    )
    share = 3 * spots // 8
    cells = (SUB, LANES)
    shared, coefs = call(
        functools.partial(inner_kernel, (norb, layers, group, len(grams), share), ncell),
        [(group, layers, share) + cells, flat],
        [(SUB, norb)],
        0,
        planes,
        perturb_planes,
        *grams,
    )
    (rest,) = call(
        functools.partial(alone_kernel, (norb, layers, group, share)),
        [(group, layers, spots - 2 * share) + cells],
        [],
        0,
        planes,
        perturb_planes,
        coefs,
    )
    inner, source, partial, overlap, along, square = call(
        functools.partial(local_kernel, (norb, layers, group, len(grams), halves, share), ncell),
        [own, own, own, (norb, norb, LANES), flat, (group,) + cells],
        [flat, (SUB, norb)],
        2,
        omega,
        energies,
        planes,
        perturb_planes,
        potential_planes,
        shared,
        rest,
        coefs,
        *grams,
    )
    before, after = shifted(shared, "brick", 1), shifted(shared, "brick", -1)
    pieces = 1 if group % 2 else 2
    each = group // pieces
    halos = call(
        functools.partial(halo_kernel, (layers, group)),
        [(each, layers, share) + cells] * pieces,
        [],
        0,
        before,
        after,
        square,
    )
    partner = [lax.ppermute(halo, "freq", [(0, 1), (1, 0)]) for halo in halos]
    count = group * norb + group
    before_rest, after_rest = shifted(rest, "brick", 1), shifted(rest, "brick", -1)
    mine, earlier = call(
        functools.partial(mine_kernel, (norb, layers, group), share),
        [shared.shape, (count, LANES)],
        [(count,) + cells],
        0,
        planes,
        inner,
        partial,
        *halos,
    )
    other, earlier = call(
        functools.partial(other_kernel, (norb, layers, group), share),
        [shared.shape, (count, LANES)],
        [(count,) + cells],
        0,
        planes,
        inner,
        partial,
        earlier,
        *partner[::-1],
    )
    applied, *sums = call(
        functools.partial(rest_kernel, (norb, layers, group), share),
        [own] + copies("brick", SUB, LANES),
        [rest.shape, (count,) + cells],
        0,
        planes,
        inner,
        partial,
        square,
        mine,
        other,
        earlier,
        after_rest,
        before_rest,
    )
    sums = parts_of(sums, "brick")
    runs = group
    part = group // runs
    steps = [
        call(
            functools.partial(residual_kernel, (norb, layers, group, len(sums), i * part, part), ncell),
            [(part,) + own[1:], (part * norb, LANES), (3 * part, LANES)],
            [(part * norb, LANES)],
            0,
            planes,
            source,
            applied,
            overlap,
            along,
            *sums,
        )
        for i in range(runs)
    ]
    aheads, plains, numbers = zip(*steps)
    afters = [shifted(ahead, "brick", -1) for ahead in aheads]
    residual, acc = call(
        functools.partial(second_kernel, (norb, layers, group, halves, runs)),
        [own, (3 * group,) + cells],
        [],
        2,
        omega,
        energies,
        planes,
        potential_planes,
        source,
        applied,
        *aheads,
        *plains,
        *numbers,
    )
    sums = call(
        functools.partial(pairs_kernel, (layers, group, runs)),
        copies("brick", SUB, LANES),
        [],
        0,
        acc,
        *aheads,
        *afters,
    )
    sums = parts_of(sums, "brick")
    width = NY // members
    margin = 2
    span = width + 2 * margin
    edge = 2 * halves * span
    cut = (layers * halves * span, LANES)
    cuts, scales = call(
        functools.partial(density_kernel, (layers, group, len(sums), halves, members, width, margin, runs)),
        [(members,) + cut, (2 * group, LANES)],
        [(layers, halves, NY + 2 * SUB, LANES)],
        0,
        planes,
        source,
        residual,
        *sums,
        *numbers,
    )
    others = [shifted(cuts[k], "orb", k) for k in range(1, members)]
    (response,) = call(
        functools.partial(response_kernel, (layers, group, halves)),
        [(layers * tiles * group, LANES)],
        [],
        0,
        source,
        residual,
        scales,
    )
    dense, top, bottom = call(
        functools.partial(gather_kernel, edge), [cut, (edge, LANES), (edge, LANES)], [], 0, cuts, *others[::-1]
    )
    before, after = shifted(top, "brick", 1), shifted(bottom, "brick", -1)
    (induced,) = call(
        functools.partial(jacobi_kernel, (layers, halves, width, margin)),
        [(layers, width * halves * LANES)],
        [((layers + 4) * halves * span + SUB, LANES), (layers * halves * (-(-span // SUB) * SUB), LANES)],
        0,
        dense,
        before,
        after,
    )
    response = response.reshape(layers, tiles, group, LANES).transpose(2, 0, 1, 3)
    return response.reshape(group, layers, columns), induced


def solution(mesh):
    placed = (P(None, "brick", None), P("brick", None), P("brick", None), P("orb"), P("freq"))
    return jax.shard_map(
        per_device,
        mesh=mesh,
        in_specs=placed,
        out_specs=(P(("freq", "orb"), "brick", None), P(("freq", "brick"), "orb")),
        check_vma=False,
    )
```

```python
import functools
import jax
import jax.numpy as jnp
from jax import lax
from jax.experimental import pallas as pl
from jax.experimental.pallas import tpu as pltpu
from jax.sharding import PartitionSpec as P

NY = 32
LANES = 128
SUB = 8

COEFFS = (
    -5369.0 / 1800.0,
    12.0 / 7.0,
    -15.0 / 56.0,
    10.0 / 189.0,
    -1.0 / 112.0,
    2.0 / 825.0,
    -1.0 / 5544.0,
)
SCREEN = 0.25
HIGHEST = lax.Precision.HIGHEST
VMEM_LIMIT = 16 * 1024 * 1024
SMEM = pl.BlockSpec(memory_space=pltpu.SMEM)
VMEM = pl.BlockSpec(memory_space=pltpu.VMEM)
HBM = pl.BlockSpec(memory_space=pltpu.HBM)
f32 = jnp.float32


def call(kernel, outs, scratch, smem, *args, far=0, limit=VMEM_LIMIT):
    return pl.pallas_call(
        kernel,
        out_shape=[jax.ShapeDtypeStruct(s, f32) for s in outs],
        in_specs=[SMEM] * smem + [HBM] * far + [VMEM] * (len(args) - smem - far),
        out_specs=[VMEM] * len(outs),
        scratch_shapes=[pltpu.VMEM(s, f32) if isinstance(s, tuple) else s for s in scratch],
        compiler_params=pltpu.CompilerParams(vmem_limit_bytes=limit),
    )(*args)


def copies(axis, rows, columns):
    size = lax.axis_size(axis)
    direct = size <= 4 and size & (size - 1) == 0
    return [(rows, columns) for k in range(size - 1 if direct else 1)]


def parts_of(arrays, axis):
    size = lax.axis_size(axis)
    if len(arrays) < size - 1:
        return [lax.psum(arrays[0], axis)]
    others = [
        lax.ppermute(array, axis, [(i, i ^ (k + 1)) for i in range(size)]) for k, array in enumerate(arrays)
    ]
    return [arrays[0]] + others


def put_copies(refs, value):
    rows = value.shape[0]
    for ref in refs:
        ref[:rows, :] = value
        if ref.shape[0] > rows:
            ref[rows:, :] = jnp.zeros((ref.shape[0] - rows, ref.shape[1]), f32)


def shifted(array, axis, step):
    size = lax.axis_size(axis)
    return lax.ppermute(array, axis, [(i, (i + step) % size) for i in range(size)])


def add_all(refs):
    total = refs[0][...]
    for ref in refs[1:]:
        total = total + ref[: total.shape[0], :]
    return total


def rows_to_lanes(matrix):
    count = matrix.shape[0]
    lane = lax.broadcasted_iota(jnp.int32, (count, LANES), 1)
    row = lax.broadcasted_iota(jnp.int32, (count, LANES), 0)
    value = jnp.broadcast_to(jnp.sum(matrix, axis=1, keepdims=True), (count, LANES))
    line = jnp.sum(jnp.where(lane == row, value, 0.0), axis=0, keepdims=True)
    return jnp.broadcast_to(line, (SUB, LANES))


def lanes_to_rows(line, count):
    wide = line.shape[1]
    lane = lax.broadcasted_iota(jnp.int32, (count, wide), 1)
    row = lax.broadcasted_iota(jnp.int32, (count, wide), 0)
    picked = jnp.where(lane == row, jnp.broadcast_to(line, (count, wide)), 0.0)
    return jnp.broadcast_to(jnp.sum(picked, axis=1, keepdims=True), (count, LANES))


def blocks(plane):
    return plane.reshape(-1, NY, LANES)


def gram_kernel(shape, far_rows_ref, far_perturb_ref, *refs):
    gram_refs, (rows_ref, perturb_ref, row_sems, perturb_sem) = refs[:-4], refs[-4:]
    norb, layers, halves, group = shape
    groups = norb // SUB
    tiles = NY * halves
    step = 32
    ahead = 3
    size = norb * tiles
    own = lax.axis_index("orb") * group // SUB

    def fetch(z):
        piece = pl.ds(z * size, size)
        return pltpu.make_async_copy(far_rows_ref.at[piece], rows_ref.at[piece], row_sems.at[z])

    weights = pltpu.make_async_copy(far_perturb_ref, perturb_ref, perturb_sem)
    fetch(0).start()
    weights.start()
    for z in range(1, min(ahead, layers)):
        fetch(z).start()
    weights.wait()

    def tile_row(z, t, c0):
        base = ((z * groups + t) * tiles + c0) * SUB
        return jnp.concatenate([rows_ref[pl.ds(base + c * SUB, SUB), :] for c in range(step)], axis=1)

    def rounded(value):
        return value.astype(jnp.bfloat16).astype(f32)

    def layer(z, total):
        fetch(z).wait()

        @pl.when(z + ahead < layers)
        def _():
            fetch(z + ahead).start()

        for c0 in range(0, tiles, step):
            field = jnp.concatenate([tile_row(z, t, c0) for t in range(groups)], axis=0)
            weighted = perturb_ref[pl.ds(z, 1), c0 * LANES : (c0 + step) * LANES] * tile_row(z, own, c0)
            rest = (field - rounded(field)).astype(jnp.bfloat16)
            field = field.astype(jnp.bfloat16)
            pair = jnp.concatenate([weighted, weighted - rounded(weighted)], axis=0).astype(jnp.bfloat16)
            left = jnp.concatenate([field, pair], axis=0)
            right = jnp.concatenate([field, rest], axis=0)
            total = total + lax.dot_general(
                left, right, (((1,), (1,)), ((), ())), preferred_element_type=f32
            )
        return total

    total = lax.fori_loop(0, layers, layer, jnp.zeros((norb + 2 * SUB, 2 * norb), f32))
    cross = total[:norb, norb:]
    overlap = total[:norb, :norb] + cross + cross.T
    total = total[norb:, :norb] + total[norb:, norb:]
    put_copies(gram_refs, jnp.concatenate([overlap, total[:SUB] + total[SUB:]], axis=0))


def tile_kernel(shape, rows_ref, perturb_ref, potential_ref, planes_ref, *refs):
    norb, layers, halves = shape
    tiles = NY * halves

    def layer(z, carry):
        for m in range(norb):
            base = (z * (norb // SUB) + m // SUB) * tiles * SUB + m % SUB
            for h in range(halves):
                for q in range(NY // SUB):
                    start = base + (q * SUB * halves + h) * SUB
                    planes_ref[m, z, h * (NY // SUB) + q] = rows_ref[pl.ds(start, SUB, stride=SUB * halves), :]
        return carry

    lax.fori_loop(0, layers, layer, 0)
    for array_ref, planes_ref in zip((perturb_ref, potential_ref), refs):
        for z in range(layers):
            for y in range(NY):
                for h in range(halves):
                    c = y * halves + h
                    planes_ref[z, h * (NY // SUB) + y // SUB, y % SUB : y % SUB + 1, :] = array_ref[
                        z : z + 1, c * LANES : (c + 1) * LANES
                    ]


def small_matrices(shape, ncell, gram_refs, lines_ref):
    norb, group = shape
    total = add_all(gram_refs)
    overlap = total[:norb]
    lines_ref[...] = total[norb:]
    start = lax.rem(lax.axis_index("orb") * group, SUB)
    rows = []
    for n in range(group):
        line = lines_ref[pl.ds(start + n, 1), :]
        again = jnp.sum(lanes_to_rows(line, norb)[:, :norb] * overlap, axis=0, keepdims=True)
        rows.append((line, again * (1.0 / ncell)))
    return overlap, rows


def whole(ref, n, z):
    return ref[n, z]


def combine(layers, group, norb, planes_ref, coef_ref, start, finish, pick=whole):
    def layer(z, carry):
        sums = [start(n, z) for n in range(group)]
        for m in range(norb):
            field = pick(planes_ref, m, z)
            for n in range(group):
                sums[n] = sums[n] + field * coef_ref[pl.ds(n * norb + m, 1), :]
        for n in range(group):
            finish(n, z, sums[n])
        return carry

    lax.fori_loop(0, layers, layer, 0)


def inner_kernel(shape, ncell, planes_ref, perturb_ref, *refs):
    norb, layers, group, parts, share = shape
    gram_refs = refs[:parts]
    shared_ref, coef_ref, lines_ref = refs[parts:]
    first = lax.axis_index("orb") * group
    overlap, rows = small_matrices((norb, group), ncell, gram_refs, lines_ref)
    for n, (line, again) in enumerate(rows):
        coefs = (2.0 * line - again) * (1.0 / ncell)
        coef_ref[n * norb : (n + 1) * norb, :] = lanes_to_rows(coefs, norb)
    mine = pl.ds(lax.axis_index("freq") * share, share)

    def pick(ref, n, z):
        return ref[n, z, mine]

    def start(n, z):
        return -(perturb_ref[z, mine] * pick(planes_ref, first + n, z))

    def finish(n, z, value):
        shared_ref[n, z] = value

    combine(layers, group, norb, planes_ref, coef_ref, start, finish, pick)


def alone_kernel(shape, planes_ref, perturb_ref, coef_ref, rest_ref):
    norb, layers, group, share = shape
    first = lax.axis_index("orb") * group

    def pick(ref, n, z):
        return ref[n, z, 2 * share :]

    def start(n, z):
        return -(perturb_ref[z, 2 * share :] * pick(planes_ref, first + n, z))

    def finish(n, z, value):
        rest_ref[n, z] = value

    combine(layers, group, norb, planes_ref, coef_ref, start, finish, pick)


def roll_x(halves_list, amount):
    count = len(halves_list)
    lane = lax.broadcasted_iota(jnp.int32, halves_list[0].shape, 1)
    turned = [pltpu.roll(v, amount % LANES, 1) for v in halves_list]
    if amount > 0:
        return [jnp.where(lane >= amount, turned[h], turned[(h - 1) % count]) for h in range(count)]
    return [
        jnp.where(lane < LANES + amount, turned[h], turned[(h + 1) % count]) for h in range(count)
    ]


def roll_y(value, amount):
    return pltpu.roll(value, amount % NY, 0)


def local_kernel(shape, ncell, omega_ref, energies_ref, planes_ref, perturb_ref, potential_ref, shared_ref, rest_ref, inner_coef_ref, *refs):
    norb, layers, group, parts, halves, share = shape
    gram_refs = refs[:parts]
    inner_ref, source_ref, partial_ref, overlap_ref, along_ref, square_ref, coef_ref, lines_ref = refs[parts:]
    first = lax.axis_index("orb") * group
    overlap, rows = small_matrices((norb, group), ncell, gram_refs, lines_ref)
    for m in range(norb):
        overlap_ref[m] = jnp.broadcast_to(overlap[:, m : m + 1], (norb, LANES))
    for n, (line, again) in enumerate(rows):
        place = slice(n * norb, (n + 1) * norb)
        coef_ref[place, :] = lanes_to_rows(line * (1.0 / ncell), norb)
        along_ref[place, :] = lanes_to_rows(again - line, norb)
    square_ref[...] = jnp.zeros_like(square_ref)

    def start(n, z):
        return -(perturb_ref[z] * planes_ref[first + n, z])

    def finish(n, z, value):
        source_ref[n, z] = value
        square_ref[n] += jnp.sum(value * value, axis=0)

    combine(layers, group, norb, planes_ref, coef_ref, start, finish)

    place = lax.axis_index("freq") * share
    mine, other = pl.ds(place, share), pl.ds(share - place, share)

    def start_other(n, z):
        return -(perturb_ref[z, other] * planes_ref[first + n, z, other])

    def finish_other(n, z, value):
        inner_ref[n, z, other] = value
        inner_ref[n, z, mine] = shared_ref[n, z]
        inner_ref[n, z, 2 * share :] = rest_ref[n, z]

    def pick_other(ref, n, z):
        return ref[n, z, other]

    combine(layers, group, norb, planes_ref, inner_coef_ref, start_other, finish_other, pick_other)

    for n in range(group):
        def layer(z, carry):
            plane = blocks(inner_ref[n, z])
            sheets = [plane[h] for h in range(halves)]
            sums = [(3.0 * COEFFS[0]) * v for v in sheets]
            for k in range(1, 7):
                right, left = roll_x(sheets, k), roll_x(sheets, -k)
                for h in range(halves):
                    around = right[h] + left[h] + roll_y(sheets[h], k) + roll_y(sheets[h], -k)
                    sums[h] = sums[h] + COEFFS[k] * around
            total = jnp.stack(sums).reshape(inner_ref.shape[2:])
            shift = potential_ref[z] + (omega_ref[0] - energies_ref[n])
            partial_ref[n, z] = shift * inner_ref[n, z] - 0.5 * total
            return carry

        lax.fori_loop(0, layers, layer, 0)
        for z in range(layers):
            total = None
            for other in range(layers):
                k = abs(other - z)
                if k == 0 or k > 6:
                    continue
                term = (-0.5 * COEFFS[k]) * inner_ref[n, other]
                total = term if total is None else total + term
            if total is not None:
                partial_ref[n, z] += total


def halo_sum(layers, n, z, before_ref, after_ref):
    total = None
    for j in range(layers):
        for k, ref in ((z + layers - j, before_ref), (j + layers - z, after_ref)):
            if k <= 6:
                term = (-0.5 * COEFFS[k]) * ref[n, j]
                total = term if total is None else total + term
    return total


def halo_kernel(shape, before_ref, after_ref, square_ref, *halo_refs):
    layers, group = shape
    each = group // len(halo_refs)
    for n in range(group):
        for z in range(layers):
            halo_refs[n // each][n % each, z] = halo_sum(layers, n, z, before_ref, after_ref)


def multiply(shape, spots, planes_ref, inner_ref, field_ref, acc_ref):
    norb, layers, group = shape
    acc_ref[...] = jnp.zeros_like(acc_ref)

    def layer(z, carry):
        fields = [field_ref[n, z] for n in range(group)]
        for n in range(group):
            acc_ref[group * norb + n] += jnp.sum(fields[n] * inner_ref[n, z, spots], axis=0)
        for m in range(norb):
            orbital = planes_ref[m, z, spots]
            for n in range(group):
                acc_ref[n * norb + m] += jnp.sum(orbital * fields[n], axis=0)
        return carry

    lax.fori_loop(0, layers, layer, 0)
    return jnp.sum(acc_ref[...], axis=1)


def mine_kernel(shape, share, planes_ref, inner_ref, partial_ref, *refs):
    norb, layers, group = shape
    field_ref, sums_ref, acc_ref = refs[-3:]
    each = group // (len(refs) - 3)
    spots = pl.ds(lax.axis_index("freq") * share, share)
    for n in range(group):
        for z in range(layers):
            field_ref[n, z] = partial_ref[n, z, spots] + refs[n // each][n % each, z]
    sums_ref[...] = multiply(shape, spots, planes_ref, inner_ref, field_ref, acc_ref)


def other_kernel(shape, share, planes_ref, inner_ref, partial_ref, earlier_ref, *refs):
    norb, layers, group = shape
    refs = refs[:-3][::-1] + refs[-3:]
    field_ref, sums_ref, acc_ref = refs[-3:]
    each = group // (len(refs) - 3)
    spots = pl.ds(share - lax.axis_index("freq") * share, share)
    for n in range(group):
        for z in range(layers):
            field_ref[n, z] = partial_ref[n, z, spots] + refs[n // each][n % each, z]
    sums = multiply(shape, spots, planes_ref, inner_ref, field_ref, acc_ref)
    sums_ref[...] = sums + earlier_ref[...]


def rest_kernel(shape, share, planes_ref, inner_ref, partial_ref, square_ref, mine_ref, other_ref, earlier_ref, after_ref, before_ref, *refs):
    norb, layers, group = shape
    applied_ref, sums_refs, (field_ref, acc_ref) = refs[0], refs[1:-2], refs[-2:]
    place = lax.axis_index("freq") * share
    mine, other = pl.ds(place, share), pl.ds(share - place, share)
    spots = pl.ds(2 * share, field_ref.shape[2])
    for n in range(group):
        for z in range(layers):
            field = partial_ref[n, z, spots] + halo_sum(layers, n, z, before_ref, after_ref)
            field_ref[n, z] = field
            applied_ref[n, z, 2 * share :] = field
            applied_ref[n, z, mine] = mine_ref[n, z]
            applied_ref[n, z, other] = other_ref[n, z]
    sums = multiply(shape, spots, planes_ref, inner_ref, field_ref, acc_ref) + earlier_ref[...]
    sums = rows_to_lanes(jnp.concatenate([sums, jnp.sum(square_ref[...], axis=1)], axis=0))
    put_copies(sums_refs, sums)


def residual_kernel(shape, ncell, planes_ref, source_ref, applied_ref, overlap_ref, along_ref, *refs):
    norb, layers, group, parts, begin, count = shape
    sums_refs = refs[:parts]
    ahead_ref, plain_ref, numbers_ref, coef_ref = refs[parts:]
    size = group * norb
    total = lanes_to_rows(add_all(sums_refs)[:1], size + 2 * group)
    curve = total[size + begin : size + begin + count]
    norm = total[size + group + begin : size + group + begin + count]
    step = norm / curve
    numbers_ref[:count, :] = norm
    numbers_ref[count : 2 * count, :] = curve
    numbers_ref[2 * count : 3 * count, :] = step
    for i in range(count):
        n = begin + i
        rows = slice(i * norb, (i + 1) * norb)
        product = total[n * norb : (n + 1) * norb]
        alpha = step[i : i + 1]
        again = jnp.zeros((norb, LANES), f32)
        for m in range(norb):
            again = again + overlap_ref[m] * product[m : m + 1]
        left = along_ref[n * norb : (n + 1) * norb, :] - alpha * (product - again * (1.0 / ncell))
        plain_ref[rows, :] = alpha * product * (1.0 / ncell)
        coef_ref[rows, :] = (alpha * product - left) * (1.0 / ncell)

    def start(i, z):
        return source_ref[begin + i, z] - numbers_ref[2 * count + i : 2 * count + i + 1, :] * applied_ref[begin + i, z]

    def finish(i, z, value):
        ahead_ref[i, z] = value

    combine(layers, count, norb, planes_ref, coef_ref, start, finish)


def second_kernel(shape, omega_ref, energies_ref, planes_ref, potential_ref, source_ref, applied_ref, *refs):
    norb, layers, group, halves, parts = shape
    ahead_refs, plain_refs, numbers_refs = refs[:parts], refs[parts : 2 * parts], refs[2 * parts : 3 * parts]
    residual_ref, acc_ref = refs[3 * parts :]
    each = group // parts
    acc_ref[...] = jnp.zeros_like(acc_ref)

    for part in range(parts):
        first = part * each

        def start(i, z):
            alpha = numbers_refs[part][2 * each + i : 2 * each + i + 1, :]
            return source_ref[first + i, z] - alpha * applied_ref[first + i, z]

        def finish(i, z, value):
            residual_ref[first + i, z] = value
            acc_ref[2 * group + first + i] += jnp.sum(value * value, axis=0)

        combine(layers, each, norb, planes_ref, plain_refs[part], start, finish)

    for n in range(group):
        ahead_ref, i = ahead_refs[n // each], n % each

        def layer(z, carry):
            whole = ahead_ref[i, z]
            plane = blocks(whole)
            sheets = [plane[h] for h in range(halves)]
            sums = [(-1.5 * COEFFS[0]) * v for v in sheets]
            for k in range(1, 7):
                right = roll_x(sheets, k)
                for h in range(halves):
                    sums[h] = sums[h] - COEFFS[k] * (right[h] + roll_y(sheets[h], k))
            total = jnp.stack(sums).reshape(whole.shape)
            total = total + (potential_ref[z] + (omega_ref[0] - energies_ref[n])) * whole
            acc_ref[n] += jnp.sum(whole * total, axis=0)
            acc_ref[group + n] += jnp.sum(whole * applied_ref[n, z], axis=0)
            return carry

        lax.fori_loop(0, layers, layer, 0)
        for z in range(layers - 1):
            total = None
            for other in range(z + 1, min(layers, z + 7)):
                term = -COEFFS[other - z] * ahead_ref[i, other]
                total = term if total is None else total + term
            acc_ref[n] += jnp.sum(ahead_ref[i, z] * total, axis=0)


def pairs_kernel(shape, acc_ref, *refs):
    layers, group, parts = shape
    ahead_refs, after_refs, sums_refs = refs[:parts], refs[parts : 2 * parts], refs[2 * parts :]
    each = group // parts
    sums = jnp.sum(acc_ref[...], axis=1)
    lines = []
    for n in range(group):
        ahead_ref, after_ref, i = ahead_refs[n // each], after_refs[n // each], n % each
        total = None
        for z in range(layers):
            line = None
            for j in range(layers):
                k = j + layers - z
                if k <= 6:
                    term = -COEFFS[k] * after_ref[i, j]
                    line = term if line is None else line + term
            if line is not None:
                line = line * ahead_ref[i, z]
                total = line if total is None else total + line
        lines.append(jnp.sum(jnp.sum(total, axis=0), axis=0, keepdims=True))
    sums = jnp.concatenate([sums[:group] + jnp.concatenate(lines, axis=0), sums[group:]], axis=0)
    put_copies(sums_refs, rows_to_lanes(sums))


def density_kernel(shape, planes_ref, source_ref, residual_ref, *refs):
    layers, group, parts, halves, members, width, margin, cut = shape
    sums_refs, numbers_refs, refs = refs[:parts], refs[parts : parts + cut], refs[parts + cut :]
    cuts_ref, scales_ref, ring_ref = refs
    each = group // cut
    first = lax.axis_index("orb")
    total = lanes_to_rows(add_all(sums_refs)[:1], 3 * group)
    norm, curve, alpha = (
        jnp.concatenate([ref[i * each : (i + 1) * each, :] for ref in numbers_refs], axis=0) for i in range(3)
    )
    squares, cross, bend = total[2 * group : 3 * group], total[group : 2 * group], total[:group]
    beta = squares / norm
    bend = bend + 2.0 * beta * cross + beta * beta * curve
    second = squares / bend
    scales_ref[:group, :] = alpha + second * beta
    scales_ref[group : 2 * group, :] = second

    def layer(z, carry):
        total = jnp.zeros(planes_ref.shape[2:], f32)
        for n in range(group):
            field = scales_ref[n : n + 1, :] * source_ref[n, z]
            field = field + scales_ref[group + n : group + n + 1, :] * residual_ref[n, z]
            total = total + field * planes_ref[first * group + n, z]
        total = blocks(4.0 * total)
        for h in range(halves):
            ring_ref[z, h, SUB : SUB + NY, :] = total[h]
            ring_ref[z, h, :SUB, :] = total[h, NY - SUB :]
            ring_ref[z, h, SUB + NY :, :] = total[h, :SUB]
        return carry

    lax.fori_loop(0, layers, layer, 0)
    for k in range(members):
        owner = lax.rem(first + k, members)
        for z in range(layers):
            for h in range(halves):
                rows = width + 2 * margin
                cuts_ref[k, pl.ds((z * halves + h) * rows, rows)] = ring_ref[
                    z, h, pl.ds(owner * width + SUB - margin, rows), :
                ]


def response_kernel(shape, source_ref, residual_ref, scales_ref, response_ref):
    layers, group, halves = shape
    tiles = NY * halves

    def layer(z, carry):
        for n in range(group):
            field = scales_ref[n : n + 1, :] * source_ref[n, z]
            field = field + scales_ref[group + n : group + n + 1, :] * residual_ref[n, z]
            for h in range(halves):
                for q in range(NY // SUB):
                    start = (z * tiles + q * SUB * halves + h) * group + n
                    response_ref[pl.ds(start, SUB, stride=group * halves), :] = field[h * (NY // SUB) + q]
        return carry

    lax.fori_loop(0, layers, layer, 0)


def gather_kernel(edge, cuts_ref, *refs):
    dense_ref, top_ref, bottom_ref = refs[-3:]
    total = cuts_ref[0]
    for ref in refs[:-3]:
        total = total + ref[...]
    dense_ref[...] = total
    top_ref[...] = total[-edge:]
    bottom_ref[...] = total[:edge]


def jacobi_kernel(shape, dense_ref, before_ref, after_ref, induced_ref, slab_ref, out_ref):
    layers, halves, width, margin = shape
    rows = width + 2 * margin
    full = -(-rows // SUB) * SUB
    scale = 1.0 / (6.0 + SCREEN)
    edge = 2 * halves * rows
    middle = layers * halves * rows
    slab_ref[:edge, :] = before_ref[...]
    slab_ref[edge : edge + middle, :] = dense_ref[...]
    slab_ref[edge + middle : 2 * edge + middle, :] = after_ref[...]
    slab_ref[2 * edge + middle :, :] = jnp.zeros((slab_ref.shape[0] - 2 * edge - middle, LANES), f32)
    dense = [
        [slab_ref[(z * halves + h) * rows : (z * halves + h) * rows + full, :] for h in range(halves)]
        for z in range(layers + 4)
    ]
    field = [[scale * v for v in sheet] for sheet in dense]

    def up(value):
        return pltpu.roll(value, 1, 0)

    def down(value):
        return pltpu.roll(value, full - 1, 0)

    for sweep in range(2):
        fresh = []
        for z in range(1, len(field) - 1):
            right, left = roll_x(field[z], 1), roll_x(field[z], -1)
            sheet = []
            for h in range(halves):
                value = dense[z][h] + field[z - 1][h] + field[z + 1][h] + right[h] + left[h]
                value = value + up(field[z][h]) + down(field[z][h])
                sheet.append(scale * value)
            fresh.append(sheet)
        field, dense = fresh, dense[1:-1]
    for z in range(layers):
        for h in range(halves):
            out_ref[pl.ds((z * halves + h) * full, full), :] = field[z][h]
    for h in range(halves):
        for y in range(width):
            c = y * halves + h
            induced_ref[:, c * LANES : (c + 1) * LANES] = out_ref[
                pl.ds(h * full + margin + y, layers, stride=halves * full), :
            ]


def per_device(orbitals, potential, perturb, energies, omega):
    norb, layers, columns = orbitals.shape
    group = energies.shape[0]
    bricks, members = lax.axis_size("brick"), lax.axis_size("orb")
    ncell = layers * bricks * columns
    halves = columns // NY // LANES
    tiles = columns // LANES
    spots = tiles // SUB
    rows = orbitals.transpose(1, 0, 2).reshape(layers, norb // SUB, SUB, tiles, LANES)
    rows = rows.transpose(0, 1, 3, 2, 4).reshape(layers * norb * tiles, LANES)
    own = (group, layers, spots, SUB, LANES)
    flat = (group * norb, LANES)

    size = norb * tiles
    gram = call(
        functools.partial(gram_kernel, (norb, layers, halves, group)),
        copies("brick", norb + SUB, norb),
        [
            (layers * size, LANES),
            (layers, columns),
            pltpu.SemaphoreType.DMA((layers,)),
            pltpu.SemaphoreType.DMA,
        ],
        0,
        rows,
        perturb,
        far=2,
        limit=60 * 1024 * 1024,
    )
    grams = parts_of(gram, "brick")
    plane = (layers, spots, SUB, LANES)
    planes, perturb_planes, potential_planes = call(
        functools.partial(tile_kernel, (norb, layers, halves)),
        [(norb,) + plane, plane, plane],
        [],
        0,
        rows,
        perturb,
        potential,
    )
    share = 3 * spots // 8
    cells = (SUB, LANES)
    shared, coefs = call(
        functools.partial(inner_kernel, (norb, layers, group, len(grams), share), ncell),
        [(group, layers, share) + cells, flat],
        [(SUB, norb)],
        0,
        planes,
        perturb_planes,
        *grams,
    )
    (rest,) = call(
        functools.partial(alone_kernel, (norb, layers, group, share)),
        [(group, layers, spots - 2 * share) + cells],
        [],
        0,
        planes,
        perturb_planes,
        coefs,
    )
    inner, source, partial, overlap, along, square = call(
        functools.partial(local_kernel, (norb, layers, group, len(grams), halves, share), ncell),
        [own, own, own, (norb, norb, LANES), flat, (group,) + cells],
        [flat, (SUB, norb)],
        2,
        omega,
        energies,
        planes,
        perturb_planes,
        potential_planes,
        shared,
        rest,
        coefs,
        *grams,
    )
    before, after = shifted(shared, "brick", 1), shifted(shared, "brick", -1)
    pieces = 1 if group % 2 else 2
    each = group // pieces
    halos = call(
        functools.partial(halo_kernel, (layers, group)),
        [(each, layers, share) + cells] * pieces,
        [],
        0,
        before,
        after,
        square,
    )
    partner = [lax.ppermute(halo, "freq", [(0, 1), (1, 0)]) for halo in halos]
    count = group * norb + group
    before_rest, after_rest = shifted(rest, "brick", 1), shifted(rest, "brick", -1)
    mine, earlier = call(
        functools.partial(mine_kernel, (norb, layers, group), share),
        [shared.shape, (count, LANES)],
        [(count,) + cells],
        0,
        planes,
        inner,
        partial,
        *halos,
    )
    other, earlier = call(
        functools.partial(other_kernel, (norb, layers, group), share),
        [shared.shape, (count, LANES)],
        [(count,) + cells],
        0,
        planes,
        inner,
        partial,
        earlier,
        *partner[::-1],
    )
    applied, *sums = call(
        functools.partial(rest_kernel, (norb, layers, group), share),
        [own] + copies("brick", SUB, LANES),
        [rest.shape, (count,) + cells],
        0,
        planes,
        inner,
        partial,
        square,
        mine,
        other,
        earlier,
        after_rest,
        before_rest,
    )
    sums = parts_of(sums, "brick")
    runs = group
    part = group // runs
    steps = [
        call(
            functools.partial(residual_kernel, (norb, layers, group, len(sums), i * part, part), ncell),
            [(part,) + own[1:], (part * norb, LANES), (3 * part, LANES)],
            [(part * norb, LANES)],
            0,
            planes,
            source,
            applied,
            overlap,
            along,
            *sums,
        )
        for i in range(runs)
    ]
    aheads, plains, numbers = zip(*steps)
    afters = [shifted(ahead, "brick", -1) for ahead in aheads]
    residual, acc = call(
        functools.partial(second_kernel, (norb, layers, group, halves, runs)),
        [own, (3 * group,) + cells],
        [],
        2,
        omega,
        energies,
        planes,
        potential_planes,
        source,
        applied,
        *aheads,
        *plains,
        *numbers,
    )
    sums = call(
        functools.partial(pairs_kernel, (layers, group, runs)),
        copies("brick", SUB, LANES),
        [],
        0,
        acc,
        *aheads,
        *afters,
    )
    sums = parts_of(sums, "brick")
    width = NY // members
    margin = 2
    span = width + 2 * margin
    edge = 2 * halves * span
    cut = (layers * halves * span, LANES)
    cuts, scales = call(
        functools.partial(density_kernel, (layers, group, len(sums), halves, members, width, margin, runs)),
        [(members,) + cut, (2 * group, LANES)],
        [(layers, halves, NY + 2 * SUB, LANES)],
        0,
        planes,
        source,
        residual,
        *sums,
        *numbers,
    )
    others = [shifted(cuts[k], "orb", k) for k in range(1, members)]
    (response,) = call(
        functools.partial(response_kernel, (layers, group, halves)),
        [(layers * tiles * group, LANES)],
        [],
        0,
        source,
        residual,
        scales,
    )
    dense, top, bottom = call(
        functools.partial(gather_kernel, edge), [cut, (edge, LANES), (edge, LANES)], [], 0, cuts, *others[::-1]
    )
    before, after = shifted(top, "brick", 1), shifted(bottom, "brick", -1)
    (induced,) = call(
        functools.partial(jacobi_kernel, (layers, halves, width, margin)),
        [(layers, width * halves * LANES)],
        [((layers + 4) * halves * span + SUB, LANES), (layers * halves * (-(-span // SUB) * SUB), LANES)],
        0,
        dense,
        before,
        after,
    )
    response = response.reshape(layers, tiles, group, LANES).transpose(2, 0, 1, 3)
    return response.reshape(group, layers, columns), induced


def solution(mesh):
    placed = (P(None, "brick", None), P("brick", None), P("brick", None), P("orb"), P("freq"))
    return jax.shard_map(
        per_device,
        mesh=mesh,
        in_specs=placed,
        out_specs=(P(("freq", "orb"), "brick", None), P(("freq", "brick"), "orb")),
        check_vma=False,
    )
```
